256 devices in a mesh: seq: 64 (over x, y, z_hi), row: 2 (over z_lo), col: 2 (over core).
Axes of the slice: x: 4, y: 4, z: 8 (z_hi: 4, z_lo: 2; z = z_hi * 2 + z_lo), core: 2. Of those that a mesh axis runs over, the one named last changes fastest.
Arguments:
- layer_input: bfloat16 [8192, 4096], P('seq', ('row', 'col')), may hold values from -6 to 6
- attn_out: bfloat16 [8192, 8192], P(('row', 'col'), 'seq'), may hold values from -6 to 6
- out_grad: bfloat16 [8192, 4096], P('seq', ('row', 'col')), may hold values from -0.3125 to 0.3125
- q_grad: bfloat16 [8192, 8192], P(('row', 'col'), 'seq'), may hold values from -0.875 to 0.875
- k_grad: bfloat16 [8192, 8192], P(('row', 'col'), 'seq'), may hold values from -0.3125 to 0.3125
- q_weight: bfloat16 [4096, 8192], P(('row', 'col'), 'seq'), may hold values from -0.375 to 0.375
- k_weight: bfloat16 [64, 512, 128], P('seq', ('row', 'col')), may hold values from -0.375 to 0.375
- o_weight: bfloat16 [8192, 4096], P('seq', ('row', 'col')), may hold values from -0.375 to 0.375
Outputs:
- input_grad: bfloat16 [8192, 4096], P('seq', ('row', 'col'))
- attn_grad: bfloat16 [8192, 8192], P(('row', 'col'), 'seq')
- q_weight_grad: float32 [4096, 8192], P(('row', 'col'), 'seq')
- k_weight_grad: float32 [64, 512, 128], P('seq', ('row', 'col'))
- o_weight_grad: float32 [8192, 4096], P('seq', ('row', 'col'))
The draws below stay inside these ranges and needn't reach their ends.
All inputs are finite; a program needn't handle non-finite values.
Results may differ from the reference program's by a relative error of at most 0.001.
Values may be sent and summed in bfloat16 or wider, within the bound.
A program may use at most 192 MiB of HBM per device.

```python
import jax
import jax.numpy as jnp

FEATURE_SHARD = 4096
HEAD_DIMENSION = 128
QUERIES_PER_KEY = 8
HQ = 64
KEY_HEADS = 8
TOKENS = 8192
KEY_PIECE_ROWS = 128
N_ROW = 2
N_COL = 2


def spiked(array, stream_key, source, target, blocks, factor):
    owner, partner = [(jnp.arange(array.shape[position]) // (array.shape[position] // blocks)).reshape([-1 if axis == position else 1 for axis in range(array.ndim)]) for position in (source, target)]
    chosen = jax.random.permutation(stream_key, blocks)[partner]
    strong = (owner == chosen) | (owner == (partner + blocks // 2) % blocks)
    return jnp.where(strong, factor * array, array)


def steps_of(own_key, shape, pieces, least, high):
    factor_of, own = 1.0, jax.random.fold_in(own_key, 6)
    for axis_at, blocks in pieces:
        steps = jnp.exp(jax.random.uniform(jax.random.fold_in(own, axis_at), (blocks,), jnp.float32, least / len(pieces), high / len(pieces)))
        factor_of = factor_of * jnp.repeat(steps, shape[axis_at] // blocks).reshape([-1 if axis == axis_at else 1 for axis in range(len(shape))])
    return factor_of


def noise(own_key, shape, width, bound, pieces=(), held_as=jnp.bfloat16):
    entries = width * jax.random.normal(own_key, shape, jnp.float32)
    if pieces:
        entries = entries * steps_of(own_key, shape, pieces, -0.22, 0.18)
    return jnp.clip(entries, -bound, bound).astype(held_as)


def gaussian_with(stream_key, shape, deviation, bound, cuts, heavy, kind=jnp.bfloat16):
    entries = deviation * jax.random.normal(stream_key, shape, jnp.float32)
    if cuts:
        entries = entries * steps_of(stream_key, shape, cuts, -0.22, 0.18)
    return jnp.clip(spiked(entries, jax.random.fold_in(stream_key, 3), *heavy), -bound, bound).astype(kind)


def setup_inputs(seed: int = 0) -> dict:
    streams_of = jax.random.split(jax.random.key(seed), 9)
    return {
        "layer_input": noise(streams_of[0], (TOKENS, FEATURE_SHARD), 1.0, 6.0, ((0, 64), (1, 4))),
        "attn_out": noise(streams_of[1], (TOKENS, HQ * HEAD_DIMENSION), 1.0, 6.0, ((0, 4), (1, 64))),
        "out_grad": noise(streams_of[2], (TOKENS, FEATURE_SHARD), 0.05, 0.3125, ((0, 64), (1, 4))),
        "q_grad": gaussian_with(streams_of[3], (TOKENS, HQ * HEAD_DIMENSION), 0.05, 0.875, ((0, 4), (1, 64)), (1, 0, 64, 4.0)),
        "k_grad": noise(streams_of[4], (TOKENS, HQ * HEAD_DIMENSION), 0.05, 0.3125, ((0, 4), (1, 64))),
        "q_weight": noise(streams_of[5], (FEATURE_SHARD, HQ * HEAD_DIMENSION), (2 * HEAD_DIMENSION) ** -0.5, 0.375, ((0, 4), (1, 64))),
        "k_weight": noise(streams_of[6], (HQ, FEATURE_SHARD // QUERIES_PER_KEY, HEAD_DIMENSION), (2 * HEAD_DIMENSION) ** -0.5, 0.375, ((0, 64), (1, 4))),
        "o_weight": noise(streams_of[7], (HQ * HEAD_DIMENSION, FEATURE_SHARD), (2 * HEAD_DIMENSION) ** -0.5, 0.375, ((0, 64), (1, 4))),
    }


def stored_to_matrix(device_shards):
    weight_pieces = N_ROW * N_COL
    storage_layout = device_shards.reshape(KEY_HEADS, QUERIES_PER_KEY, weight_pieces, KEY_PIECE_ROWS, HEAD_DIMENSION)
    storage_layout = jnp.transpose(storage_layout, (2, 1, 3, 0, 4))
    return storage_layout.reshape(FEATURE_SHARD, KEY_HEADS * HEAD_DIMENSION)


def matrix_to_stored(dense_matrix):
    weight_pieces = N_ROW * N_COL
    storage_layout = dense_matrix.reshape(weight_pieces, QUERIES_PER_KEY, KEY_PIECE_ROWS, KEY_HEADS, HEAD_DIMENSION)
    storage_layout = jnp.transpose(storage_layout, (3, 1, 0, 2, 4))
    return storage_layout.reshape(HQ, weight_pieces * KEY_PIECE_ROWS, HEAD_DIMENSION)


def widen(dense_matrix):
    spread_rows = jnp.repeat(dense_matrix.reshape(FEATURE_SHARD, KEY_HEADS, 1, HEAD_DIMENSION), QUERIES_PER_KEY, axis=2)
    return spread_rows.reshape(FEATURE_SHARD, HQ * HEAD_DIMENSION)


def reference(layer_input, attn_out, out_grad, q_grad, k_grad, q_weight, k_weight, o_weight):
    attn_grad = jnp.dot(out_grad, o_weight.T, preferred_element_type=jnp.float32).astype(jnp.bfloat16)
    o_weight_grad = jnp.dot(attn_out.T, out_grad, preferred_element_type=jnp.float32)
    key_wide = widen(stored_to_matrix(k_weight))
    total = jnp.dot(q_grad, q_weight.T, preferred_element_type=jnp.float32)
    total = total + jnp.dot(k_grad, key_wide.T, preferred_element_type=jnp.float32)
    input_grad = total.astype(jnp.bfloat16)
    q_weight_grad = jnp.dot(layer_input.T, q_grad, preferred_element_type=jnp.float32)
    key_partial_sums = jnp.dot(layer_input.T, k_grad, preferred_element_type=jnp.float32)
    key_partial_sums = key_partial_sums.reshape(FEATURE_SHARD, KEY_HEADS, QUERIES_PER_KEY, HEAD_DIMENSION).sum(axis=2).reshape(FEATURE_SHARD, KEY_HEADS * HEAD_DIMENSION)
    k_weight_grad = matrix_to_stored(key_partial_sums)
    return (input_grad, attn_grad, q_weight_grad, k_weight_grad, o_weight_grad)
```

```python
import jax
import jax.numpy as jnp
from jax import lax
from jax.experimental import pallas as pl
from jax.experimental.pallas import tpu as pltpu
from jax.sharding import PartitionSpec as P

MESH = pl.DeviceIdType.MESH
COPIES = 160
F32 = jnp.float32
BF16 = jnp.bfloat16


def rem(value, size):
    return lax.rem(value + size, size)


def at128(index):
    return pl.ds(pl.multiple_of(index * 128, 128), 128)


def at1024(index):
    return pl.ds(pl.multiple_of(index * 1024, 1024), 1024)


def kernel(
    li, ao, og, q, k, qw, kw, ow,
    ig_out, ag_out, qwg_out, kwg_out, owg_out,
    lit, ogt, qkt, aot, w3, w1, km, kbuf,
    ig, iga, igb, iga2, igb2,
    qwg, owg, kwg, qwr, owr, kwr, kwy,
    ag, agr, agb, fin,
    ssem, rsem, lsem,
):
    seq = lax.axis_index("seq")
    x, y, zh = lax.div(seq, 16), lax.rem(lax.div(seq, 4), 4), lax.rem(seq, 4)
    zlo, col = lax.axis_index("row"), lax.axis_index("col")
    z = zh * 2 + zlo
    ylo = lax.rem(y, 2)
    quarter = zlo * 2 + col

    def device(dx, dy, dz, other=False):
        zz = rem(z + dz, 8)
        return (
            rem(x + dx, 4) * 16 + rem(y + dy, 4) * 4 + lax.div(zz, 2),
            lax.rem(zz, 2),
            1 - col if other else col,
        )

    xs = [device(d, 0, 0) for d in (1, 2, 3)]
    ys = [device(0, d, 0) for d in (1, 2, 3)]
    zs = [device(0, 0, d) for d in range(1, 8)]
    sibling = device(0, 0, 0, True)
    zpartner = device(0, 0, 1 - 2 * zlo)
    ypartner = device(0, 1 - 2 * ylo, 0)
    left, right = device(0, 0, -1), device(0, 0, 1)

    barrier = pltpu.get_barrier_semaphore()
    peers = xs + ys + zs + [sibling]
    for peer in peers:
        pl.semaphore_signal(barrier, inc=1, device_id=peer, device_id_type=MESH)
    pl.semaphore_wait(barrier, len(peers))

    sent, local = [], []

    def send(src, dst, to):
        n = len(sent)
        copy = pltpu.make_async_remote_copy(
            src_ref=src, dst_ref=dst, send_sem=ssem.at[n], recv_sem=rsem.at[n],
            device_id=to, device_id_type=MESH,
        )
        copy.start()
        sent.append(copy)
        return copy

    def place(src, dst):
        copy = pltpu.make_async_copy(src, dst, lsem.at[len(local)])
        copy.start()
        local.append(copy)
        return copy

    def arrive(copies):
        for copy in copies:
            copy.wait_recv()

    def settle(copies):
        for copy in copies:
            copy.wait()

    def regroup(src, tile):
        mine = place(src.at[zlo], tile.at[x, y, :, at1024(zlo)])
        return mine, send(src.at[1 - zlo], tile.at[x, y, :, at1024(zlo)], zpartner)

    def gather_first(tile, parts):
        parts[0].wait()
        parts[1].wait_recv()
        a, b = tile.at[x, y, pl.ds(0, 32)], tile.at[x, y, pl.ds(32, 32)]
        return [send(a, a, to) for to in xs], [send(b, b, to) for to in ys]

    def gather_second(tile, parts):
        arrive(parts[0])
        a = tile.at[:, y, pl.ds(0, 32)]
        first = [send(a, a, to) for to in ys]
        arrive(parts[1])
        b = tile.at[x, :, pl.ds(32, 32)]
        return first + [send(b, b, to) for to in xs]

    def spread(src, slot):
        copies = [
            send(src.at[:, rem(z + d, 8)], slot(zh, zlo), zs[d - 1]) for d in range(1, 8)
        ]
        return place(src.at[:, z], slot(zh, zlo)), copies

    def ring_gather(piece):
        own = piece(z, None)
        steps = [[send(own, own, left), send(own, own, right)]]

        def step(s):
            arrive(steps[-1])
            half = s == 4
            a = piece(rem(z + s - 1, 8), 0 if half else None)
            b = piece(rem(z - s + 1, 8), 1 if half else None)
            steps.append([send(a, a, left), send(b, b, right)])

        return step, lambda: arrive(steps[-1])

    def ring_reduce(piece, got, half_rows):
        far = rem(z + 4, 8)
        h0, h1 = pl.ds(0, half_rows), pl.ds(half_rows, half_rows)
        steps = [[
            send(piece(far).at[h0], got.at[0, 0, h0], left),
            send(piece(far).at[h1], got.at[1, 0, h1], right),
        ]]

        def step(s):
            arrive(steps[-1])
            a, b = piece(rem(z - (5 - s), 8)), piece(rem(z + (5 - s), 8))
            if s == 2:
                a[h0] = a[h0] + got[0, 0, h0]
                b[h1] = b[h1] + got[1, 0, h1]
            else:
                a[...] = a[...] + got[0, s - 2]
                b[...] = b[...] + got[1, s - 2]
            steps.append([
                send(a, got.at[0, s - 1], left), send(b, got.at[1, s - 1], right)
            ])

        def total():
            arrive(steps[-1])
            return piece(z)[...] + got[0, 3] + got[1, 3]

        return step, total

    def qw_slot(zz, half):
        rows = pl.ds(0, 1024) if half is None else pl.ds(half * 512, 512)
        return w3.at[lax.rem(zz, 2), rows, at128(lax.div(zz, 2))]

    def km_slot(zz, half):
        pairs = pl.ds(0, 2) if half is None else pl.ds(half, 1)
        return km.at[lax.rem(zz, 2), pairs, lax.div(zz, 2)]

    def ow_slot(zz, half):
        rows = pl.ds(0, 128) if half is None else pl.ds(half * 64, 64)
        return w1.at[lax.div(zz, 2), rows, at1024(lax.rem(zz, 2))]


    li_parts = regroup(li, lit)
    og_parts = regroup(og, ogt)
    km_own = place(kw, km.at[zlo, ylo, zh])
    km_sent = send(kw, km.at[zlo, ylo, zh], ypartner)
    qw_own = place(qw, qw_slot(z, None))
    ow_own = place(ow, ow_slot(z, None))

    def head_slot(tile):
        return lambda h, lo: tile.at[quarter, :, :, at128(h)]

    q_own, q_copies = spread(q, head_slot(qkt))
    k_own, k_copies = spread(k, lambda h, lo: kbuf.at[h, lo])
    qw_own.wait()
    qw_step, qw_done = ring_gather(qw_slot)
    li_first = gather_first(lit, li_parts)
    og_first = gather_first(ogt, og_parts)
    km_own.wait()
    km_sent.wait_recv()
    km_step, km_done = ring_gather(km_slot)
    ao_own, ao_copies = spread(ao, head_slot(aot))
    qw_step(2)
    km_step(2)
    li_second = gather_second(lit, li_first)
    qw_step(3)
    km_step(3)
    og_second = gather_second(ogt, og_first)
    ow_own.wait()
    ow_step, ow_done = ring_gather(ow_slot)
    qw_step(4)
    km_step(4)

    k_own.wait()
    arrive(k_copies)

    for lo in range(2):
        total = kbuf[0, lo].astype(F32)
        for h in range(1, 4):
            total = total + kbuf[h, lo].astype(F32)
        high = total.astype(BF16)
        qkt[lo * 2 + col, :, :, pl.ds(512, 128)] = high
        qkt[lo * 2 + col, :, :, pl.ds(640, 128)] = (total - high.astype(F32)).astype(BF16)
    q_own.wait()
    arrive(q_copies)

    def exchange(tile):
        views = [tile.at[lo * 2 + col] for lo in range(2)]
        return [send(view, view, sibling) for view in views]

    q_shared = exchange(qkt)
    ow_step(2)
    arrive(li_second)
    arrive(q_shared)

    for lo in range(2):
        def block(i, _, lo=lo):
            cols = pl.ds(pl.multiple_of(lo * 1024 + i * 256, 256), 256)
            rows = pl.ds(pl.multiple_of(i * 256, 256), 256)
            part = lax.dot_general(
                lit[:, :, :, cols].reshape(1024, 256), qkt[...].reshape(1024, 768),
                (((0,), (0,)), ((), ())), preferred_element_type=F32,
            )
            for h in range(4):
                qwg[lo, h, rows, :] = part[:, h * 128 : h * 128 + 128]
            sums = part[:, 512:640] + part[:, 640:768]
            kwg[lo, lax.div(i, 2), pl.ds(lax.rem(i, 2) * 2, 2)] = sums.reshape(2, 128, 128)
            return 0
        lax.fori_loop(0, 4, block, 0)
    kwg_sent = send(kwg.at[:, 1 - ylo], kwy, ypartner)
    qwg_step, qwg_total = ring_reduce(
        lambda zz: qwg.at[lax.rem(zz, 2), lax.div(zz, 2)], qwr, 512
    )

    qw_done()
    km_done()
    for lo in range(2):
        keys = km[lo].reshape(1024, 128)
        w3[lo, :, pl.ds(512, 128)] = keys
        w3[lo, :, pl.ds(640, 128)] = keys
    for lo in range(2):
        def block(i, _, lo=lo):
            cols = pl.ds(pl.multiple_of(lo * 1024 + i * 256, 256), 256)
            rows = pl.ds(pl.multiple_of(i * 256, 256), 256)
            part = lax.dot_general(
                qkt[...].reshape(1024, 768), w3[lo, rows, :],
                (((1,), (1,)), ((), ())), preferred_element_type=F32,
            )
            ig[:, :, :, cols] = part.reshape(4, 4, 64, 256)
            return 0
        lax.fori_loop(0, 4, block, 0)
    a_rows, b_rows = pl.ds(0, 32), pl.ds(32, 32)
    ig_first = [
        send(ig.at[:, rem(y + d, 4), a_rows], iga.at[d - 1], ys[d - 1]) for d in (1, 2, 3)
    ] + [
        send(ig.at[rem(x + d, 4), :, b_rows], igb.at[d - 1], xs[d - 1]) for d in (1, 2, 3)
    ]
    ow_step(3)

    ao_own.wait()
    arrive(ao_copies)
    ao_shared = exchange(aot)
    arrive(og_second)
    arrive(ao_shared)
    for lo in range(2):
        def block(i, _, lo=lo):
            cols = pl.ds(pl.multiple_of(lo * 1024 + i * 512, 512), 512)
            part = lax.dot_general(
                aot[...].reshape(1024, 512), ogt[:, :, :, cols].reshape(1024, 512),
                (((0,), (0,)), ((), ())), preferred_element_type=F32,
            )
            owg[:, lo, :, pl.ds(pl.multiple_of(i * 512, 512), 512)] = part.reshape(4, 128, 512)
            return 0
        lax.fori_loop(0, 2, block, 0)
    owg_step, owg_total = ring_reduce(
        lambda zz: owg.at[lax.div(zz, 2), lax.rem(zz, 2)], owr, 64
    )
    ow_step(4)
    kwg_sent.wait()
    kwg[:, ylo] = kwg[:, ylo] + kwy[...]
    kwg_step, kwg_total = ring_reduce(
        lambda zz: kwg.at[lax.rem(zz, 2), ylo, lax.div(zz, 2)], kwr, 64
    )
    qwg_step(2)
    owg_step(2)
    kwg_step(2)

    ow_done()

    def block(i, _):
        part = lax.dot_general(
            ogt[i].reshape(256, 2048), w1[...].reshape(512, 2048),
            (((1,), (1,)), ((), ())), preferred_element_type=F32,
        )
        ag[i] = part.reshape(4, 64, 512)
        return 0

    lax.fori_loop(0, 4, block, 0)
    ag_sent = [send(ag.at[lo * 2 + 1 - col], agr.at[lo], sibling) for lo in range(2)]
    for lo in range(2):
        ag_sent[lo].wait_recv()
        agb[lo] = (ag[lo * 2 + col] + agr[lo]).astype(BF16)
    ag_own = place(agb.at[zlo, :, :, at128(zh)], ag_out.at[:, z])
    ag_copies = []
    for d in range(1, 8):
        zz = rem(z + d, 8)
        ag_copies.append(send(
            agb.at[lax.rem(zz, 2), :, :, at128(lax.div(zz, 2))], ag_out.at[:, z], zs[d - 1]
        ))

    arrive(ig_first)

    def add_a(i, _):
        ig[i, y, a_rows] = ig[i, y, a_rows] + iga[0, i] + iga[1, i] + iga[2, i]
        return 0

    def add_b(i, _):
        ig[x, i, b_rows] = ig[x, i, b_rows] + igb[0, i] + igb[1, i] + igb[2, i]
        return 0

    lax.fori_loop(0, 4, add_a, 0)
    lax.fori_loop(0, 4, add_b, 0)
    ig_second = [
        send(ig.at[rem(x + d, 4), y, a_rows], iga2.at[d - 1], xs[d - 1]) for d in (1, 2, 3)
    ] + [
        send(ig.at[x, rem(y + d, 4), b_rows], igb2.at[d - 1], ys[d - 1]) for d in (1, 2, 3)
    ]
    qwg_step(3)
    owg_step(3)
    kwg_step(3)
    arrive(ig_second)
    fin[pl.ds(0, 32), :] = (ig[x, y, a_rows] + iga2[0] + iga2[1] + iga2[2]).astype(BF16)
    fin[pl.ds(32, 32), :] = (ig[x, y, b_rows] + igb2[0] + igb2[1] + igb2[2]).astype(BF16)
    ig_own = place(fin.at[:, at1024(zlo)], ig_out.at[zlo])
    ig_sent = send(fin.at[:, at1024(1 - zlo)], ig_out.at[zlo], zpartner)
    qwg_step(4)
    owg_step(4)
    kwg_step(4)
    qwg_out[...] = qwg_total()
    kwg_out[...] = kwg_total()
    owg_out[...] = owg_total()
    arrive(ag_copies)
    ag_own.wait()
    ig_sent.wait_recv()
    ig_own.wait()
    for copy in sent:
        if copy is not kwg_sent:
            copy.wait_send()


def shards(layer_input, attn_out, out_grad, q_grad, k_grad, q_weight, k_weight, o_weight):
    shapes = (
        ((2, 64, 1024), BF16), ((4, 8, 64, 128), BF16), ((1024, 128), F32),
        ((128, 128), F32), ((128, 1024), F32),
    )
    vmem = pltpu.VMEM
    scratch = [
        vmem((4, 4, 64, 2048), BF16),
        vmem((4, 4, 64, 2048), BF16),
        vmem((4, 4, 64, 768), BF16),
        vmem((4, 4, 64, 512), BF16),
        vmem((2, 1024, 768), BF16),
        vmem((4, 128, 2048), BF16),
        vmem((2, 2, 4, 128, 128), BF16),
        vmem((4, 2, 4, 64, 128), BF16),
        vmem((4, 4, 64, 2048), F32),
        vmem((3, 4, 32, 2048), F32),
        vmem((3, 4, 32, 2048), F32),
        vmem((3, 32, 2048), F32),
        vmem((3, 32, 2048), F32),
        vmem((2, 4, 1024, 128), F32),
        vmem((4, 2, 128, 1024), F32),
        vmem((2, 2, 4, 128, 128), F32),
        vmem((2, 4, 1024, 128), F32),
        vmem((2, 4, 128, 1024), F32),
        vmem((2, 4, 128, 128), F32),
        vmem((2, 4, 128, 128), F32),
        vmem((4, 4, 64, 512), F32),
        vmem((2, 4, 64, 512), F32),
        vmem((2, 4, 64, 512), BF16),
        vmem((64, 2048), BF16),
        pltpu.SemaphoreType.DMA((COPIES,)),
        pltpu.SemaphoreType.DMA((COPIES,)),
        pltpu.SemaphoreType.DMA((16,)),
    ]
    ig, ag, qwg, kwg, owg = pl.pallas_call(
        kernel,
        out_shape=[jax.ShapeDtypeStruct(*shape) for shape in shapes],
        in_specs=[pl.BlockSpec(memory_space=pl.ANY)] * 8,
        out_specs=[pl.BlockSpec(memory_space=pltpu.VMEM)] * 5,
        scratch_shapes=scratch,
        compiler_params=pltpu.CompilerParams(
            collective_id=0, has_side_effects=True, vmem_limit_bytes=62 * 2**20
        ),
        cost_estimate=pl.CostEstimate(flops=14 * 10**9, bytes_accessed=5 * 10**6, transcendentals=0),
    )(
        layer_input.reshape(2, 64, 1024),
        attn_out.reshape(4, 8, 64, 128),
        out_grad.reshape(2, 64, 1024),
        q_grad.reshape(4, 8, 64, 128),
        k_grad.reshape(4, 8, 64, 128),
        q_weight,
        k_weight[0],
        o_weight,
    )
    return (
        ig.reshape(128, 1024),
        ag.reshape(2048, 128),
        qwg,
        kwg[None],
        owg,
    )


def solution(mesh):
    return jax.shard_map(
        shards,
        mesh=mesh,
        in_specs=(
            P("seq", ("row", "col")),
            P(("row", "col"), "seq"),
            P("seq", ("row", "col")),
            P(("row", "col"), "seq"),
            P(("row", "col"), "seq"),
            P(("row", "col"), "seq"),
            P("seq", ("row", "col"), None),
            P("seq", ("row", "col")),
        ),
        out_specs=(
            P("seq", ("row", "col")),
            P(("row", "col"), "seq"),
            P(("row", "col"), "seq"),
            P("seq", ("row", "col"), None),
            P("seq", ("row", "col")),
        ),
        check_vma=False,
    )
```

```python
import jax
import jax.numpy as jnp
from jax import lax
from jax.experimental import pallas as pl
from jax.experimental.pallas import tpu as pltpu
from jax.sharding import PartitionSpec as P

MESH = pl.DeviceIdType.MESH
COPIES = 160
F32 = jnp.float32
BF16 = jnp.bfloat16


def rem(value, size):
    return lax.rem(value + size, size)


def at128(index):
    return pl.ds(pl.multiple_of(index * 128, 128), 128)


def at1024(index):
    return pl.ds(pl.multiple_of(index * 1024, 1024), 1024)


def kernel(
    li, ao, og, q, k, qw, kw, ow,
    ig_out, ag_out, qwg_out, kwg_out, owg_out,
    lit, owt, ogt, qkt, aot, w3, km, kbuf,
    ig, owg, ig_got, owg_got,
    qwg, kwg, qw_far, qw_full, kw_far, kw_full, kwy,
    agr, agb, fin,
    ssem, rsem, lsem, gsem,
):
    seq = lax.axis_index("seq")
    x, y, zh = lax.div(seq, 16), lax.rem(lax.div(seq, 4), 4), lax.rem(seq, 4)
    zlo, col = lax.axis_index("row"), lax.axis_index("col")
    z = zh * 2 + zlo
    yhi, ylo = lax.div(y, 2), lax.rem(y, 2)
    quarter = zlo * 2 + col

    def at(xx, yy, lo, core):
        return (xx * 16 + yy * 4 + zh, lo, core)

    def device(dx, dy, dz):
        zz = rem(z + dz, 8)
        return (
            rem(x + dx, 4) * 16 + rem(y + dy, 4) * 4 + lax.div(zz, 2), lax.rem(zz, 2), col
        )

    zs = [device(0, 0, d) for d in range(1, 8)]
    sibling = at(x, y, zlo, 1 - col)
    zpartner = device(0, 0, 1 - 2 * zlo)
    ypartner = device(0, 1 - 2 * ylo, 0)
    x_ring = (4, x, device(-1, 0, 0), device(1, 0, 0))
    y_ring = (4, y, device(0, -1, 0), device(0, 1, 0))
    z_ring = (8, z, device(0, 0, -1), device(0, 0, 1))

    square = ylo == zlo
    home = jnp.logical_and(x == quarter, y == col * 2 + zlo)
    spread_ow = [(at(x, yhi * 2 + r, ylo, col), jnp.logical_and(square, ylo == r)) for r in range(2)]
    return_ow = [(at(x, yhi * 2 + zlo, b, col), jnp.logical_and(square, zlo == b)) for b in range(2)]
    spread_ao = [(at(quarter, j, ylo, yhi), jnp.logical_and(home, y == j)) for j in range(4)]
    return_ag = [
        (at(i, col * 2 + zlo, lax.div(x, 2), lax.rem(x, 2)), jnp.logical_and(home, x == i))
        for i in range(4)
    ]

    barrier = pltpu.get_barrier_semaphore()
    peers = list(x_ring[2:]) + list(y_ring[2:]) + zs + [sibling]
    for peer in peers:
        pl.semaphore_signal(barrier, inc=1, device_id=peer, device_id_type=MESH)
    for peer, own in spread_ow + return_ow + spread_ao + return_ag:
        @pl.when(jnp.logical_not(own))
        def _(peer=peer):
            pl.semaphore_signal(barrier, inc=1, device_id=peer, device_id_type=MESH)
    count = len(peers) + 12 - 2 * square.astype(jnp.int32) - 2 * home.astype(jnp.int32)
    pl.semaphore_wait(barrier, count)

    sent, local, guarded = [], [], []

    def send(src, dst, to):
        n = len(sent)
        copy = pltpu.make_async_remote_copy(
            src_ref=src, dst_ref=dst, send_sem=ssem.at[n], recv_sem=rsem.at[n],
            device_id=to, device_id_type=MESH,
        )
        copy.start()
        sent.append(copy)
        return copy

    def place(src, dst):
        copy = pltpu.make_async_copy(src, dst, lsem.at[len(local)])
        copy.start()
        local.append(copy)
        return copy

    def post(src, dst, partner, slot):
        to, own = partner
        copy = pltpu.make_async_remote_copy(
            src_ref=src, dst_ref=dst, send_sem=gsem.at[16 + len(guarded)],
            recv_sem=gsem.at[slot], device_id=to, device_id_type=MESH,
        )

        @pl.when(jnp.logical_not(own))
        def _():
            copy.start()

        @pl.when(own)
        def _():
            pltpu.make_async_copy(src, dst, gsem.at[slot]).start()

        guarded.append((copy, own))

    def collect(dst, slot):
        pltpu.make_async_copy(dst, dst, gsem.at[slot]).wait()

    def arrive(copies):
        for copy in copies:
            copy.wait_recv()

    def add(dst, *parts):
        if len(dst.shape) == 3:
            def row(i, _):
                total = dst[i]
                for part in parts:
                    total = total + part[i]
                dst[i] = total
                return 0
            lax.fori_loop(0, dst.shape[0], row, 0)
        else:
            total = dst[...]
            for part in parts:
                total = total + part[...]
            dst[...] = total

    def ring_gather(ring, piece):
        n, me, left, right = ring
        own = piece(me, None)
        steps = [[send(own, own, left), send(own, own, right)]]

        def step(s):
            arrive(steps[-1])
            half = s == n // 2
            a = piece(rem(me + s - 1, n), 0 if half else None)
            b = piece(rem(me - s + 1, n), 1 if half else None)
            steps.append([send(a, a, left), send(b, b, right)])

        return step, lambda: arrive(steps[-1])

    def ring_reduce(ring, piece, far, full):
        n, me, left, right = ring
        size = far(0).shape[0]
        halves = [pl.ds(0, size), pl.ds(size, size)]
        last = n // 2
        across = piece(rem(me + last, n))
        steps = [[
            send(across.at[halves[0]], far(0), left), send(across.at[halves[1]], far(1), right)
        ]]

        def step(s):
            arrive(steps[-1])
            a, b = piece(rem(me - (last + 1 - s), n)), piece(rem(me + (last + 1 - s), n))
            if s == 2:
                add(a.at[halves[0]], far(0))
                add(b.at[halves[1]], far(1))
            else:
                add(a, full(0, s - 3))
                add(b, full(1, s - 3))
            steps.append([send(a, full(0, s - 2), left), send(b, full(1, s - 2), right)])

        def total():
            arrive(steps[-1])
            add(piece(me), full(0, last - 2), full(1, last - 2))
            return piece(me)

        return step, total

    def part_of(size, half):
        return pl.ds(0, size) if half is None else pl.ds(half * (size // 2), size // 2)

    def rows_of(start, half):
        return pl.ds(start, 32) if half is None else pl.ds(start + half * 16, 16)

    class Gather:
        def __init__(self, tile):
            self.tile = tile
            self.a = ring_gather(x_ring, lambda i, h: tile.at[i, y, rows_of(0, h)])
            self.b = ring_gather(y_ring, lambda j, h: tile.at[x, j, rows_of(32, h)])

        def inner(self):
            self.a[0](2)
            self.b[0](2)

        def outer(self):
            tile = self.tile
            self.a[1]()
            self.a = ring_gather(y_ring, lambda j, h: tile.at[part_of(4, h), j, pl.ds(0, 32)])
            self.b[1]()
            self.b = ring_gather(x_ring, lambda i, h: tile.at[i, part_of(4, h), pl.ds(32, 32)])

        def done(self):
            self.a[1]()
            self.b[1]()

    class Reduce:
        def __init__(self, tile, got):
            self.tile, self.got = tile, got
            far, full = got[0], got[1]
            self.a = ring_reduce(
                y_ring, lambda j: tile.at[:, j, pl.ds(0, 32)],
                lambda d: far.at[0, d], lambda d, s: full.at[0, d],
            )
            self.b = ring_reduce(
                x_ring, lambda i: tile.at[i, :, pl.ds(32, 32)],
                lambda d: far.at[1, d], lambda d, s: full.at[1, d],
            )

        def second(self):
            self.a[0](2)
            self.b[0](2)

        def inner(self):
            tile = self.tile
            far, full = self.got[2], self.got[3]
            self.a[1]()
            self.a = ring_reduce(
                x_ring, lambda i: tile.at[i, y, pl.ds(0, 32)],
                lambda d: far.at[0, d], lambda d, s: full.at[0, d],
            )
            self.b[1]()
            self.b = ring_reduce(
                y_ring, lambda j: tile.at[x, j, pl.ds(32, 32)],
                lambda d: far.at[1, d], lambda d, s: full.at[1, d],
            )

        def total(self):
            self.a[1]()
            self.b[1]()

    def spread(src, slot):
        copies = [
            send(src.at[:, rem(z + d, 8)], slot, zs[d - 1]) for d in range(1, 8)
        ]
        return place(src.at[:, z], slot), copies

    def qw_slot(zz, half):
        return w3.at[lax.rem(zz, 2), part_of(1024, half), at128(lax.div(zz, 2))]

    def km_slot(zz, half):
        return km.at[lax.rem(zz, 2), part_of(2, half), lax.div(zz, 2)]

    def og_slot(zz, half):
        return ogt.at[lax.div(zz, 2), part_of(128, half), at1024(lax.rem(zz, 2))]

    li_slot = lit.at[x, y, :, at1024(zlo)]
    li_own = place(li.at[zlo], li_slot)
    li_sent = send(li.at[1 - zlo], li_slot, zpartner)
    for r in range(2):
        post(
            ow.at[pl.ds(r * 64, 64)], owt.at[x, yhi * 2 + r, :, at1024(zlo)], spread_ow[r], zlo
        )
    km_own = place(kw, km.at[zlo, ylo, zh])
    km_sent = send(kw, km.at[zlo, ylo, zh], ypartner)
    qw_own = place(qw, qw_slot(z, None))
    og_own = place(og, og_slot(z, None))
    q_own, q_copies = spread(q, qkt.at[quarter, :, :, at128(zh)])
    qw_own.wait()
    qw_step, qw_done = ring_gather(z_ring, qw_slot)
    k_own, k_copies = spread(k, kbuf.at[zh, zlo])
    li_own.wait()
    li_sent.wait_recv()
    li_all = Gather(lit)
    for b in range(2):
        collect(owt.at[x, y, :, pl.ds(b * 1024, 1024)], b)
    ow_all = Gather(owt)
    for j in range(4):
        post(ao.at[j], aot.at[yhi, :, :, at128(x)], spread_ao[j], 2 + x)
    km_own.wait()
    km_sent.wait_recv()
    km_step, km_done = ring_gather(z_ring, km_slot)
    li_all.inner()
    ow_all.inner()
    qw_step(2)
    og_own.wait()
    og_step, og_done = ring_gather(z_ring, og_slot)
    km_step(2)
    li_all.outer()
    qw_step(3)
    km_step(3)
    ow_all.outer()
    og_step(2)
    qw_step(4)
    km_step(4)
    li_all.inner()
    og_step(3)
    ow_all.inner()

    k_own.wait()
    arrive(k_copies)
    for lo in range(2):
        total = kbuf[0, lo].astype(F32)
        for h in range(1, 4):
            total = total + kbuf[h, lo].astype(F32)
        high = total.astype(BF16)
        qkt[lo * 2 + col, :, :, pl.ds(512, 128)] = high
        qkt[lo * 2 + col, :, :, pl.ds(640, 128)] = (total - high.astype(F32)).astype(BF16)
    q_own.wait()
    arrive(q_copies)
    q_shared = [send(v, v, sibling) for v in [qkt.at[lo * 2 + col] for lo in range(2)]]

    qw_done()
    km_done()
    for lo in range(2):
        keys = km[lo].reshape(1024, 128)
        w3[lo, :, pl.ds(512, 128)] = keys
        w3[lo, :, pl.ds(640, 128)] = keys
    arrive(q_shared)
    for lo in range(2):
        def block(i, _, lo=lo):
            cols = pl.ds(pl.multiple_of(lo * 1024 + i * 256, 256), 256)
            rows = pl.ds(pl.multiple_of(i * 256, 256), 256)
            part = lax.dot_general(
                qkt[...].reshape(1024, 768), w3[lo, rows, :],
                (((1,), (1,)), ((), ())), preferred_element_type=F32,
            )
            ig[:, :, :, cols] = part.reshape(4, 4, 64, 256)
            return 0
        lax.fori_loop(0, 4, block, 0)
    ig_sum = Reduce(ig, ig_got)
    og_step(4)

    li_all.done()
    for lo in range(2):
        def block(i, _, lo=lo):
            cols = pl.ds(pl.multiple_of(lo * 1024 + i * 256, 256), 256)
            rows = pl.ds(pl.multiple_of(i * 256, 256), 256)
            part = lax.dot_general(
                lit[:, :, :, cols].reshape(1024, 256), qkt[...].reshape(1024, 768),
                (((0,), (0,)), ((), ())), preferred_element_type=F32,
            )
            for h in range(4):
                qwg[lo, h, rows, :] = part[:, h * 128 : h * 128 + 128]
            sums = part[:, 512:640] + part[:, 640:768]
            kwg[lo, lax.div(i, 2), pl.ds(lax.rem(i, 2) * 2, 2)] = sums.reshape(2, 128, 128)
            return 0
        lax.fori_loop(0, 4, block, 0)
    qwg_step, qwg_total = ring_reduce(
        z_ring, lambda zz: qwg.at[lax.rem(zz, 2), lax.div(zz, 2)],
        lambda d: qw_far.at[d], lambda d, s: qw_full.at[d, s],
    )
    kwg_step, kwg_total = ring_reduce(
        z_ring, lambda zz: kwg.at[lax.rem(zz, 2), :, lax.div(zz, 2)],
        lambda d: kw_far.at[d], lambda d, s: kw_full.at[d, s],
    )

    for i in range(4):
        collect(aot.at[col, :, :, pl.ds(i * 128, 128)], 2 + i)
    ao_shared = send(aot.at[col], aot.at[col], sibling)
    ow_all.done()
    og_done()
    for h in range(2):
        part = lax.dot_general(
            ogt[...].reshape(512, 2048), owt[:, pl.ds(2 * h, 2)].reshape(512, 2048),
            (((1,), (1,)), ((), ())), preferred_element_type=F32,
        ).reshape(4, 2, 64, 512)
        owg[h, :, :, pl.ds(0, 512)] = part[:, 0]
        owg[h, :, :, pl.ds(512, 512)] = part[:, 1]
    ag_sent = send(owg.at[1 - col, :, :, pl.ds(0, 1024)], agr, sibling)
    qwg_step(2)
    kwg_step(2)
    ag_sent.wait()
    for half in range(2):
        cols = pl.ds(half * 512, 512)
        agb[:, pl.ds(half * 64, 64), :] = (owg[col, :, :, cols] + agr[:, :, cols]).astype(BF16)

    ao_shared.wait_recv()
    for h in range(2):
        def block(i, _, h=h):
            cols = pl.ds(pl.multiple_of(i * 512, 512), 512)
            part = lax.dot_general(
                aot[h].reshape(512, 512), ogt[:, :, cols].reshape(512, 512),
                (((0,), (0,)), ((), ())), preferred_element_type=F32,
            )
            owg[:, pl.ds(2 * h, 2), :, cols] = part.reshape(4, 2, 64, 512)
            return 0
        lax.fori_loop(0, 4, block, 0)
    owg_sum = Reduce(owg, owg_got)
    for i in range(4):
        post(agb.at[:, :, pl.ds(i * 128, 128)], ag_out.at[y], return_ag[i], 6 + y)

    ig_sum.second()
    qwg_step(3)
    kwg_step(3)
    owg_sum.second()
    qwg_step(4)
    kwg_step(4)
    ig_sum.inner()
    ig_sum.second()
    kwg_mine = kwg_total()
    kwg_sent = send(kwg_mine.at[1 - ylo], kwy, ypartner)
    qwg_own = place(qwg_total(), qwg_out)
    owg_sum.inner()
    ig_sum.total()
    fin[...] = ig[x, y].astype(BF16)
    ig_own = place(fin.at[:, at1024(zlo)], ig_out.at[zlo])
    ig_sent = send(fin.at[:, at1024(1 - zlo)], ig_out.at[zlo], zpartner)
    kwg_sent.wait_recv()
    kwy[...] = kwy[...] + kwg_mine[ylo]
    kwg_own = place(kwy, kwg_out)
    owg_sum.second()
    owg_sum.total()
    for b in range(2):
        post(
            owg.at[x, y, :, pl.ds(b * 1024, 1024)],
            owg_out.at[pl.ds(pl.multiple_of(ylo * 64, 64), 64)], return_ow[b], 10 + ylo,
        )
    for copy in sent:
        if copy is not ag_sent:
            copy.wait_send()
    for copy, own in guarded:
        @pl.when(jnp.logical_not(own))
        def _(copy=copy):
            copy.wait_send()
    for j in range(4):
        collect(ag_out.at[j], 6 + j)
    for r in range(2):
        collect(owg_out.at[pl.ds(r * 64, 64)], 10 + r)
    ig_sent.wait_recv()
    for copy in (qwg_own, ig_own, kwg_own):
        copy.wait()


def shards(layer_input, attn_out, out_grad, q_grad, k_grad, q_weight, k_weight, o_weight):
    shapes = (
        ((2, 64, 1024), BF16), ((4, 4, 128, 128), BF16), ((1024, 128), F32),
        ((128, 128), F32), ((128, 1024), F32),
    )
    vmem = pltpu.VMEM
    def reduction():
        return (
            vmem((2, 2, 2, 32, 2048), F32), vmem((2, 2, 4, 32, 2048), F32),
            vmem((2, 2, 16, 2048), F32), vmem((2, 2, 32, 2048), F32),
        )

    scratch = [
        vmem((4, 4, 64, 2048), BF16),
        vmem((4, 4, 64, 2048), BF16),
        vmem((4, 128, 2048), BF16),
        vmem((4, 4, 64, 768), BF16),
        vmem((2, 4, 128, 512), BF16),
        vmem((2, 1024, 768), BF16),
        vmem((2, 2, 4, 128, 128), BF16),
        vmem((4, 2, 4, 64, 128), BF16),
        vmem((4, 4, 64, 2048), F32),
        vmem((4, 4, 64, 2048), F32),
        reduction(),
        reduction(),
        vmem((2, 4, 1024, 128), F32),
        vmem((2, 2, 4, 128, 128), F32),
        vmem((2, 512, 128), F32),
        vmem((2, 3, 1024, 128), F32),
        vmem((2, 1, 128, 128), F32),
        vmem((2, 3, 2, 128, 128), F32),
        vmem((128, 128), F32),
        vmem((4, 64, 1024), F32),
        vmem((4, 128, 512), BF16),
        vmem((64, 2048), BF16),
        pltpu.SemaphoreType.DMA((COPIES,)),
        pltpu.SemaphoreType.DMA((COPIES,)),
        pltpu.SemaphoreType.DMA((16,)),
        pltpu.SemaphoreType.DMA((32,)),
    ]
    ig, ag, qwg, kwg, owg = pl.pallas_call(
        kernel,
        out_shape=[jax.ShapeDtypeStruct(*shape) for shape in shapes],
        in_specs=[pl.BlockSpec(memory_space=pl.ANY)] * 8,
        out_specs=[pl.BlockSpec(memory_space=pl.ANY)] * 5,
        scratch_shapes=scratch,
        compiler_params=pltpu.CompilerParams(
            collective_id=0, has_side_effects=True, vmem_limit_bytes=63 * 2**20
        ),
        cost_estimate=pl.CostEstimate(flops=14 * 10**9, bytes_accessed=5 * 10**6, transcendentals=0),
    )(
        layer_input.reshape(2, 64, 1024),
        attn_out.reshape(4, 4, 128, 128),
        out_grad,
        q_grad.reshape(4, 8, 64, 128),
        k_grad.reshape(4, 8, 64, 128),
        q_weight,
        k_weight[0],
        o_weight,
    )
    return (
        ig.reshape(128, 1024),
        ag.reshape(2048, 128),
        qwg,
        kwg[None],
        owg,
    )


def solution(mesh):
    return jax.shard_map(
        shards,
        mesh=mesh,
        in_specs=(
            P("seq", ("row", "col")),
            P(("row", "col"), "seq"),
            P("seq", ("row", "col")),
            P(("row", "col"), "seq"),
            P(("row", "col"), "seq"),
            P(("row", "col"), "seq"),
            P("seq", ("row", "col"), None),
            P("seq", ("row", "col")),
        ),
        out_specs=(
            P("seq", ("row", "col")),
            P(("row", "col"), "seq"),
            P(("row", "col"), "seq"),
            P("seq", ("row", "col"), None),
            P("seq", ("row", "col")),
        ),
        check_vma=False,
    )
```

```python
import jax
import jax.numpy as jnp
from jax import lax
from jax.experimental import pallas as pl
from jax.experimental.pallas import tpu as pltpu
from jax.sharding import PartitionSpec as P

MESH = pl.DeviceIdType.MESH
COPIES = 160
F32 = jnp.float32
BF16 = jnp.bfloat16


def rem(value, size):
    return lax.rem(value + size, size)


def at128(index):
    return pl.ds(pl.multiple_of(index * 128, 128), 128)


def at1024(index):
    return pl.ds(pl.multiple_of(index * 1024, 1024), 1024)


def kernel(
    li, ao, og, q, k, qw, kw, ow,
    ig_out, ag_out, qwg_out, kwg_out, owg_out,
    lit, owt, ogt, qkt, aot, w3, km, kbuf,
    ig, owg, ig_got, owg_got,
    qwg, kwg, qw_far, qw_full, kw_far, kw_full, kwy,
    agr, agb, fin,
    ssem, rsem, lsem, gsem,
):
    seq = lax.axis_index("seq")
    x, y, zh = lax.div(seq, 16), lax.rem(lax.div(seq, 4), 4), lax.rem(seq, 4)
    zlo, col = lax.axis_index("row"), lax.axis_index("col")
    z = zh * 2 + zlo
    yhi, ylo = lax.div(y, 2), lax.rem(y, 2)
    quarter = zlo * 2 + col

    def at(xx, yy, lo, core):
        return (xx * 16 + yy * 4 + zh, lo, core)

    def device(dx, dy, dz):
        zz = rem(z + dz, 8)
        return (
            rem(x + dx, 4) * 16 + rem(y + dy, 4) * 4 + lax.div(zz, 2), lax.rem(zz, 2), col
        )

    zs = [device(0, 0, d) for d in range(1, 8)]
    sibling = at(x, y, zlo, 1 - col)
    zpartner = device(0, 0, 1 - 2 * zlo)
    ypartner = device(0, 1 - 2 * ylo, 0)
    x_ring = (4, x, device(-1, 0, 0), device(1, 0, 0))
    y_ring = (4, y, device(0, -1, 0), device(0, 1, 0))
    z_ring = (8, z, device(0, 0, -1), device(0, 0, 1))

    square = ylo == zlo
    home = jnp.logical_and(x == quarter, y == col * 2 + zlo)
    spread_ow = [(at(x, yhi * 2 + r, ylo, col), jnp.logical_and(square, ylo == r)) for r in range(2)]
    return_ow = [(at(x, yhi * 2 + zlo, b, col), jnp.logical_and(square, zlo == b)) for b in range(2)]
    spread_ao = [(at(quarter, j, ylo, yhi), jnp.logical_and(home, y == j)) for j in range(4)]
    return_ag = [
        (at(i, col * 2 + zlo, lax.div(x, 2), lax.rem(x, 2)), jnp.logical_and(home, x == i))
        for i in range(4)
    ]

    barrier = pltpu.get_barrier_semaphore()
    peers = list(x_ring[2:]) + list(y_ring[2:]) + zs + [sibling]
    for peer in peers:
        pl.semaphore_signal(barrier, inc=1, device_id=peer, device_id_type=MESH)
    for peer, own in spread_ow + return_ow + spread_ao + return_ag:
        @pl.when(jnp.logical_not(own))
        def _(peer=peer):
            pl.semaphore_signal(barrier, inc=1, device_id=peer, device_id_type=MESH)
    count = len(peers) + 12 - 2 * square.astype(jnp.int32) - 2 * home.astype(jnp.int32)
    pl.semaphore_wait(barrier, count)

    sent, local, guarded = [], [], []

    def send(src, dst, to):
        n = len(sent)
        copy = pltpu.make_async_remote_copy(
            src_ref=src, dst_ref=dst, send_sem=ssem.at[n], recv_sem=rsem.at[n],
            device_id=to, device_id_type=MESH,
        )
        copy.start()
        sent.append(copy)
        return copy

    def place(src, dst):
        copy = pltpu.make_async_copy(src, dst, lsem.at[len(local)])
        copy.start()
        local.append(copy)
        return copy

    def post(src, dst, partner, slot):
        to, own = partner
        copy = pltpu.make_async_remote_copy(
            src_ref=src, dst_ref=dst, send_sem=gsem.at[16 + len(guarded)],
            recv_sem=gsem.at[slot], device_id=to, device_id_type=MESH,
        )

        @pl.when(jnp.logical_not(own))
        def _():
            copy.start()

        @pl.when(own)
        def _():
            pltpu.make_async_copy(src, dst, gsem.at[slot]).start()

        guarded.append((copy, own))

    def collect(dst, slot):
        pltpu.make_async_copy(dst, dst, gsem.at[slot]).wait()

    def arrive(copies):
        for copy in copies:
            copy.wait_recv()

    def add(dst, *parts):
        if len(dst.shape) == 3:
            def row(i, _):
                total = dst[i]
                for part in parts:
                    total = total + part[i]
                dst[i] = total
                return 0
            lax.fori_loop(0, dst.shape[0], row, 0)
        else:
            total = dst[...]
            for part in parts:
                total = total + part[...]
            dst[...] = total

    def ring_gather(ring, piece):
        n, me, left, right = ring
        own = piece(me, None)
        steps = [[send(own, own, left), send(own, own, right)]]

        def step(s):
            arrive(steps[-1])
            half = s == n // 2
            a = piece(rem(me + s - 1, n), 0 if half else None)
            b = piece(rem(me - s + 1, n), 1 if half else None)
            steps.append([send(a, a, left), send(b, b, right)])

        return step, lambda: arrive(steps[-1])

    def ring_reduce(ring, piece, far, full):
        n, me, left, right = ring
        size = far(0).shape[0]
        halves = [pl.ds(0, size), pl.ds(size, size)]
        last = n // 2
        across = piece(rem(me + last, n))
        steps = [[
            send(across.at[halves[0]], far(0), left), send(across.at[halves[1]], far(1), right)
        ]]

        def step(s):
            arrive(steps[-1])
            a, b = piece(rem(me - (last + 1 - s), n)), piece(rem(me + (last + 1 - s), n))
            if s == 2:
                add(a.at[halves[0]], far(0))
                add(b.at[halves[1]], far(1))
            else:
                add(a, full(0, s - 3))
                add(b, full(1, s - 3))
            steps.append([send(a, full(0, s - 2), left), send(b, full(1, s - 2), right)])

        def total():
            arrive(steps[-1])
            add(piece(me), full(0, last - 2), full(1, last - 2))
            return piece(me)

        return step, total

    def part_of(size, half):
        return pl.ds(0, size) if half is None else pl.ds(half * (size // 2), size // 2)

    def rows_of(start, half):
        return pl.ds(start, 32) if half is None else pl.ds(start + half * 16, 16)

    class Gather:
        def __init__(self, tile):
            self.tile = tile
            self.a = ring_gather(x_ring, lambda i, h: tile.at[i, y, rows_of(0, h)])
            self.b = ring_gather(y_ring, lambda j, h: tile.at[x, j, rows_of(32, h)])

        def inner(self):
            self.a[0](2)
            self.b[0](2)

        def outer(self):
            tile = self.tile
            self.a[1]()
            self.a = ring_gather(y_ring, lambda j, h: tile.at[part_of(4, h), j, pl.ds(0, 32)])
            self.b[1]()
            self.b = ring_gather(x_ring, lambda i, h: tile.at[i, part_of(4, h), pl.ds(32, 32)])

        def done(self):
            self.a[1]()
            self.b[1]()

    class Reduce:
        def __init__(self, tile, got):
            self.tile, self.got = tile, got
            far, full = got[0], got[1]
            self.a = ring_reduce(
                y_ring, lambda j: tile.at[:, j, pl.ds(0, 32)],
                lambda d: far.at[0, d], lambda d, s: full.at[0, d],
            )
            self.b = ring_reduce(
                x_ring, lambda i: tile.at[i, :, pl.ds(32, 32)],
                lambda d: far.at[1, d], lambda d, s: full.at[1, d],
            )

        def second(self):
            self.a[0](2)
            self.b[0](2)

        def inner(self):
            tile = self.tile
            far, full = self.got[2], self.got[3]
            self.a[1]()
            self.a = ring_reduce(
                x_ring, lambda i: tile.at[i, y, pl.ds(0, 32)],
                lambda d: far.at[0, d], lambda d, s: full.at[0, d],
            )
            self.b[1]()
            self.b = ring_reduce(
                y_ring, lambda j: tile.at[x, j, pl.ds(32, 32)],
                lambda d: far.at[1, d], lambda d, s: full.at[1, d],
            )

        def total(self):
            self.a[1]()
            self.b[1]()

    def spread(src, slot):
        copies = [
            send(src.at[:, rem(z + d, 8)], slot, zs[d - 1]) for d in range(1, 8)
        ]
        return place(src.at[:, z], slot), copies

    def qw_slot(zz, half):
        return w3.at[lax.rem(zz, 2), part_of(1024, half), at128(lax.div(zz, 2))]

    def km_slot(zz, half):
        return km.at[lax.rem(zz, 2), part_of(2, half), lax.div(zz, 2)]

    def og_slot(zz, half):
        return ogt.at[lax.div(zz, 2), part_of(128, half), at1024(lax.rem(zz, 2))]

    og_own = place(og, og_slot(z, None))
    for r in range(2):
        post(
            ow.at[pl.ds(r * 64, 64)], owt.at[x, yhi * 2 + r, :, at1024(zlo)], spread_ow[r], zlo
        )
    og_own.wait()
    og_step, og_done = ring_gather(z_ring, og_slot)
    for j in range(4):
        post(ao.at[j], aot.at[yhi, :, :, at128(x)], spread_ao[j], 2 + x)
    li_slot = lit.at[x, y, :, at1024(zlo)]
    li_own = place(li.at[zlo], li_slot)
    li_sent = send(li.at[1 - zlo], li_slot, zpartner)
    km_own = place(kw, km.at[zlo, ylo, zh])
    km_sent = send(kw, km.at[zlo, ylo, zh], ypartner)
    qw_own = place(qw, qw_slot(z, None))
    for b in range(2):
        collect(owt.at[x, y, :, pl.ds(b * 1024, 1024)], b)
    ow_all = Gather(owt)
    og_step(2)
    ow_all.inner()
    li_own.wait()
    li_sent.wait_recv()
    li_all = Gather(lit)
    og_step(3)
    q_own, q_copies = spread(q, qkt.at[quarter, :, :, at128(zh)])
    li_all.inner()
    og_step(4)
    k_own, k_copies = spread(k, kbuf.at[zh, zlo])
    qw_own.wait()
    qw_step, qw_done = ring_gather(z_ring, qw_slot)
    ow_all.outer()

    for i in range(4):
        collect(aot.at[col, :, :, pl.ds(i * 128, 128)], 2 + i)
    ao_shared = send(aot.at[col], aot.at[col], sibling)
    og_done()
    ao_shared.wait_recv()
    for h in range(2):
        def block(i, _, h=h):
            cols = pl.ds(pl.multiple_of(i * 512, 512), 512)
            part = lax.dot_general(
                aot[h].reshape(512, 512), ogt[:, :, cols].reshape(512, 512),
                (((0,), (0,)), ((), ())), preferred_element_type=F32,
            )
            owg[:, pl.ds(2 * h, 2), :, cols] = part.reshape(4, 2, 64, 512)
            return 0
        lax.fori_loop(0, 4, block, 0)
    owg_sum = Reduce(owg, owg_got)
    km_own.wait()
    km_sent.wait_recv()
    km_step, km_done = ring_gather(z_ring, km_slot)
    qw_step(2)
    ow_all.inner()
    li_all.outer()

    ow_all.done()
    for h in range(2):
        part = lax.dot_general(
            ogt[...].reshape(512, 2048), owt[:, pl.ds(2 * h, 2)].reshape(512, 2048),
            (((1,), (1,)), ((), ())), preferred_element_type=F32,
        ).reshape(4, 2, 64, 512)
        ig[h, :, :, pl.ds(0, 512)] = part[:, 0]
        ig[h, :, :, pl.ds(512, 512)] = part[:, 1]
    ag_sent = send(ig.at[1 - col, :, :, pl.ds(0, 1024)], agr, sibling)
    qw_step(3)
    km_step(2)
    ag_sent.wait()
    for half in range(2):
        cols = pl.ds(half * 512, 512)
        agb[:, pl.ds(half * 64, 64), :] = (ig[col, :, :, cols] + agr[:, :, cols]).astype(BF16)
    owg_sum.second()
    for i in range(4):
        post(agb.at[:, :, pl.ds(i * 128, 128)], ag_out.at[y], return_ag[i], 6 + y)
    li_all.inner()
    qw_step(4)
    km_step(3)

    k_own.wait()
    arrive(k_copies)
    for lo in range(2):
        total = kbuf[0, lo].astype(F32)
        for h in range(1, 4):
            total = total + kbuf[h, lo].astype(F32)
        high = total.astype(BF16)
        qkt[lo * 2 + col, :, :, pl.ds(512, 128)] = high
        qkt[lo * 2 + col, :, :, pl.ds(640, 128)] = (total - high.astype(F32)).astype(BF16)
    q_own.wait()
    arrive(q_copies)
    q_shared = [send(v, v, sibling) for v in [qkt.at[lo * 2 + col] for lo in range(2)]]
    km_step(4)
    li_all.done()
    arrive(q_shared)

    for lo in range(2):
        def block(i, _, lo=lo):
            cols = pl.ds(pl.multiple_of(lo * 1024 + i * 256, 256), 256)
            rows = pl.ds(pl.multiple_of(i * 256, 256), 256)
            part = lax.dot_general(
                lit[:, :, :, cols].reshape(1024, 256), qkt[...].reshape(1024, 768),
                (((0,), (0,)), ((), ())), preferred_element_type=F32,
            )
            for h in range(4):
                qwg[lo, h, rows, :] = part[:, h * 128 : h * 128 + 128]
            sums = part[:, 512:640] + part[:, 640:768]
            kwg[lo, lax.div(i, 2), pl.ds(lax.rem(i, 2) * 2, 2)] = sums.reshape(2, 128, 128)
            return 0
        lax.fori_loop(0, 4, block, 0)
    qwg_step, qwg_total = ring_reduce(
        z_ring, lambda zz: qwg.at[lax.rem(zz, 2), lax.div(zz, 2)],
        lambda d: qw_far.at[d], lambda d, s: qw_full.at[d, s],
    )
    kwg_step, kwg_total = ring_reduce(
        z_ring, lambda zz: kwg.at[lax.rem(zz, 2), :, lax.div(zz, 2)],
        lambda d: kw_far.at[d], lambda d, s: kw_full.at[d, s],
    )

    qw_done()
    km_done()
    for lo in range(2):
        keys = km[lo].reshape(1024, 128)
        w3[lo, :, pl.ds(512, 128)] = keys
        w3[lo, :, pl.ds(640, 128)] = keys
    for lo in range(2):
        def block(i, _, lo=lo):
            cols = pl.ds(pl.multiple_of(lo * 1024 + i * 256, 256), 256)
            rows = pl.ds(pl.multiple_of(i * 256, 256), 256)
            part = lax.dot_general(
                qkt[...].reshape(1024, 768), w3[lo, rows, :],
                (((1,), (1,)), ((), ())), preferred_element_type=F32,
            )
            ig[:, :, :, cols] = part.reshape(4, 4, 64, 256)
            return 0
        lax.fori_loop(0, 4, block, 0)
    ig_sum = Reduce(ig, ig_got)

    qwg_step(2)
    kwg_step(2)
    owg_sum.inner()
    qwg_step(3)
    kwg_step(3)
    owg_sum.second()
    ig_sum.second()
    qwg_step(4)
    kwg_step(4)
    owg_sum.total()
    for b in range(2):
        post(
            owg.at[x, y, :, pl.ds(b * 1024, 1024)],
            owg_out.at[pl.ds(pl.multiple_of(ylo * 64, 64), 64)], return_ow[b], 10 + ylo,
        )
    kwg_mine = kwg_total()
    kwg_sent = send(kwg_mine.at[1 - ylo], kwy, ypartner)
    qwg_own = place(qwg_total(), qwg_out)
    ig_sum.inner()
    kwg_sent.wait_recv()
    kwy[...] = kwy[...] + kwg_mine[ylo]
    kwg_own = place(kwy, kwg_out)
    ig_sum.second()
    ig_sum.total()
    fin[...] = ig[x, y].astype(BF16)
    ig_own = place(fin.at[:, at1024(zlo)], ig_out.at[zlo])
    ig_sent = send(fin.at[:, at1024(1 - zlo)], ig_out.at[zlo], zpartner)
    for copy in sent:
        if copy is not ag_sent:
            copy.wait_send()
    for copy, own in guarded:
        @pl.when(jnp.logical_not(own))
        def _(copy=copy):
            copy.wait_send()
    for j in range(4):
        collect(ag_out.at[j], 6 + j)
    for r in range(2):
        collect(owg_out.at[pl.ds(r * 64, 64)], 10 + r)
    ig_sent.wait_recv()
    for copy in (qwg_own, ig_own, kwg_own):
        copy.wait()


def finish(*refs):
    sems = refs[-1]
    count = (len(refs) - 1) // 2
    copies = [
        pltpu.make_async_copy(refs[n], refs[count + n], sems.at[n]) for n in range(count)
    ]
    for copy in copies:
        copy.start()
    for copy in copies:
        copy.wait()


def shards(layer_input, attn_out, out_grad, q_grad, k_grad, q_weight, k_weight, o_weight):
    shapes = (
        ((2, 64, 1024), BF16), ((4, 4, 128, 128), BF16), ((1024, 128), F32),
        ((128, 128), F32), ((128, 1024), F32),
    )
    vmem = pltpu.VMEM
    def reduction():
        return (
            vmem((2, 2, 2, 32, 2048), F32), vmem((2, 2, 4, 32, 2048), F32),
            vmem((2, 2, 16, 2048), F32), vmem((2, 2, 32, 2048), F32),
        )

    scratch = [
        vmem((4, 4, 64, 2048), BF16),
        vmem((4, 4, 64, 2048), BF16),
        vmem((4, 128, 2048), BF16),
        vmem((4, 4, 64, 768), BF16),
        vmem((2, 4, 128, 512), BF16),
        vmem((2, 1024, 768), BF16),
        vmem((2, 2, 4, 128, 128), BF16),
        vmem((4, 2, 4, 64, 128), BF16),
        vmem((4, 4, 64, 2048), F32),
        vmem((4, 4, 64, 2048), F32),
        reduction(),
        reduction(),
        vmem((2, 4, 1024, 128), F32),
        vmem((2, 2, 4, 128, 128), F32),
        vmem((2, 512, 128), F32),
        vmem((2, 3, 1024, 128), F32),
        vmem((2, 1, 128, 128), F32),
        vmem((2, 3, 2, 128, 128), F32),
        vmem((128, 128), F32),
        vmem((4, 64, 1024), F32),
        vmem((4, 128, 512), BF16),
        vmem((64, 2048), BF16),
        pltpu.SemaphoreType.DMA((COPIES,)),
        pltpu.SemaphoreType.DMA((COPIES,)),
        pltpu.SemaphoreType.DMA((16,)),
        pltpu.SemaphoreType.DMA((32,)),
    ]
    ig, ag, qwg, kwg, owg = pl.pallas_call(
        kernel,
        out_shape=[jax.ShapeDtypeStruct(*shape) for shape in shapes],
        in_specs=[pl.BlockSpec(memory_space=pl.ANY)] * 8,
        out_specs=[pl.BlockSpec(memory_space=pl.ANY)] * 5,
        scratch_shapes=scratch,
        compiler_params=pltpu.CompilerParams(
            collective_id=0, has_side_effects=True, vmem_limit_bytes=63 * 2**20
        ),
        cost_estimate=pl.CostEstimate(flops=14 * 10**9, bytes_accessed=5 * 10**6, transcendentals=0),
    )(
        layer_input.reshape(2, 64, 1024),
        attn_out.reshape(4, 4, 128, 128),
        out_grad,
        q_grad.reshape(4, 8, 64, 128),
        k_grad.reshape(4, 8, 64, 128),
        q_weight,
        k_weight[0],
        o_weight,
    )
    parts = (ig.reshape(128, 1024), ag.reshape(2048, 128), qwg, kwg, owg)
    ig, ag, qwg, kwg, owg = pl.pallas_call(
        finish,
        out_shape=[jax.ShapeDtypeStruct(part.shape, part.dtype) for part in parts],
        in_specs=[pl.BlockSpec(memory_space=pl.ANY)] * 5,
        out_specs=[pl.BlockSpec(memory_space=pl.ANY)] * 5,
        scratch_shapes=[pltpu.SemaphoreType.DMA((5,))],
        compiler_params=pltpu.CompilerParams(vmem_limit_bytes=63 * 2**20),
    )(*parts)
    return ig, ag, qwg, kwg[None], owg


def solution(mesh):
    return jax.shard_map(
        shards,
        mesh=mesh,
        in_specs=(
            P("seq", ("row", "col")),
            P(("row", "col"), "seq"),
            P("seq", ("row", "col")),
            P(("row", "col"), "seq"),
            P(("row", "col"), "seq"),
            P(("row", "col"), "seq"),
            P("seq", ("row", "col"), None),
            P("seq", ("row", "col")),
        ),
        out_specs=(
            P("seq", ("row", "col")),
            P(("row", "col"), "seq"),
            P(("row", "col"), "seq"),
            P("seq", ("row", "col"), None),
            P("seq", ("row", "col")),
        ),
        check_vma=False,
    )
```

```python
import jax
import jax.numpy as jnp
from jax import lax
from jax.experimental import pallas as pl
from jax.experimental.pallas import tpu as pltpu
from jax.sharding import PartitionSpec as P

MESH = pl.DeviceIdType.MESH
COPIES = 160
F32 = jnp.float32
BF16 = jnp.bfloat16


def rem(value, size):
    return lax.rem(value + size, size)


def at128(index):
    return pl.ds(pl.multiple_of(index * 128, 128), 128)


def at1024(index):
    return pl.ds(pl.multiple_of(index * 1024, 1024), 1024)


def kernel(
    li, ao, og, q, k, qw, kw, ow,
    ig_out, ag_out, qwg_out, kwg_out, owg_out,
    lit, owt, ogt, qkt, aot, w3, km, kbuf,
    ig, owg, ig_got, owg_got,
    qwg, kwg, qw_far, qw_full, kw_far, kw_full, kwy,
    agr, agb, fin,
    ssem, rsem, lsem, gsem,
):
    seq = lax.axis_index("seq")
    x, y, zh = lax.div(seq, 16), lax.rem(lax.div(seq, 4), 4), lax.rem(seq, 4)
    zlo, col = lax.axis_index("row"), lax.axis_index("col")
    z = zh * 2 + zlo
    yhi, ylo = lax.div(y, 2), lax.rem(y, 2)
    quarter = zlo * 2 + col

    def at(xx, yy, lo, core):
        return (xx * 16 + yy * 4 + zh, lo, core)

    def device(dx, dy, dz):
        zz = rem(z + dz, 8)
        return (
            rem(x + dx, 4) * 16 + rem(y + dy, 4) * 4 + lax.div(zz, 2), lax.rem(zz, 2), col
        )

    zs = [device(0, 0, d) for d in range(1, 8)]
    sibling = at(x, y, zlo, 1 - col)
    zpartner = device(0, 0, 1 - 2 * zlo)
    ypartner = device(0, 1 - 2 * ylo, 0)
    x_ring = (4, x, device(-1, 0, 0), device(1, 0, 0))
    y_ring = (4, y, device(0, -1, 0), device(0, 1, 0))
    z_ring = (8, z, device(0, 0, -1), device(0, 0, 1))

    square = ylo == zlo
    home = jnp.logical_and(x == quarter, y == col * 2 + zlo)
    spread_ow = [(at(x, yhi * 2 + r, ylo, col), jnp.logical_and(square, ylo == r)) for r in range(2)]
    return_ow = [(at(x, yhi * 2 + zlo, b, col), jnp.logical_and(square, zlo == b)) for b in range(2)]
    spread_ao = [(at(quarter, j, ylo, yhi), jnp.logical_and(home, y == j)) for j in range(4)]
    return_ag = [
        (at(i, col * 2 + zlo, lax.div(x, 2), lax.rem(x, 2)), jnp.logical_and(home, x == i))
        for i in range(4)
    ]

    barrier = pltpu.get_barrier_semaphore()
    peers = list(x_ring[2:]) + list(y_ring[2:]) + zs + [sibling]
    for peer in peers:
        pl.semaphore_signal(barrier, inc=1, device_id=peer, device_id_type=MESH)
    for peer, own in spread_ow + return_ow + spread_ao + return_ag:
        @pl.when(jnp.logical_not(own))
        def _(peer=peer):
            pl.semaphore_signal(barrier, inc=1, device_id=peer, device_id_type=MESH)
    count = len(peers) + 12 - 2 * square.astype(jnp.int32) - 2 * home.astype(jnp.int32)
    pl.semaphore_wait(barrier, count)

    sent, local, guarded = [], [], []

    def send(src, dst, to):
        n = len(sent)
        copy = pltpu.make_async_remote_copy(
            src_ref=src, dst_ref=dst, send_sem=ssem.at[n], recv_sem=rsem.at[n],
            device_id=to, device_id_type=MESH,
        )
        copy.start()
        sent.append(copy)
        return copy

    def place(src, dst):
        copy = pltpu.make_async_copy(src, dst, lsem.at[len(local)])
        copy.start()
        local.append(copy)
        return copy

    def post(src, dst, partner, slot):
        to, own = partner
        copy = pltpu.make_async_remote_copy(
            src_ref=src, dst_ref=dst, send_sem=gsem.at[16 + len(guarded)],
            recv_sem=gsem.at[slot], device_id=to, device_id_type=MESH,
        )

        @pl.when(jnp.logical_not(own))
        def _():
            copy.start()

        @pl.when(own)
        def _():
            pltpu.make_async_copy(src, dst, gsem.at[slot]).start()

        guarded.append((copy, own))

    def collect(dst, slot):
        pltpu.make_async_copy(dst, dst, gsem.at[slot]).wait()

    def arrive(copies):
        for copy in copies:
            copy.wait_recv()

    def add(dst, *parts):
        if len(dst.shape) == 3:
            def row(i, _):
                total = dst[i]
                for part in parts:
                    total = total + part[i]
                dst[i] = total
                return 0
            lax.fori_loop(0, dst.shape[0], row, 0)
        else:
            total = dst[...]
            for part in parts:
                total = total + part[...]
            dst[...] = total

    def ring_gather(ring, piece):
        n, me, left, right = ring
        own = piece(me, None)
        steps = [[send(own, own, left), send(own, own, right)]]

        def step(s):
            arrive(steps[-1])
            half = s == n // 2
            a = piece(rem(me + s - 1, n), 0 if half else None)
            b = piece(rem(me - s + 1, n), 1 if half else None)
            steps.append([send(a, a, left), send(b, b, right)])

        return step, lambda: arrive(steps[-1])

    def ring_reduce(ring, piece, far, full):
        n, me, left, right = ring
        size = far(0).shape[0]
        halves = [pl.ds(0, size), pl.ds(size, size)]
        last = n // 2
        across = piece(rem(me + last, n))
        steps = [[
            send(across.at[halves[0]], far(0), left), send(across.at[halves[1]], far(1), right)
        ]]

        def step(s):
            arrive(steps[-1])
            a, b = piece(rem(me - (last + 1 - s), n)), piece(rem(me + (last + 1 - s), n))
            if s == 2:
                add(a.at[halves[0]], far(0))
                add(b.at[halves[1]], far(1))
            else:
                add(a, full(0, s - 3))
                add(b, full(1, s - 3))
            steps.append([send(a, full(0, s - 2), left), send(b, full(1, s - 2), right)])

        def total():
            arrive(steps[-1])
            add(piece(me), full(0, last - 2), full(1, last - 2))
            return piece(me)

        return step, total

    def part_of(size, half):
        return pl.ds(0, size) if half is None else pl.ds(half * (size // 2), size // 2)

    def rows_of(start, half):
        return pl.ds(start, 32) if half is None else pl.ds(start + half * 16, 16)

    class Gather:
        def __init__(self, tile):
            self.tile = tile
            self.a = ring_gather(x_ring, lambda i, h: tile.at[i, y, rows_of(0, h)])
            self.b = ring_gather(y_ring, lambda j, h: tile.at[x, j, rows_of(32, h)])

        def inner(self):
            self.a[0](2)
            self.b[0](2)

        def outer(self):
            tile = self.tile
            self.a[1]()
            self.a = ring_gather(y_ring, lambda j, h: tile.at[part_of(4, h), j, pl.ds(0, 32)])
            self.b[1]()
            self.b = ring_gather(x_ring, lambda i, h: tile.at[i, part_of(4, h), pl.ds(32, 32)])

        def done(self):
            self.a[1]()
            self.b[1]()

    class Reduce:
        def __init__(self, tile, got):
            self.tile, self.got = tile, got
            far, full = got[0], got[1]
            self.a = ring_reduce(
                y_ring, lambda j: tile.at[:, j, pl.ds(0, 32)],
                lambda d: far.at[0, d], lambda d, s: full.at[0, d],
            )
            self.b = ring_reduce(
                x_ring, lambda i: tile.at[i, :, pl.ds(32, 32)],
                lambda d: far.at[1, d], lambda d, s: full.at[1, d],
            )

        def second(self):
            self.a[0](2)
            self.b[0](2)

        def inner(self):
            tile = self.tile
            far, full = self.got[2], self.got[3]
            self.a[1]()
            self.a = ring_reduce(
                x_ring, lambda i: tile.at[i, y, pl.ds(0, 32)],
                lambda d: far.at[0, d], lambda d, s: full.at[0, d],
            )
            self.b[1]()
            self.b = ring_reduce(
                y_ring, lambda j: tile.at[x, j, pl.ds(32, 32)],
                lambda d: far.at[1, d], lambda d, s: full.at[1, d],
            )

        def total(self):
            self.a[1]()
            self.b[1]()

    def spread(src, slot):
        copies = [
            send(src.at[:, rem(z + d, 8)], slot, zs[d - 1]) for d in range(1, 8)
        ]
        return place(src.at[:, z], slot), copies

    def qw_slot(zz, half):
        return w3.at[lax.rem(zz, 2), part_of(1024, half), at128(lax.div(zz, 2))]

    def km_slot(zz, half):
        return km.at[lax.rem(zz, 2), part_of(2, half), lax.div(zz, 2)]

    def og_slot(zz, half):
        return ogt.at[lax.div(zz, 2), part_of(128, half), at1024(lax.rem(zz, 2))]

    for j in range(4):
        post(ao.at[j], aot.at[yhi, :, :, at128(x)], spread_ao[j], 2 + x)
    for r in range(2):
        post(
            ow.at[pl.ds(r * 64, 64)], owt.at[x, yhi * 2 + r, :, at1024(zlo)], spread_ow[r], zlo
        )
    og_own = place(og, og_slot(z, None))
    li_slot = lit.at[x, y, :, at1024(zlo)]
    li_own = place(li.at[zlo], li_slot)
    li_sent = send(li.at[1 - zlo], li_slot, zpartner)
    for b in range(2):
        collect(owt.at[x, y, :, pl.ds(b * 1024, 1024)], b)
    ow_all = Gather(owt)
    og_own.wait()
    og_step, og_done = ring_gather(z_ring, og_slot)
    li_own.wait()
    li_sent.wait_recv()
    li_all = Gather(lit)
    ow_all.inner()
    q_own, q_copies = spread(q, qkt.at[quarter, :, :, at128(zh)])
    li_all.inner()
    og_step(2)
    km_own = place(kw, km.at[zlo, ylo, zh])
    km_sent = send(kw, km.at[zlo, ylo, zh], ypartner)
    ow_all.outer()
    for i in range(4):
        collect(aot.at[col, :, :, pl.ds(i * 128, 128)], 2 + i)
    ao_shared = send(aot.at[col], aot.at[col], sibling)
    km_own.wait()
    km_sent.wait_recv()
    km_step, km_done = ring_gather(z_ring, km_slot)
    li_all.outer()
    og_step(3)
    qw_own = place(qw, qw_slot(z, None))
    ow_all.inner()
    km_step(2)
    og_step(4)
    km_step(3)
    qw_own.wait()
    qw_step, qw_done = ring_gather(z_ring, qw_slot)
    li_all.inner()
    og_done()
    ao_shared.wait_recv()
    for h in range(2):
        def block(i, _, h=h):
            cols = pl.ds(pl.multiple_of(i * 512, 512), 512)
            part = lax.dot_general(
                aot[h].reshape(512, 512), ogt[:, :, cols].reshape(512, 512),
                (((0,), (0,)), ((), ())), preferred_element_type=F32,
            )
            owg[:, pl.ds(2 * h, 2), :, cols] = part.reshape(4, 2, 64, 512)
            return 0
        lax.fori_loop(0, 4, block, 0)
    owg_sum = Reduce(owg, owg_got)
    k_own, k_copies = spread(k, kbuf.at[zh, zlo])
    ow_all.done()
    for h in range(2):
        part = lax.dot_general(
            ogt[...].reshape(512, 2048), owt[:, pl.ds(2 * h, 2)].reshape(512, 2048),
            (((1,), (1,)), ((), ())), preferred_element_type=F32,
        ).reshape(4, 2, 64, 512)
        ig[h, :, :, pl.ds(0, 512)] = part[:, 0]
        ig[h, :, :, pl.ds(512, 512)] = part[:, 1]
    ag_sent = send(ig.at[1 - col, :, :, pl.ds(0, 1024)], agr, sibling)
    qw_step(2)
    ag_sent.wait()
    for half in range(2):
        cols = pl.ds(half * 512, 512)
        agb[:, pl.ds(half * 64, 64), :] = (ig[col, :, :, cols] + agr[:, :, cols]).astype(BF16)
    for i in range(4):
        post(agb.at[:, :, pl.ds(i * 128, 128)], ag_out.at[y], return_ag[i], 6 + y)
    owg_sum.second()
    km_step(4)
    k_own.wait()
    arrive(k_copies)
    for lo in range(2):
        total = kbuf[0, lo].astype(F32)
        for h in range(1, 4):
            total = total + kbuf[h, lo].astype(F32)
        high = total.astype(BF16)
        qkt[lo * 2 + col, :, :, pl.ds(512, 128)] = high
        qkt[lo * 2 + col, :, :, pl.ds(640, 128)] = (total - high.astype(F32)).astype(BF16)
    qw_step(3)
    q_own.wait()
    arrive(q_copies)
    q_shared = [send(v, v, sibling) for v in [qkt.at[lo * 2 + col] for lo in range(2)]]
    qw_step(4)
    li_all.done()
    arrive(q_shared)

    for lo in range(2):
        def block(i, _, lo=lo):
            cols = pl.ds(pl.multiple_of(lo * 1024 + i * 256, 256), 256)
            rows = pl.ds(pl.multiple_of(i * 256, 256), 256)
            part = lax.dot_general(
                lit[:, :, :, cols].reshape(1024, 256), qkt[...].reshape(1024, 768),
                (((0,), (0,)), ((), ())), preferred_element_type=F32,
            )
            for h in range(4):
                qwg[lo, h, rows, :] = part[:, h * 128 : h * 128 + 128]
            sums = part[:, 512:640] + part[:, 640:768]
            kwg[lo, lax.div(i, 2), pl.ds(lax.rem(i, 2) * 2, 2)] = sums.reshape(2, 128, 128)
            return 0
        lax.fori_loop(0, 4, block, 0)
    qwg_step, qwg_total = ring_reduce(
        z_ring, lambda zz: qwg.at[lax.rem(zz, 2), lax.div(zz, 2)],
        lambda d: qw_far.at[d], lambda d, s: qw_full.at[d, s],
    )
    kwg_step, kwg_total = ring_reduce(
        z_ring, lambda zz: kwg.at[lax.rem(zz, 2), :, lax.div(zz, 2)],
        lambda d: kw_far.at[d], lambda d, s: kw_full.at[d, s],
    )

    qw_done()
    km_done()
    for lo in range(2):
        keys = km[lo].reshape(1024, 128)
        w3[lo, :, pl.ds(512, 128)] = keys
        w3[lo, :, pl.ds(640, 128)] = keys
    for lo in range(2):
        def block(i, _, lo=lo):
            cols = pl.ds(pl.multiple_of(lo * 1024 + i * 256, 256), 256)
            rows = pl.ds(pl.multiple_of(i * 256, 256), 256)
            part = lax.dot_general(
                qkt[...].reshape(1024, 768), w3[lo, rows, :],
                (((1,), (1,)), ((), ())), preferred_element_type=F32,
            )
            ig[:, :, :, cols] = part.reshape(4, 4, 64, 256)
            return 0
        lax.fori_loop(0, 4, block, 0)
    ig_sum = Reduce(ig, ig_got)

    qwg_step(2)
    ig_sum.second()
    kwg_step(2)
    kwg_step(3)
    qwg_step(3)
    kwg_step(4)
    qwg_step(4)
    kwg_mine = kwg_total()
    kwg_sent = send(kwg_mine.at[1 - ylo], kwy, ypartner)
    owg_sum.inner()
    ig_sum.inner()
    kwg_sent.wait_recv()
    kwy[...] = kwy[...] + kwg_mine[ylo]
    kwg_own = place(kwy, kwg_out)
    owg_sum.second()
    ig_sum.second()
    qwg_own = place(qwg_total(), qwg_out)
    owg_sum.total()
    for b in range(2):
        post(
            owg.at[x, y, :, pl.ds(b * 1024, 1024)],
            owg_out.at[pl.ds(pl.multiple_of(ylo * 64, 64), 64)], return_ow[b], 10 + ylo,
        )
    ig_sum.total()
    fin[...] = ig[x, y].astype(BF16)
    ig_own = place(fin.at[:, at1024(zlo)], ig_out.at[zlo])
    ig_sent = send(fin.at[:, at1024(1 - zlo)], ig_out.at[zlo], zpartner)
    for copy in sent:
        if copy is not ag_sent:
            copy.wait_send()
    for copy, own in guarded:
        @pl.when(jnp.logical_not(own))
        def _(copy=copy):
            copy.wait_send()
    for j in range(4):
        collect(ag_out.at[j], 6 + j)
    for r in range(2):
        collect(owg_out.at[pl.ds(r * 64, 64)], 10 + r)
    ig_sent.wait_recv()
    for copy in (qwg_own, ig_own, kwg_own):
        copy.wait()


def finish(*refs):
    for source, target in zip(refs[:5], refs[5:]):
        target[...] = source[...]


def shards(layer_input, attn_out, out_grad, q_grad, k_grad, q_weight, k_weight, o_weight):
    shapes = (
        ((2, 64, 1024), BF16), ((4, 4, 128, 128), BF16), ((1024, 128), F32),
        ((128, 128), F32), ((128, 1024), F32),
    )
    vmem = pltpu.VMEM
    def reduction():
        return (
            vmem((2, 2, 2, 32, 2048), F32), vmem((2, 2, 4, 32, 2048), F32),
            vmem((2, 2, 16, 2048), F32), vmem((2, 2, 32, 2048), F32),
        )

    scratch = [
        vmem((4, 4, 64, 2048), BF16),
        vmem((4, 4, 64, 2048), BF16),
        vmem((4, 128, 2048), BF16),
        vmem((4, 4, 64, 768), BF16),
        vmem((2, 4, 128, 512), BF16),
        vmem((2, 1024, 768), BF16),
        vmem((2, 2, 4, 128, 128), BF16),
        vmem((4, 2, 4, 64, 128), BF16),
        vmem((4, 4, 64, 2048), F32),
        vmem((4, 4, 64, 2048), F32),
        reduction(),
        reduction(),
        vmem((2, 4, 1024, 128), F32),
        vmem((2, 2, 4, 128, 128), F32),
        vmem((2, 512, 128), F32),
        vmem((2, 3, 1024, 128), F32),
        vmem((2, 1, 128, 128), F32),
        vmem((2, 3, 2, 128, 128), F32),
        vmem((128, 128), F32),
        vmem((4, 64, 1024), F32),
        vmem((4, 128, 512), BF16),
        vmem((64, 2048), BF16),
        pltpu.SemaphoreType.DMA((COPIES,)),
        pltpu.SemaphoreType.DMA((COPIES,)),
        pltpu.SemaphoreType.DMA((16,)),
        pltpu.SemaphoreType.DMA((32,)),
    ]
    ig, ag, qwg, kwg, owg = pl.pallas_call(
        kernel,
        out_shape=[jax.ShapeDtypeStruct(*shape) for shape in shapes],
        in_specs=[pl.BlockSpec(memory_space=pl.ANY)] * 8,
        out_specs=[pl.BlockSpec(memory_space=pl.ANY)] * 5,
        scratch_shapes=scratch,
        compiler_params=pltpu.CompilerParams(
            collective_id=0, has_side_effects=True, vmem_limit_bytes=63 * 2**20
        ),
        cost_estimate=pl.CostEstimate(flops=14 * 10**9, bytes_accessed=5 * 10**6, transcendentals=0),
    )(
        layer_input.reshape(2, 64, 1024),
        attn_out.reshape(4, 4, 128, 128),
        out_grad,
        q_grad.reshape(4, 8, 64, 128),
        k_grad.reshape(4, 8, 64, 128),
        q_weight,
        k_weight[0],
        o_weight,
    )
    parts = (ig.reshape(128, 1024), ag.reshape(2048, 128), qwg, kwg, owg)
    ig, ag, qwg, kwg, owg = pl.pallas_call(
        finish,
        out_shape=[jax.ShapeDtypeStruct(part.shape, part.dtype) for part in parts],
        in_specs=[pl.BlockSpec(memory_space=pltpu.VMEM)] * 5,
        out_specs=[pl.BlockSpec(memory_space=pltpu.VMEM)] * 5,
    )(*parts)
    return ig, ag, qwg, kwg[None], owg


def solution(mesh):
    return jax.shard_map(
        shards,
        mesh=mesh,
        in_specs=(
            P("seq", ("row", "col")),
            P(("row", "col"), "seq"),
            P("seq", ("row", "col")),
            P(("row", "col"), "seq"),
            P(("row", "col"), "seq"),
            P(("row", "col"), "seq"),
            P("seq", ("row", "col"), None),
            P("seq", ("row", "col")),
        ),
        out_specs=(
            P("seq", ("row", "col")),
            P(("row", "col"), "seq"),
            P(("row", "col"), "seq"),
            P("seq", ("row", "col"), None),
            P("seq", ("row", "col")),
        ),
        check_vma=False,
    )
```

```python
import jax
import jax.numpy as jnp
from jax import lax
from jax.experimental import pallas as pl
from jax.experimental.pallas import tpu as pltpu
from jax.sharding import PartitionSpec as P

MESH = pl.DeviceIdType.MESH
COPIES = 176
F32 = jnp.float32
BF16 = jnp.bfloat16


def rem(value, size):
    return lax.rem(value + size, size)


def at128(index):
    return pl.ds(pl.multiple_of(index * 128, 128), 128)


def at1024(index):
    return pl.ds(pl.multiple_of(index * 1024, 1024), 1024)


def kernel(
    li, ao, og, q, k, qw, kw, ow,
    ig_out, ag_out, qwg_out, kwg_out, owg_out,
    lit, owt, ogt, qkt, aot, w3, km, kbuf,
    ig, owg, ig_got, ow_far, ow_full, owy,
    qwg, kwg, qw_far, qw_full, kw_far, kw_full, kwy,
    ag, agr, agb, fin,
    ssem, rsem, lsem,
):
    seq = lax.axis_index("seq")
    x, y, zh = lax.div(seq, 16), lax.rem(lax.div(seq, 4), 4), lax.rem(seq, 4)
    zlo, col = lax.axis_index("row"), lax.axis_index("col")
    z = zh * 2 + zlo
    yhi, ylo = lax.div(y, 2), lax.rem(y, 2)
    quarter = zlo * 2 + col

    def device(dx, dy, dz):
        zz = rem(z + dz, 8)
        return (
            rem(x + dx, 4) * 16 + rem(y + dy, 4) * 4 + lax.div(zz, 2), lax.rem(zz, 2), col
        )

    zs = [device(0, 0, d) for d in range(1, 8)]
    sibling = (seq, zlo, 1 - col)
    zpartner = device(0, 0, 1 - 2 * zlo)
    ypartner = device(0, 1 - 2 * ylo, 0)
    x_ring = (4, x, device(-1, 0, 0), device(1, 0, 0))
    y_ring = (4, y, device(0, -1, 0), device(0, 1, 0))
    z_ring = (8, z, device(0, 0, -1), device(0, 0, 1))

    zh_ring = (4, zh, device(0, 0, -2), device(0, 0, 2))

    places = [
        (rem(y + d, 4), lo, device(0, d, dz)) for d in range(4)
        for lo, dz in ((zlo, 0), (1 - zlo, 1 - 2 * zlo))
    ]

    barrier = pltpu.get_barrier_semaphore()
    peers = list(x_ring[2:]) + [place[2] for place in places[1:]] + zs + [sibling]
    for peer in peers:
        pl.semaphore_signal(barrier, inc=1, device_id=peer, device_id_type=MESH)
    pl.semaphore_wait(barrier, len(peers))

    sent, local, last, stored = [], [], [], []

    def send(src, dst, to):
        n = len(sent)
        copy = pltpu.make_async_remote_copy(
            src_ref=src, dst_ref=dst, send_sem=ssem.at[n], recv_sem=rsem.at[n],
            device_id=to, device_id_type=MESH,
        )
        copy.start()
        sent.append(copy)
        return copy

    def place(src, dst):
        copy = pltpu.make_async_copy(src, dst, lsem.at[len(local)])
        copy.start()
        local.append(copy)
        return copy

    def arrive(copies):
        for copy in copies:
            copy.wait_recv()

    def add(dst, *parts):
        if len(dst.shape) == 3:
            def row(i, _):
                total = dst[i]
                for part in parts:
                    total = total + part[i]
                dst[i] = total
                return 0
            lax.fori_loop(0, dst.shape[0], row, 0)
        else:
            total = dst[...]
            for part in parts:
                total = total + part[...]
            dst[...] = total

    def ring_gather(ring, piece):
        n, me, left, right = ring
        own = piece(me, None)
        steps = [[send(own, own, left), send(own, own, right)]]

        def step(s):
            arrive(steps[-1])
            half = s == n // 2
            a = piece(rem(me + s - 1, n), 0 if half else None)
            b = piece(rem(me - s + 1, n), 1 if half else None)
            steps.append([send(a, a, left), send(b, b, right)])

        return step, lambda: arrive(steps[-1])

    def ring_reduce(ring, piece, far, full):
        n, me, left, right = ring
        size = far(0).shape[0]
        halves = [pl.ds(0, size), pl.ds(size, size)]
        last = n // 2
        across = piece(rem(me + last, n))
        steps = [[
            send(across.at[halves[0]], far(0), left), send(across.at[halves[1]], far(1), right)
        ]]

        def step(s):
            arrive(steps[-1])
            a, b = piece(rem(me - (last + 1 - s), n)), piece(rem(me + (last + 1 - s), n))
            if s == 2:
                add(a.at[halves[0]], far(0))
                add(b.at[halves[1]], far(1))
            else:
                add(a, full(0, s - 3))
                add(b, full(1, s - 3))
            steps.append([send(a, full(0, s - 2), left), send(b, full(1, s - 2), right)])

        def total():
            arrive(steps[-1])
            add(piece(me), full(0, last - 2), full(1, last - 2))
            return piece(me)

        return step, total

    def part_of(size, half):
        return pl.ds(0, size) if half is None else pl.ds(half * (size // 2), size // 2)

    def rows_of(start, half):
        return pl.ds(start, 32) if half is None else pl.ds(start + half * 16, 16)

    class Gather:
        def __init__(self, tile):
            self.tile = tile
            self.a = ring_gather(x_ring, lambda i, h: tile.at[i, y, rows_of(0, h)])
            self.b = ring_gather(y_ring, lambda j, h: tile.at[x, j, rows_of(32, h)])

        def inner(self):
            self.a[0](2)
            self.b[0](2)

        def outer(self):
            tile = self.tile
            self.a[1]()
            self.a = ring_gather(y_ring, lambda j, h: tile.at[part_of(4, h), j, pl.ds(0, 32)])
            self.b[1]()
            self.b = ring_gather(x_ring, lambda i, h: tile.at[i, part_of(4, h), pl.ds(32, 32)])

        def done(self):
            self.a[1]()
            self.b[1]()

    class Reduce:
        def __init__(self, tile, got):
            self.tile, self.got = tile, got
            far, full = got[0], got[1]
            self.a = ring_reduce(
                y_ring, lambda j: tile.at[:, j, pl.ds(0, 32)],
                lambda d: far.at[0, d], lambda d, s: full.at[0, d],
            )
            self.b = ring_reduce(
                x_ring, lambda i: tile.at[i, :, pl.ds(32, 32)],
                lambda d: far.at[1, d], lambda d, s: full.at[1, d],
            )

        def second(self):
            self.a[0](2)
            self.b[0](2)

        def inner(self):
            tile = self.tile
            far, full = self.got[2], self.got[3]
            self.a[1]()
            self.a = ring_reduce(
                x_ring, lambda i: tile.at[i, y, pl.ds(0, 32)],
                lambda d: far.at[0, d], lambda d, s: full.at[0, d],
            )
            self.b[1]()
            self.b = ring_reduce(
                y_ring, lambda j: tile.at[x, j, pl.ds(32, 32)],
                lambda d: far.at[1, d], lambda d, s: full.at[1, d],
            )

        def total(self):
            self.a[1]()
            self.b[1]()

    def spread(src, slot):
        copies = [
            send(src.at[:, rem(z + d, 8)], slot, zs[d - 1]) for d in range(1, 8)
        ]
        return place(src.at[:, z], slot), copies

    def qw_slot(zz, half):
        return w3.at[lax.rem(zz, 2), part_of(1024, half), at128(lax.div(zz, 2))]

    def km_slot(zz, half):
        return km.at[lax.rem(zz, 2), part_of(2, half), lax.div(zz, 2)]

    og_slot = ogt.at[x, zh, :, at1024(zlo)]
    og_own = place(og.at[zlo], og_slot)
    og_sent = send(og.at[1 - zlo], og_slot, zpartner)
    km_own = place(kw, km.at[zlo, ylo, zh])
    km_sent = send(kw, km.at[zlo, ylo, zh], ypartner)
    qw_own = place(qw, qw_slot(z, None))
    li_slot = lit.at[x, y, :, at1024(zlo)]
    li_own = place(li.at[zlo], li_slot)
    li_sent = send(li.at[1 - zlo], li_slot, zpartner)
    og_own.wait()
    og_sent.wait_recv()
    og_step, og_done = ring_gather(zh_ring, lambda i, h: ogt.at[x, i, part_of(64, h)])
    li_own.wait()
    li_sent.wait_recv()
    li_all = Gather(lit)
    li_all.inner()
    li_all.outer()
    og_step(2)
    og_done()
    og_step, og_done = ring_gather(x_ring, lambda i, h: ogt.at[i, part_of(4, h)])
    ao_slot = aot.at[quarter, :, :, at128(y)]
    ao_own = place(ao.at[y, :, zlo], ao_slot)
    ao_copies = [send(ao.at[j, :, lo], ao_slot, to) for j, lo, to in places[1:]]
    km_own.wait()
    km_sent.wait_recv()
    km_step, km_done = ring_gather(z_ring, km_slot)
    ow_slot = owt.at[y, :, at1024(zlo)]
    ow_own = place(ow, ow_slot)
    ow_sent = send(ow, ow_slot, zpartner)
    ao_own.wait()
    arrive(ao_copies)
    ao_shared = [send(v, v, sibling) for v in [aot.at[lo * 2 + col] for lo in range(2)]]
    k_own, k_copies = spread(k, kbuf.at[zh, zlo])
    ow_own.wait()
    ow_sent.wait_recv()
    ow_step, ow_done = ring_gather(y_ring, lambda j, h: owt.at[j, part_of(128, h)])
    og_step(2)
    qw_own.wait()
    qw_step, qw_done = ring_gather(z_ring, qw_slot)
    ow_step(2)
    q_own, q_copies = spread(q, qkt.at[quarter, :, :, at128(zh)])
    km_step(2)
    li_all.inner()
    og_done()
    arrive(ao_shared)
    for lo in range(2):
        for i in range(1):
            part = lax.dot_general(
                aot[...].reshape(1024, 512),
                ogt[:, :, :, pl.ds(lo * 1024 + 0 + i * 512, 512)].reshape(1024, 512),
                (((0,), (0,)), ((), ())), preferred_element_type=F32,
            )
            owg[0, :, lo, :, pl.ds(i * 512, 512)] = part.reshape(4, 128, 512)
    owg_a_step, owg_a_total = ring_reduce(
        y_ring, lambda j: owg.at[0, j], lambda d: ow_far.at[0, d],
        lambda d, s: ow_full.at[0, d, s],
    )
    qw_step(2)
    for lo in range(2):
        for i in range(1):
            part = lax.dot_general(
                aot[...].reshape(1024, 512),
                ogt[:, :, :, pl.ds(lo * 1024 + 512 + i * 512, 512)].reshape(1024, 512),
                (((0,), (0,)), ((), ())), preferred_element_type=F32,
            )
            owg[1, :, lo, :, pl.ds(i * 512, 512)] = part.reshape(4, 128, 512)
    owg_b_step, owg_b_total = ring_reduce(
        y_ring, lambda j: owg.at[1, j], lambda d: ow_far.at[1, d],
        lambda d, s: ow_full.at[1, d, s],
    )
    ow_done()

    def block(i, _):
        ag[i] = lax.dot_general(
            ogt[i].reshape(256, 2048), owt[...].reshape(512, 2048),
            (((1,), (1,)), ((), ())), preferred_element_type=F32,
        ).reshape(4, 64, 512)
        return 0

    lax.fori_loop(0, 4, block, 0)
    ag_sent = [send(ag.at[lo * 2 + 1 - col], agr.at[lo], sibling) for lo in range(2)]
    k_own.wait()
    arrive(k_copies)
    for lo in range(2):
        total = kbuf[0, lo].astype(F32)
        for h in range(1, 4):
            total = total + kbuf[h, lo].astype(F32)
        high = total.astype(BF16)
        qkt[lo * 2 + col, :, :, pl.ds(512, 128)] = high
        qkt[lo * 2 + col, :, :, pl.ds(640, 128)] = (total - high.astype(F32)).astype(BF16)
    km_step(3)
    owg_a_step(2)
    arrive(ag_sent)
    for lo in range(2):
        agb[lo] = (ag[lo * 2 + col] + agr[lo]).astype(BF16)
    ag_slot = ag_out.at[y, :, zlo]
    stored.append(place(agb.at[zlo, :, :, at128(y)], ag_slot))
    last += [send(agb.at[lo, :, :, at128(j)], ag_slot, to) for j, lo, to in places[1:]]
    q_own.wait()
    arrive(q_copies)
    q_shared = [send(v, v, sibling) for v in [qkt.at[lo * 2 + col] for lo in range(2)]]
    owg_b_step(2)
    qw_step(3)
    km_step(4)
    li_all.done()
    arrive(q_shared)

    for lo in range(2):
        def block(i, _, lo=lo):
            cols = pl.ds(pl.multiple_of(lo * 1024 + i * 256, 256), 256)
            rows = pl.ds(pl.multiple_of(i * 256, 256), 256)
            part = lax.dot_general(
                lit[:, :, :, cols].reshape(1024, 256), qkt[...].reshape(1024, 768),
                (((0,), (0,)), ((), ())), preferred_element_type=F32,
            )
            for h in range(4):
                qwg[lo, h, rows, :] = part[:, h * 128 : h * 128 + 128]
            sums = part[:, 512:640] + part[:, 640:768]
            kwg[lo, lax.div(i, 2), pl.ds(lax.rem(i, 2) * 2, 2)] = sums.reshape(2, 128, 128)
            return 0
        lax.fori_loop(0, 4, block, 0)
    qwg_a_step, qwg_a_total = ring_reduce(
        z_ring,
        lambda zz: qwg.at[lax.rem(zz, 2), lax.div(zz, 2), pl.ds(0, 512)],
        lambda d: qw_far.at[0, d], lambda d, s: qw_full.at[0, d, s],
    )
    qwg_b_step, qwg_b_total = ring_reduce(
        z_ring,
        lambda zz: qwg.at[lax.rem(zz, 2), lax.div(zz, 2), pl.ds(512, 512)],
        lambda d: qw_far.at[1, d], lambda d, s: qw_full.at[1, d, s],
    )
    kwg_step, kwg_total = ring_reduce(
        z_ring, lambda zz: kwg.at[lax.rem(zz, 2), :, lax.div(zz, 2)],
        lambda d: kw_far.at[d], lambda d, s: kw_full.at[d, s],
    )

    qw_step(4)
    qwg_a_step(2)
    qw_done()
    km_done()
    for lo in range(2):
        keys = km[lo].reshape(1024, 128)
        w3[lo, :, pl.ds(512, 128)] = keys
        w3[lo, :, pl.ds(640, 128)] = keys
    for lo in range(2):
        def block(i, _, lo=lo):
            rows = pl.ds(pl.multiple_of(0 + i * 256, 256), 256)
            part = lax.dot_general(
                qkt[...].reshape(1024, 768), w3[lo, rows, :],
                (((1,), (1,)), ((), ())), preferred_element_type=F32,
            )
            cols = pl.ds(pl.multiple_of(lo * 512 + i * 256, 256), 256)
            ig[0, :, :, :, cols] = part.reshape(4, 4, 64, 256)
            return 0
        lax.fori_loop(0, 2, block, 0)
    ig_sum_a = Reduce(ig.at[0], ig_got[0])
    qwg_b_step(2)
    kwg_step(2)
    for lo in range(2):
        def block(i, _, lo=lo):
            rows = pl.ds(pl.multiple_of(512 + i * 256, 256), 256)
            part = lax.dot_general(
                qkt[...].reshape(1024, 768), w3[lo, rows, :],
                (((1,), (1,)), ((), ())), preferred_element_type=F32,
            )
            cols = pl.ds(pl.multiple_of(lo * 512 + i * 256, 256), 256)
            ig[1, :, :, :, cols] = part.reshape(4, 4, 64, 256)
            return 0
        lax.fori_loop(0, 2, block, 0)
    ig_sum_b = Reduce(ig.at[1], ig_got[1])
    owg_a_mine = owg_a_total()
    owg_a_sent = send(owg_a_mine.at[1 - zlo], owy.at[0], zpartner)
    qwg_a_step(3)
    kwg_step(3)
    ig_sum_a.second()
    owg_b_mine = owg_b_total()
    owg_b_sent = send(owg_b_mine.at[1 - zlo], owy.at[1], zpartner)
    qwg_b_step(3)
    ig_sum_b.second()
    ig_sum_a.inner()
    owg_a_sent.wait_recv()
    add(owg_a_mine.at[zlo], owy.at[0])
    stored.append(place(owg_a_mine.at[zlo], owg_out.at[:, pl.ds(0, 512)]))
    kwg_step(4)
    qwg_a_step(4)
    kwg_mine = kwg_total()
    kwg_sent = send(kwg_mine.at[1 - ylo], kwy, ypartner)
    ig_sum_b.inner()
    qwg_b_step(4)
    kwg_sent.wait_recv()
    kwy[...] = kwy[...] + kwg_mine[ylo]
    stored.append(place(kwy, kwg_out))
    ig_sum_a.second()
    owg_b_sent.wait_recv()
    add(owg_b_mine.at[zlo], owy.at[1])
    stored.append(place(owg_b_mine.at[zlo], owg_out.at[:, pl.ds(512, 512)]))
    ig_sum_b.second()
    ig_sum_a.total()
    fin[0] = ig[0, x, y].astype(BF16)
    cols = pl.ds(0, 512)
    mine, other = [
        fin.at[0, :, pl.ds(pl.multiple_of(lo * 512, 512), 512)] for lo in (zlo, 1 - zlo)
    ]
    stored.append(place(mine, ig_out.at[zlo, :, cols]))
    last.append(send(other, ig_out.at[zlo, :, cols], zpartner))
    stored.append(place(qwg_a_total(), qwg_out.at[pl.ds(0, 512)]))
    stored.append(place(qwg_b_total(), qwg_out.at[pl.ds(512, 512)]))
    ig_sum_b.total()
    fin[1] = ig[1, x, y].astype(BF16)
    cols = pl.ds(512, 512)
    mine, other = [
        fin.at[1, :, pl.ds(pl.multiple_of(lo * 512, 512), 512)] for lo in (zlo, 1 - zlo)
    ]
    stored.append(place(mine, ig_out.at[zlo, :, cols]))
    last.append(send(other, ig_out.at[zlo, :, cols], zpartner))
    arrive(last)
    for copy in stored:
        copy.wait()
    for copy in sent:
        copy.wait_send()


def finish(*refs):
    for source, target in zip(refs[:5], refs[5:]):
        target[...] = source[...]


def shards(layer_input, attn_out, out_grad, q_grad, k_grad, q_weight, k_weight, o_weight):
    shapes = (
        ((2, 64, 1024), BF16), ((4, 4, 2, 64, 128), BF16), ((1024, 128), F32),
        ((128, 128), F32), ((128, 1024), F32),
    )
    vmem = pltpu.VMEM
    def reduction():
        return (
            vmem((2, 2, 2, 32, 1024), F32), vmem((2, 2, 4, 32, 1024), F32),
            vmem((2, 2, 16, 1024), F32), vmem((2, 2, 32, 1024), F32),
        )

    scratch = [
        vmem((4, 4, 64, 2048), BF16),
        vmem((4, 128, 2048), BF16),
        vmem((4, 4, 64, 2048), BF16),
        vmem((4, 4, 64, 768), BF16),
        vmem((4, 4, 64, 512), BF16),
        vmem((2, 1024, 768), BF16),
        vmem((2, 2, 4, 128, 128), BF16),
        vmem((4, 2, 4, 64, 128), BF16),
        vmem((2, 4, 4, 64, 1024), F32),
        vmem((2, 4, 2, 128, 512), F32),
        tuple(reduction() for _ in range(2)),
        vmem((2, 2, 1, 128, 512), F32),
        vmem((2, 2, 1, 2, 128, 512), F32),
        vmem((2, 128, 512), F32),
        vmem((2, 4, 1024, 128), F32),
        vmem((2, 2, 4, 128, 128), F32),
        vmem((2, 2, 256, 128), F32),
        vmem((2, 2, 3, 512, 128), F32),
        vmem((2, 1, 128, 128), F32),
        vmem((2, 3, 2, 128, 128), F32),
        vmem((128, 128), F32),
        vmem((4, 4, 64, 512), F32),
        vmem((2, 4, 64, 512), F32),
        vmem((2, 4, 64, 512), BF16),
        vmem((2, 64, 1024), BF16),
        pltpu.SemaphoreType.DMA((COPIES,)),
        pltpu.SemaphoreType.DMA((COPIES,)),
        pltpu.SemaphoreType.DMA((24,)),
    ]
    ig, ag, qwg, kwg, owg = pl.pallas_call(
        kernel,
        out_shape=[jax.ShapeDtypeStruct(*shape) for shape in shapes],
        in_specs=[pl.BlockSpec(memory_space=pl.ANY)] * 8,
        out_specs=[pl.BlockSpec(memory_space=pl.ANY)] * 5,
        scratch_shapes=scratch,
        compiler_params=pltpu.CompilerParams(
            collective_id=0, has_side_effects=True, vmem_limit_bytes=63 * 2**20
        ),
        cost_estimate=pl.CostEstimate(flops=14 * 10**9, bytes_accessed=5 * 10**6, transcendentals=0),
    )(
        layer_input.reshape(2, 64, 1024),
        attn_out.reshape(4, 4, 2, 64, 128),
        out_grad.reshape(2, 64, 1024),
        q_grad.reshape(4, 8, 64, 128),
        k_grad.reshape(4, 8, 64, 128),
        q_weight,
        k_weight[0],
        o_weight,
    )
    parts = (ig.reshape(128, 1024), ag.reshape(2048, 128), qwg, kwg, owg)
    ig, ag, qwg, kwg, owg = pl.pallas_call(
        finish,
        out_shape=[jax.ShapeDtypeStruct(part.shape, part.dtype) for part in parts],
        in_specs=[pl.BlockSpec(memory_space=pltpu.VMEM)] * 5,
        out_specs=[pl.BlockSpec(memory_space=pltpu.VMEM)] * 5,
    )(*parts)
    return ig, ag, qwg, kwg[None], owg


def solution(mesh):
    return jax.shard_map(
        shards,
        mesh=mesh,
        in_specs=(
            P("seq", ("row", "col")),
            P(("row", "col"), "seq"),
            P("seq", ("row", "col")),
            P(("row", "col"), "seq"),
            P(("row", "col"), "seq"),
            P(("row", "col"), "seq"),
            P("seq", ("row", "col"), None),
            P("seq", ("row", "col")),
        ),
        out_specs=(
            P("seq", ("row", "col")),
            P(("row", "col"), "seq"),
            P(("row", "col"), "seq"),
            P("seq", ("row", "col"), None),
            P("seq", ("row", "col")),
        ),
        check_vma=False,
    )
```

```python
import jax
import jax.numpy as jnp
from jax import lax
from jax.experimental import pallas as pl
from jax.experimental.pallas import tpu as pltpu
from jax.sharding import PartitionSpec as P

MESH = pl.DeviceIdType.MESH
COPIES = 176
F32 = jnp.float32
BF16 = jnp.bfloat16


def rem(value, size):
    return lax.rem(value + size, size)


def at128(index):
    return pl.ds(pl.multiple_of(index * 128, 128), 128)


def at1024(index):
    return pl.ds(pl.multiple_of(index * 1024, 1024), 1024)


def kernel(
    li, ao, og, q, k, qw, kw, ow,
    ig_out, ag_out, qwg_out, kwg_out, owg_out,
    lit, owt, ogt, qkt, aot, w3, km, kbuf,
    ig, owg, ig_got, ow_far, ow_full, owy,
    qwg, kwg, qw_far, qw_full, kw_far, kw_full, kwy,
    ag, agr, agb, fin,
    ssem, rsem, lsem,
):
    seq = lax.axis_index("seq")
    x, y, zh = lax.div(seq, 16), lax.rem(lax.div(seq, 4), 4), lax.rem(seq, 4)
    zlo, col = lax.axis_index("row"), lax.axis_index("col")
    z = zh * 2 + zlo
    yhi, ylo = lax.div(y, 2), lax.rem(y, 2)
    quarter = zlo * 2 + col

    def device(dx, dy, dz):
        zz = rem(z + dz, 8)
        return (
            rem(x + dx, 4) * 16 + rem(y + dy, 4) * 4 + lax.div(zz, 2), lax.rem(zz, 2), col
        )

    zs = [device(0, 0, d) for d in range(1, 8)]
    sibling = (seq, zlo, 1 - col)
    zpartner = device(0, 0, 1 - 2 * zlo)
    ypartner = device(0, 1 - 2 * ylo, 0)
    x_ring = (4, x, device(-1, 0, 0), device(1, 0, 0))
    y_ring = (4, y, device(0, -1, 0), device(0, 1, 0))
    z_ring = (8, z, device(0, 0, -1), device(0, 0, 1))
    odd = zlo == 1
    across = device(0, 0, 2 * zlo - 1)

    zh_ring = (4, zh, device(0, 0, -2), device(0, 0, 2))

    places = [
        (rem(y + d, 4), lo, device(0, d, dz)) for d in range(4)
        for lo, dz in ((zlo, 0), (1 - zlo, 1 - 2 * zlo))
    ]

    barrier = pltpu.get_barrier_semaphore()
    peers = list(x_ring[2:]) + [place[2] for place in places[1:]] + zs + [sibling]
    for peer in peers:
        pl.semaphore_signal(barrier, inc=1, device_id=peer, device_id_type=MESH)
    pl.semaphore_wait(barrier, len(peers))

    sent, local, last, stored = [], [], [], []

    def send(src, dst, to):
        n = len(sent)
        copy = pltpu.make_async_remote_copy(
            src_ref=src, dst_ref=dst, send_sem=ssem.at[n], recv_sem=rsem.at[n],
            device_id=to, device_id_type=MESH,
        )
        copy.start()
        sent.append(copy)
        return copy

    def place(src, dst):
        copy = pltpu.make_async_copy(src, dst, lsem.at[len(local)])
        copy.start()
        local.append(copy)
        return copy

    def arrive(copies):
        for copy in copies:
            copy.wait_recv()

    def add(dst, *parts):
        if len(dst.shape) == 3:
            def row(i, _):
                total = dst[i]
                for part in parts:
                    total = total + part[i]
                dst[i] = total
                return 0
            lax.fori_loop(0, dst.shape[0], row, 0)
        else:
            total = dst[...]
            for part in parts:
                total = total + part[...]
            dst[...] = total

    def ring_gather(ring, piece):
        n, me, left, right = ring
        own = piece(me, None)
        steps = [[send(own, own, left), send(own, own, right)]]

        def step(s):
            arrive(steps[-1])
            half = s == n // 2
            if half and n == 8:
                far = piece(lax.select(odd, rem(me - 3, n), rem(me + 3, n)), None)
                steps.append([send(far, far, across)])
                return
            a = piece(rem(me + s - 1, n), 0 if half else None)
            b = piece(rem(me - s + 1, n), 1 if half else None)
            steps.append([send(a, a, left), send(b, b, right)])

        return step, lambda: arrive(steps[-1])

    def ring_reduce(ring, piece, far, full):
        n, me, left, right = ring
        size = far(0).shape[0]
        halves = [pl.ds(0, size), pl.ds(size, size)]
        last = n // 2
        opposite = piece(rem(me + last, n))
        if n == 8:
            steps = [[send(opposite, far(0), across)]]
        else:
            steps = [[
                send(opposite.at[halves[0]], far(0), left),
                send(opposite.at[halves[1]], far(1), right),
            ]]

        def step(s):
            arrive(steps[-1])
            a, b = piece(rem(me - (last + 1 - s), n)), piece(rem(me + (last + 1 - s), n))
            if s == 2 and n == 8:
                add(piece(lax.select(odd, rem(me - 3, n), rem(me + 3, n))), far(0))
            elif s == 2:
                add(a.at[halves[0]], far(0))
                add(b.at[halves[1]], far(1))
            else:
                add(a, full(0, s - 3))
                add(b, full(1, s - 3))
            steps.append([send(a, full(0, s - 2), left), send(b, full(1, s - 2), right)])

        def total():
            arrive(steps[-1])
            add(piece(me), full(0, last - 2), full(1, last - 2))
            return piece(me)

        return step, total

    def part_of(size, half):
        return pl.ds(0, size) if half is None else pl.ds(half * (size // 2), size // 2)

    def rows_of(start, half):
        return pl.ds(start, 32) if half is None else pl.ds(start + half * 16, 16)

    class Gather:
        def __init__(self, tile):
            self.tile = tile
            self.a = ring_gather(x_ring, lambda i, h: tile.at[i, y, rows_of(0, h)])
            self.b = ring_gather(y_ring, lambda j, h: tile.at[x, j, rows_of(32, h)])

        def inner(self):
            self.a[0](2)
            self.b[0](2)

        def outer(self):
            tile = self.tile
            self.a[1]()
            self.a = ring_gather(y_ring, lambda j, h: tile.at[part_of(4, h), j, pl.ds(0, 32)])
            self.b[1]()
            self.b = ring_gather(x_ring, lambda i, h: tile.at[i, part_of(4, h), pl.ds(32, 32)])

        def done(self):
            self.a[1]()
            self.b[1]()

    class Reduce:
        def __init__(self, tile, got):
            self.tile, self.got = tile, got
            far, full = got[0], got[1]
            self.a = ring_reduce(
                y_ring, lambda j: tile.at[:, j, pl.ds(0, 32)],
                lambda d: far.at[0, d], lambda d, s: full.at[0, d],
            )
            self.b = ring_reduce(
                x_ring, lambda i: tile.at[i, :, pl.ds(32, 32)],
                lambda d: far.at[1, d], lambda d, s: full.at[1, d],
            )

        def second(self):
            self.a[0](2)
            self.b[0](2)

        def inner(self):
            tile = self.tile
            far, full = self.got[2], self.got[3]
            self.a[1]()
            self.a = ring_reduce(
                x_ring, lambda i: tile.at[i, y, pl.ds(0, 32)],
                lambda d: far.at[0, d], lambda d, s: full.at[0, d],
            )
            self.b[1]()
            self.b = ring_reduce(
                y_ring, lambda j: tile.at[x, j, pl.ds(32, 32)],
                lambda d: far.at[1, d], lambda d, s: full.at[1, d],
            )

        def total(self):
            self.a[1]()
            self.b[1]()

    def spread(src, slot):
        copies = [
            send(src.at[:, rem(z + d, 8)], slot, zs[d - 1]) for d in range(1, 8)
        ]
        return place(src.at[:, z], slot), copies

    def qw_slot(zz, half):
        return w3.at[lax.rem(zz, 2), part_of(1024, half), at128(lax.div(zz, 2))]

    def km_slot(zz, half):
        return km.at[lax.rem(zz, 2), part_of(2, half), lax.div(zz, 2)]

    og_slot = ogt.at[x, zh, :, at1024(zlo)]
    og_own = place(og.at[zlo], og_slot)
    og_sent = send(og.at[1 - zlo], og_slot, zpartner)
    qw_own = place(qw, qw_slot(z, None))
    km_own = place(kw, km.at[zlo, ylo, zh])
    km_sent = send(kw, km.at[zlo, ylo, zh], ypartner)
    li_slot = lit.at[x, y, :, at1024(zlo)]
    li_own = place(li.at[zlo], li_slot)
    li_sent = send(li.at[1 - zlo], li_slot, zpartner)
    og_own.wait()
    og_sent.wait_recv()
    og_step, og_done = ring_gather(zh_ring, lambda i, h: ogt.at[x, i, part_of(64, h)])
    li_own.wait()
    li_sent.wait_recv()
    li_all = Gather(lit)
    li_all.inner()
    li_all.outer()
    km_own.wait()
    km_sent.wait_recv()
    km_step, km_done = ring_gather(z_ring, km_slot)
    og_step(2)
    og_done()
    og_step, og_done = ring_gather(x_ring, lambda i, h: ogt.at[i, part_of(4, h)])
    ow_slot = owt.at[y, :, at1024(zlo)]
    ow_own = place(ow, ow_slot)
    ow_sent = send(ow, ow_slot, zpartner)
    qw_own.wait()
    qw_step, qw_done = ring_gather(z_ring, qw_slot)
    ao_slot = aot.at[quarter, :, :, at128(y)]
    ao_own = place(ao.at[y, :, zlo], ao_slot)
    ao_copies = [send(ao.at[j, :, lo], ao_slot, to) for j, lo, to in places[1:]]
    ow_own.wait()
    ow_sent.wait_recv()
    ow_step, ow_done = ring_gather(y_ring, lambda j, h: owt.at[j, part_of(128, h)])
    k_own, k_copies = spread(k, kbuf.at[zh, zlo])
    qw_step(2)
    og_step(2)
    km_step(2)
    q_own, q_copies = spread(q, qkt.at[quarter, :, :, at128(zh)])
    ao_own.wait()
    arrive(ao_copies)
    ao_shared = [send(v, v, sibling) for v in [aot.at[lo * 2 + col] for lo in range(2)]]
    ow_step(2)
    li_all.inner()
    og_done()
    arrive(ao_shared)
    for lo in range(2):
        for i in range(1):
            part = lax.dot_general(
                aot[...].reshape(1024, 512),
                ogt[:, :, :, pl.ds(lo * 1024 + 0 + i * 512, 512)].reshape(1024, 512),
                (((0,), (0,)), ((), ())), preferred_element_type=F32,
            )
            owg[0, :, lo, :, pl.ds(i * 512, 512)] = part.reshape(4, 128, 512)
    owg_a_step, owg_a_total = ring_reduce(
        y_ring, lambda j: owg.at[0, j], lambda d: ow_far.at[0, d],
        lambda d, s: ow_full.at[0, d, s],
    )
    for lo in range(2):
        for i in range(1):
            part = lax.dot_general(
                aot[...].reshape(1024, 512),
                ogt[:, :, :, pl.ds(lo * 1024 + 512 + i * 512, 512)].reshape(1024, 512),
                (((0,), (0,)), ((), ())), preferred_element_type=F32,
            )
            owg[1, :, lo, :, pl.ds(i * 512, 512)] = part.reshape(4, 128, 512)
    owg_b_step, owg_b_total = ring_reduce(
        y_ring, lambda j: owg.at[1, j], lambda d: ow_far.at[1, d],
        lambda d, s: ow_full.at[1, d, s],
    )
    qw_step(3)
    ow_done()

    def block(i, _):
        ag[i] = lax.dot_general(
            ogt[i].reshape(256, 2048), owt[...].reshape(512, 2048),
            (((1,), (1,)), ((), ())), preferred_element_type=F32,
        ).reshape(4, 64, 512)
        return 0

    lax.fori_loop(0, 4, block, 0)
    ag_sent = [send(ag.at[lo * 2 + 1 - col], agr.at[lo], sibling) for lo in range(2)]
    k_own.wait()
    arrive(k_copies)
    for lo in range(2):
        total = kbuf[0, lo].astype(F32)
        for h in range(1, 4):
            total = total + kbuf[h, lo].astype(F32)
        high = total.astype(BF16)
        qkt[lo * 2 + col, :, :, pl.ds(512, 128)] = high
        qkt[lo * 2 + col, :, :, pl.ds(640, 128)] = (total - high.astype(F32)).astype(BF16)
    km_step(3)
    owg_a_step(2)
    q_own.wait()
    arrive(q_copies)
    q_shared = [send(v, v, sibling) for v in [qkt.at[lo * 2 + col] for lo in range(2)]]
    qw_step(4)
    arrive(ag_sent)
    for lo in range(2):
        agb[lo] = (ag[lo * 2 + col] + agr[lo]).astype(BF16)
    ag_slot = ag_out.at[y, :, zlo]
    stored.append(place(agb.at[zlo, :, :, at128(y)], ag_slot))
    last += [send(agb.at[lo, :, :, at128(j)], ag_slot, to) for j, lo, to in places[1:]]
    km_step(4)
    li_all.done()
    arrive(q_shared)

    for lo in range(2):
        def block(i, _, lo=lo):
            cols = pl.ds(pl.multiple_of(lo * 1024 + i * 256, 256), 256)
            rows = pl.ds(pl.multiple_of(i * 256, 256), 256)
            part = lax.dot_general(
                lit[:, :, :, cols].reshape(1024, 256), qkt[...].reshape(1024, 768),
                (((0,), (0,)), ((), ())), preferred_element_type=F32,
            )
            for h in range(4):
                qwg[lo, h, rows, :] = part[:, h * 128 : h * 128 + 128]
            sums = part[:, 512:640] + part[:, 640:768]
            kwg[lo, lax.div(i, 2), pl.ds(lax.rem(i, 2) * 2, 2)] = sums.reshape(2, 128, 128)
            return 0
        lax.fori_loop(0, 4, block, 0)
    qwg_step, qwg_total = ring_reduce(
        z_ring,
        lambda zz: qwg.at[lax.rem(zz, 2), lax.div(zz, 2), pl.ds(0, 1024)],
        lambda d: qw_far.at[0, d], lambda d, s: qw_full.at[0, d, s],
    )
    kwg_step, kwg_total = ring_reduce(
        z_ring, lambda zz: kwg.at[lax.rem(zz, 2), :, lax.div(zz, 2)],
        lambda d: kw_far.at[d], lambda d, s: kw_full.at[d, s],
    )

    qw_done()
    km_done()
    for lo in range(2):
        keys = km[lo].reshape(1024, 128)
        w3[lo, :, pl.ds(512, 128)] = keys
        w3[lo, :, pl.ds(640, 128)] = keys
    for lo in range(2):
        def block(i, _, lo=lo):
            rows = pl.ds(pl.multiple_of(0 + i * 256, 256), 256)
            part = lax.dot_general(
                qkt[...].reshape(1024, 768), w3[lo, rows, :],
                (((1,), (1,)), ((), ())), preferred_element_type=F32,
            )
            cols = pl.ds(pl.multiple_of(lo * 512 + i * 256, 256), 256)
            ig[0, :, :, :, cols] = part.reshape(4, 4, 64, 256)
            return 0
        lax.fori_loop(0, 2, block, 0)
    ig_sum_a = Reduce(ig.at[0], ig_got[0])
    owg_a_mine = owg_a_total()
    owg_a_sent = send(owg_a_mine.at[1 - zlo], owy.at[0], zpartner)
    owg_b_step(2)
    for lo in range(2):
        def block(i, _, lo=lo):
            rows = pl.ds(pl.multiple_of(512 + i * 256, 256), 256)
            part = lax.dot_general(
                qkt[...].reshape(1024, 768), w3[lo, rows, :],
                (((1,), (1,)), ((), ())), preferred_element_type=F32,
            )
            cols = pl.ds(pl.multiple_of(lo * 512 + i * 256, 256), 256)
            ig[1, :, :, :, cols] = part.reshape(4, 4, 64, 256)
            return 0
        lax.fori_loop(0, 2, block, 0)
    ig_sum_b = Reduce(ig.at[1], ig_got[1])
    kwg_step(2)
    ig_sum_a.second()
    qwg_step(2)
    kwg_step(3)
    qwg_step(3)
    ig_sum_b.second()
    kwg_step(4)
    owg_a_sent.wait_recv()
    add(owg_a_mine.at[zlo], owy.at[0])
    stored.append(place(owg_a_mine.at[zlo], owg_out.at[:, pl.ds(0, 512)]))
    owg_b_mine = owg_b_total()
    owg_b_sent = send(owg_b_mine.at[1 - zlo], owy.at[1], zpartner)
    qwg_step(4)
    ig_sum_a.inner()
    kwg_mine = kwg_total()
    kwg_sent = send(kwg_mine.at[1 - ylo], kwy, ypartner)
    ig_sum_b.inner()
    ig_sum_a.second()
    ig_sum_b.second()
    kwg_sent.wait_recv()
    kwy[...] = kwy[...] + kwg_mine[ylo]
    stored.append(place(kwy, kwg_out))
    ig_sum_a.total()
    fin[0] = ig[0, x, y].astype(BF16)
    cols = pl.ds(0, 512)
    mine, other = [
        fin.at[0, :, pl.ds(pl.multiple_of(lo * 512, 512), 512)] for lo in (zlo, 1 - zlo)
    ]
    stored.append(place(mine, ig_out.at[zlo, :, cols]))
    last.append(send(other, ig_out.at[zlo, :, cols], zpartner))
    owg_b_sent.wait_recv()
    add(owg_b_mine.at[zlo], owy.at[1])
    stored.append(place(owg_b_mine.at[zlo], owg_out.at[:, pl.ds(512, 512)]))
    ig_sum_b.total()
    fin[1] = ig[1, x, y].astype(BF16)
    cols = pl.ds(512, 512)
    mine, other = [
        fin.at[1, :, pl.ds(pl.multiple_of(lo * 512, 512), 512)] for lo in (zlo, 1 - zlo)
    ]
    stored.append(place(mine, ig_out.at[zlo, :, cols]))
    last.append(send(other, ig_out.at[zlo, :, cols], zpartner))
    stored.append(place(qwg_total(), qwg_out.at[pl.ds(0, 1024)]))
    arrive(last)
    for copy in stored:
        copy.wait()
    for copy in sent:
        copy.wait_send()


def finish(*refs):
    for source, target in zip(refs[:5], refs[5:]):
        target[...] = source[...]


def shards(layer_input, attn_out, out_grad, q_grad, k_grad, q_weight, k_weight, o_weight):
    shapes = (
        ((2, 64, 1024), BF16), ((4, 4, 2, 64, 128), BF16), ((1024, 128), F32),
        ((128, 128), F32), ((128, 1024), F32),
    )
    vmem = pltpu.VMEM
    def reduction():
        return (
            vmem((2, 2, 2, 32, 1024), F32), vmem((2, 2, 4, 32, 1024), F32),
            vmem((2, 2, 16, 1024), F32), vmem((2, 2, 32, 1024), F32),
        )

    scratch = [
        vmem((4, 4, 64, 2048), BF16),
        vmem((4, 128, 2048), BF16),
        vmem((4, 4, 64, 2048), BF16),
        vmem((4, 4, 64, 768), BF16),
        vmem((4, 4, 64, 512), BF16),
        vmem((2, 1024, 768), BF16),
        vmem((2, 2, 4, 128, 128), BF16),
        vmem((4, 2, 4, 64, 128), BF16),
        vmem((2, 4, 4, 64, 1024), F32),
        vmem((2, 4, 2, 128, 512), F32),
        tuple(reduction() for _ in range(2)),
        vmem((2, 2, 1, 128, 512), F32),
        vmem((2, 2, 1, 2, 128, 512), F32),
        vmem((2, 128, 512), F32),
        vmem((2, 4, 1024, 128), F32),
        vmem((2, 2, 4, 128, 128), F32),
        vmem((1, 1, 1024, 128), F32),
        vmem((1, 2, 3, 1024, 128), F32),
        vmem((1, 2, 128, 128), F32),
        vmem((2, 3, 2, 128, 128), F32),
        vmem((128, 128), F32),
        vmem((4, 4, 64, 512), F32),
        vmem((2, 4, 64, 512), F32),
        vmem((2, 4, 64, 512), BF16),
        vmem((2, 64, 1024), BF16),
        pltpu.SemaphoreType.DMA((COPIES,)),
        pltpu.SemaphoreType.DMA((COPIES,)),
        pltpu.SemaphoreType.DMA((24,)),
    ]
    ig, ag, qwg, kwg, owg = pl.pallas_call(
        kernel,
        out_shape=[jax.ShapeDtypeStruct(*shape) for shape in shapes],
        in_specs=[pl.BlockSpec(memory_space=pl.ANY)] * 8,
        out_specs=[pl.BlockSpec(memory_space=pl.ANY)] * 5,
        scratch_shapes=scratch,
        compiler_params=pltpu.CompilerParams(
            collective_id=0, has_side_effects=True, vmem_limit_bytes=63 * 2**20
        ),
        cost_estimate=pl.CostEstimate(flops=14 * 10**9, bytes_accessed=5 * 10**6, transcendentals=0),
    )(
        layer_input.reshape(2, 64, 1024),
        attn_out.reshape(4, 4, 2, 64, 128),
        out_grad.reshape(2, 64, 1024),
        q_grad.reshape(4, 8, 64, 128),
        k_grad.reshape(4, 8, 64, 128),
        q_weight,
        k_weight[0],
        o_weight,
    )
    parts = (ig.reshape(128, 1024), ag.reshape(2048, 128), qwg, kwg, owg)
    ig, ag, qwg, kwg, owg = pl.pallas_call(
        finish,
        out_shape=[jax.ShapeDtypeStruct(part.shape, part.dtype) for part in parts],
        in_specs=[pl.BlockSpec(memory_space=pltpu.VMEM)] * 5,
        out_specs=[pl.BlockSpec(memory_space=pltpu.VMEM)] * 5,
    )(*parts)
    return ig, ag, qwg, kwg[None], owg


def solution(mesh):
    return jax.shard_map(
        shards,
        mesh=mesh,
        in_specs=(
            P("seq", ("row", "col")),
            P(("row", "col"), "seq"),
            P("seq", ("row", "col")),
            P(("row", "col"), "seq"),
            P(("row", "col"), "seq"),
            P(("row", "col"), "seq"),
            P("seq", ("row", "col"), None),
            P("seq", ("row", "col")),
        ),
        out_specs=(
            P("seq", ("row", "col")),
            P(("row", "col"), "seq"),
            P(("row", "col"), "seq"),
            P("seq", ("row", "col"), None),
            P("seq", ("row", "col")),
        ),
        check_vma=False,
    )
```

```python
import jax
import jax.numpy as jnp
from jax import lax
from jax.experimental import pallas as pl
from jax.experimental.pallas import tpu as pltpu
from jax.sharding import PartitionSpec as P

MESH = pl.DeviceIdType.MESH
COPIES = 176
F32 = jnp.float32
BF16 = jnp.bfloat16


def rem(value, size):
    return lax.rem(value + size, size)


def at128(index):
    return pl.ds(pl.multiple_of(index * 128, 128), 128)


def at1024(index):
    return pl.ds(pl.multiple_of(index * 1024, 1024), 1024)


def kernel(
    li, ao, og, q, k, qw, kw, ow,
    ig_out, ag_out, qwg_out, kwg_out, owg_out,
    lit, owt, ogt, qkt, aot, w3, km, kbuf,
    ig, owg, ig_got, ow_far, ow_full, owy,
    qwg, kwg, qw_far, qw_full, kw_far, kw_full, kwy,
    ag, agr, agb, fin,
    ssem, rsem, lsem,
):
    seq = lax.axis_index("seq")
    x, y, zh = lax.div(seq, 16), lax.rem(lax.div(seq, 4), 4), lax.rem(seq, 4)
    zlo, col = lax.axis_index("row"), lax.axis_index("col")
    z = zh * 2 + zlo
    yhi, ylo = lax.div(y, 2), lax.rem(y, 2)
    quarter = zlo * 2 + col

    def device(dx, dy, dz):
        zz = rem(z + dz, 8)
        return (
            rem(x + dx, 4) * 16 + rem(y + dy, 4) * 4 + lax.div(zz, 2), lax.rem(zz, 2), col
        )

    zs = [device(0, 0, d) for d in range(1, 8)]
    sibling = (seq, zlo, 1 - col)
    zpartner = device(0, 0, 1 - 2 * zlo)
    ypartner = device(0, 1 - 2 * ylo, 0)
    x_ring = (4, x, device(-1, 0, 0), device(1, 0, 0))
    y_ring = (4, y, device(0, -1, 0), device(0, 1, 0))
    z_ring = (8, z, device(0, 0, -1), device(0, 0, 1))
    odd = zlo == 1
    across = device(0, 0, 2 * zlo - 1)

    zh_ring = (4, zh, device(0, 0, -2), device(0, 0, 2))

    places = [
        (rem(y + d, 4), lo, device(0, d, dz)) for d in range(4)
        for lo, dz in ((zlo, 0), (1 - zlo, 1 - 2 * zlo))
    ]

    barrier = pltpu.get_barrier_semaphore()
    peers = list(x_ring[2:]) + [place[2] for place in places[1:]] + zs + [sibling]
    for peer in peers:
        pl.semaphore_signal(barrier, inc=1, device_id=peer, device_id_type=MESH)
    pl.semaphore_wait(barrier, len(peers))

    sent, local, last, stored = [], [], [], []

    def send(src, dst, to):
        n = len(sent)
        copy = pltpu.make_async_remote_copy(
            src_ref=src, dst_ref=dst, send_sem=ssem.at[n], recv_sem=rsem.at[n],
            device_id=to, device_id_type=MESH,
        )
        copy.start()
        sent.append(copy)
        return copy

    def place(src, dst):
        copy = pltpu.make_async_copy(src, dst, lsem.at[len(local)])
        copy.start()
        local.append(copy)
        return copy

    def arrive(copies):
        for copy in copies:
            copy.wait_recv()

    def add(dst, *parts):
        if len(dst.shape) == 3:
            def row(i, _):
                total = dst[i]
                for part in parts:
                    total = total + part[i]
                dst[i] = total
                return 0
            lax.fori_loop(0, dst.shape[0], row, 0)
        else:
            total = dst[...]
            for part in parts:
                total = total + part[...]
            dst[...] = total

    def ring_gather(ring, piece):
        n, me, left, right = ring
        own = piece(me, None)
        steps = [[send(own, own, left), send(own, own, right)]]

        def step(s):
            arrive(steps[-1])
            half = s == n // 2
            if half and n == 8:
                far = piece(lax.select(odd, rem(me - 3, n), rem(me + 3, n)), None)
                steps.append([send(far, far, across)])
                return
            a = piece(rem(me + s - 1, n), 0 if half else None)
            b = piece(rem(me - s + 1, n), 1 if half else None)
            steps.append([send(a, a, left), send(b, b, right)])

        return step, lambda: arrive(steps[-1])

    def ring_reduce(ring, piece, far, full):
        n, me, left, right = ring
        size = far(0).shape[0]
        halves = [pl.ds(0, size), pl.ds(size, size)]
        last = n // 2
        opposite = piece(rem(me + last, n))
        if n == 8:
            steps = [[send(opposite, far(0), across)]]
        else:
            steps = [[
                send(opposite.at[halves[0]], far(0), left),
                send(opposite.at[halves[1]], far(1), right),
            ]]

        def step(s):
            arrive(steps[-1])
            a, b = piece(rem(me - (last + 1 - s), n)), piece(rem(me + (last + 1 - s), n))
            if s == 2 and n == 8:
                add(piece(lax.select(odd, rem(me - 3, n), rem(me + 3, n))), far(0))
            elif s == 2:
                add(a.at[halves[0]], far(0))
                add(b.at[halves[1]], far(1))
            else:
                add(a, full(0, s - 3))
                add(b, full(1, s - 3))
            steps.append([send(a, full(0, s - 2), left), send(b, full(1, s - 2), right)])

        def total():
            arrive(steps[-1])
            add(piece(me), full(0, last - 2), full(1, last - 2))
            return piece(me)

        return step, total

    def part_of(size, half):
        return pl.ds(0, size) if half is None else pl.ds(half * (size // 2), size // 2)

    def rows_of(start, half):
        return pl.ds(start, 32) if half is None else pl.ds(start + half * 16, 16)

    class Gather:
        def __init__(self, tile):
            self.tile = tile
            self.a = ring_gather(x_ring, lambda i, h: tile.at[i, y, rows_of(0, h)])
            self.b = ring_gather(y_ring, lambda j, h: tile.at[x, j, rows_of(32, h)])

        def inner(self):
            self.a[0](2)
            self.b[0](2)

        def outer(self):
            tile = self.tile
            self.a[1]()
            self.a = ring_gather(y_ring, lambda j, h: tile.at[part_of(4, h), j, pl.ds(0, 32)])
            self.b[1]()
            self.b = ring_gather(x_ring, lambda i, h: tile.at[i, part_of(4, h), pl.ds(32, 32)])

        def done(self):
            self.a[1]()
            self.b[1]()

    class Reduce:
        def __init__(self, tile, got):
            self.tile, self.got = tile, got
            far, full = got[0], got[1]
            self.a = ring_reduce(
                y_ring, lambda j: tile.at[:, j, pl.ds(0, 32)],
                lambda d: far.at[0, d], lambda d, s: full.at[0, d],
            )
            self.b = ring_reduce(
                x_ring, lambda i: tile.at[i, :, pl.ds(32, 32)],
                lambda d: far.at[1, d], lambda d, s: full.at[1, d],
            )

        def second(self):
            self.a[0](2)
            self.b[0](2)

        def inner(self):
            tile = self.tile
            far, full = self.got[2], self.got[3]
            self.a[1]()
            self.a = ring_reduce(
                x_ring, lambda i: tile.at[i, y, pl.ds(0, 32)],
                lambda d: far.at[0, d], lambda d, s: full.at[0, d],
            )
            self.b[1]()
            self.b = ring_reduce(
                y_ring, lambda j: tile.at[x, j, pl.ds(32, 32)],
                lambda d: far.at[1, d], lambda d, s: full.at[1, d],
            )

        def total(self):
            self.a[1]()
            self.b[1]()

    def spread(src, slot):
        copies = [
            send(src.at[:, rem(z + d, 8)], slot, zs[d - 1]) for d in range(1, 8)
        ]
        return place(src.at[:, z], slot), copies

    def half_of(lo):
        return pl.ds(pl.multiple_of(lo * 512, 512), 512)

    def qw_slot(c):
        def slot(zz, half):
            rows = pl.ds(c * 512, 512) if half is None else pl.ds(c * 512 + half * 256, 256)
            return w3.at[lax.rem(zz, 2), rows, at128(lax.div(zz, 2))]
        return slot

    def km_slot(zz, half):
        return km.at[lax.rem(zz, 2), part_of(2, half), lax.div(zz, 2)]

    li_slot = lit.at[x, y, :, at1024(zlo)]
    li_own = place(li.at[zlo], li_slot)
    li_sent = send(li.at[1 - zlo], li_slot, zpartner)
    og_a_slot = ogt.at[0, x, zh, :, half_of(zlo)]
    og_a_own = place(og.at[zlo, :, pl.ds(0, 512)], og_a_slot)
    og_a_sent = send(og.at[1 - zlo, :, pl.ds(0, 512)], og_a_slot, zpartner)
    qw_b_own = place(qw.at[pl.ds(512, 512)], qw_slot(1)(z, None))
    km_own = place(kw, km.at[zlo, ylo, zh])
    km_sent = send(kw, km.at[zlo, ylo, zh], ypartner)
    km_own.wait()
    km_sent.wait_recv()
    km_step, km_done = ring_gather(z_ring, km_slot)
    og_b_slot = ogt.at[1, x, zh, :, half_of(zlo)]
    og_b_own = place(og.at[zlo, :, pl.ds(512, 512)], og_b_slot)
    og_b_sent = send(og.at[1 - zlo, :, pl.ds(512, 512)], og_b_slot, zpartner)
    li_own.wait()
    li_sent.wait_recv()
    li_all = Gather(lit)
    qw_a_own = place(qw.at[pl.ds(0, 512)], qw_slot(0)(z, None))
    og_a_own.wait()
    og_a_sent.wait_recv()
    og_a_step, og_a_done = ring_gather(
        zh_ring, lambda i, h: ogt.at[0, x, i, part_of(64, h)]
    )
    li_all.inner()
    ao_slot = aot.at[quarter, :, :, at128(y)]
    ao_own = place(ao.at[y, :, zlo], ao_slot)
    ao_copies = [send(ao.at[j, :, lo], ao_slot, to) for j, lo, to in places[1:]]
    li_all.outer()
    og_a_step(2)
    ow_slot = owt.at[y, :, at1024(zlo)]
    ow_own = place(ow, ow_slot)
    ow_sent = send(ow, ow_slot, zpartner)
    og_a_done()
    og_a_step, og_a_done = ring_gather(x_ring, lambda i, h: ogt.at[0, i, part_of(4, h)])
    og_b_own.wait()
    og_b_sent.wait_recv()
    og_b_step, og_b_done = ring_gather(
        zh_ring, lambda i, h: ogt.at[1, x, i, part_of(64, h)]
    )
    qw_a_own.wait()
    qw_a_step, qw_a_done = ring_gather(z_ring, qw_slot(0))
    ow_own.wait()
    ow_sent.wait_recv()
    ow_step, ow_done = ring_gather(y_ring, lambda j, h: owt.at[j, part_of(128, h)])
    og_b_step(2)
    km_step(2)
    q_own, q_copies = spread(q, qkt.at[quarter, :, :, at128(zh)])
    ao_own.wait()
    arrive(ao_copies)
    ao_shared = [send(v, v, sibling) for v in [aot.at[lo * 2 + col] for lo in range(2)]]
    og_a_step(2)
    ow_step(2)
    og_b_done()
    og_b_step, og_b_done = ring_gather(x_ring, lambda i, h: ogt.at[1, i, part_of(4, h)])
    qw_b_own.wait()
    qw_b_step, qw_b_done = ring_gather(z_ring, qw_slot(1))
    og_a_done()
    arrive(ao_shared)
    for lo in range(2):
        for i in range(1):
            part = lax.dot_general(
                aot[...].reshape(1024, 512),
                ogt[0, :, :, :, pl.ds(lo * 512 + i * 512, 512)].reshape(1024, 512),
                (((0,), (0,)), ((), ())), preferred_element_type=F32,
            )
            owg[0, :, lo, :, pl.ds(i * 512, 512)] = part.reshape(4, 128, 512)
    owg_a_step, owg_a_total = ring_reduce(
        y_ring, lambda j: owg.at[0, j], lambda d: ow_far.at[0, d],
        lambda d, s: ow_full.at[0, d, s],
    )
    qw_a_step(2)
    km_step(3)
    k_own, k_copies = spread(k, kbuf.at[zh, zlo])
    qw_b_step(2)
    owg_a_step(2)
    og_b_step(2)
    og_b_done()
    for lo in range(2):
        for i in range(1):
            part = lax.dot_general(
                aot[...].reshape(1024, 512),
                ogt[1, :, :, :, pl.ds(lo * 512 + i * 512, 512)].reshape(1024, 512),
                (((0,), (0,)), ((), ())), preferred_element_type=F32,
            )
            owg[1, :, lo, :, pl.ds(i * 512, 512)] = part.reshape(4, 128, 512)
    owg_b_step, owg_b_total = ring_reduce(
        y_ring, lambda j: owg.at[1, j], lambda d: ow_far.at[1, d],
        lambda d, s: ow_full.at[1, d, s],
    )
    ow_done()

    def block(i, _):
        total = jnp.zeros((256, 512), F32)
        for c in range(2):
            for lo in range(2):
                total = total + lax.dot_general(
                    ogt[c, i, :, :, pl.ds(lo * 512, 512)].reshape(256, 512),
                    owt[:, :, pl.ds(lo * 1024 + c * 512, 512)].reshape(512, 512),
                    (((1,), (1,)), ((), ())), preferred_element_type=F32,
                )
        ag[i] = total.reshape(4, 64, 512)
        return 0

    lax.fori_loop(0, 4, block, 0)
    ag_sent = [send(ag.at[lo * 2 + 1 - col], agr.at[lo], sibling) for lo in range(2)]
    li_all.inner()
    qw_a_step(3)
    qw_b_step(3)
    k_own.wait()
    arrive(k_copies)
    for lo in range(2):
        total = kbuf[0, lo].astype(F32)
        for h in range(1, 4):
            total = total + kbuf[h, lo].astype(F32)
        high = total.astype(BF16)
        qkt[lo * 2 + col, :, :, pl.ds(512, 128)] = high
        qkt[lo * 2 + col, :, :, pl.ds(640, 128)] = (total - high.astype(F32)).astype(BF16)
    q_own.wait()
    arrive(q_copies)
    q_shared = [send(v, v, sibling) for v in [qkt.at[lo * 2 + col] for lo in range(2)]]
    owg_b_step(2)
    owg_a_mine = owg_a_total()
    owg_a_sent = send(owg_a_mine.at[1 - zlo], owy.at[0], zpartner)
    km_step(4)
    qw_a_step(4)
    qw_b_step(4)
    li_all.done()
    arrive(q_shared)

    for lo in range(2):
        def block(i, _, lo=lo):
            cols = pl.ds(pl.multiple_of(lo * 1024 + i * 256, 256), 256)
            rows = pl.ds(pl.multiple_of(i * 256, 256), 256)
            part = lax.dot_general(
                lit[:, :, :, cols].reshape(1024, 256), qkt[...].reshape(1024, 768),
                (((0,), (0,)), ((), ())), preferred_element_type=F32,
            )
            for h in range(4):
                qwg[lo, h, rows, :] = part[:, h * 128 : h * 128 + 128]
            sums = part[:, 512:640] + part[:, 640:768]
            kwg[lo, lax.div(i, 2), pl.ds(lax.rem(i, 2) * 2, 2)] = sums.reshape(2, 128, 128)
            return 0
        lax.fori_loop(0, 4, block, 0)
    qwg_a_step, qwg_a_total = ring_reduce(
        z_ring,
        lambda zz: qwg.at[lax.rem(zz, 2), lax.div(zz, 2), pl.ds(0, 512)],
        lambda d: qw_far.at[0, d], lambda d, s: qw_full.at[0, d, s],
    )
    qwg_b_step, qwg_b_total = ring_reduce(
        z_ring,
        lambda zz: qwg.at[lax.rem(zz, 2), lax.div(zz, 2), pl.ds(512, 512)],
        lambda d: qw_far.at[1, d], lambda d, s: qw_full.at[1, d, s],
    )
    kwg_step, kwg_total = ring_reduce(
        z_ring, lambda zz: kwg.at[lax.rem(zz, 2), :, lax.div(zz, 2)],
        lambda d: kw_far.at[d], lambda d, s: kw_full.at[d, s],
    )

    arrive(ag_sent)
    for lo in range(2):
        agb[lo] = (ag[lo * 2 + col] + agr[lo]).astype(BF16)
    ag_slot = ag_out.at[y, :, zlo]
    stored.append(place(agb.at[zlo, :, :, at128(y)], ag_slot))
    last += [send(agb.at[lo, :, :, at128(j)], ag_slot, to) for j, lo, to in places[1:]]
    qw_a_done()
    km_done()
    for lo in range(2):
        keys = km[lo].reshape(1024, 128)
        w3[lo, :, pl.ds(512, 128)] = keys
        w3[lo, :, pl.ds(640, 128)] = keys
    for lo in range(2):
        def block(i, _, lo=lo):
            rows = pl.ds(pl.multiple_of(0 + i * 256, 256), 256)
            part = lax.dot_general(
                qkt[...].reshape(1024, 768), w3[lo, rows, :],
                (((1,), (1,)), ((), ())), preferred_element_type=F32,
            )
            cols = pl.ds(pl.multiple_of(lo * 512 + i * 256, 256), 256)
            ig[0, :, :, :, cols] = part.reshape(4, 4, 64, 256)
            return 0
        lax.fori_loop(0, 2, block, 0)
    ig_sum_a = Reduce(ig.at[0], ig_got[0])
    owg_b_mine = owg_b_total()
    owg_b_sent = send(owg_b_mine.at[1 - zlo], owy.at[1], zpartner)
    qw_b_done()
    for lo in range(2):
        def block(i, _, lo=lo):
            rows = pl.ds(pl.multiple_of(512 + i * 256, 256), 256)
            part = lax.dot_general(
                qkt[...].reshape(1024, 768), w3[lo, rows, :],
                (((1,), (1,)), ((), ())), preferred_element_type=F32,
            )
            cols = pl.ds(pl.multiple_of(lo * 512 + i * 256, 256), 256)
            ig[1, :, :, :, cols] = part.reshape(4, 4, 64, 256)
            return 0
        lax.fori_loop(0, 2, block, 0)
    ig_sum_b = Reduce(ig.at[1], ig_got[1])
    qwg_b_step(2)
    kwg_step(2)
    owg_b_sent.wait_recv()
    add(owg_b_mine.at[zlo], owy.at[1])
    stored.append(place(owg_b_mine.at[zlo], owg_out.at[:, pl.ds(512, 512)]))
    ig_sum_a.second()
    qwg_a_step(2)
    kwg_step(3)
    ig_sum_b.second()
    qwg_b_step(3)
    kwg_step(4)
    qwg_a_step(3)
    qwg_b_step(4)
    ig_sum_a.inner()
    owg_a_sent.wait_recv()
    add(owg_a_mine.at[zlo], owy.at[0])
    stored.append(place(owg_a_mine.at[zlo], owg_out.at[:, pl.ds(0, 512)]))
    kwg_mine = kwg_total()
    kwg_sent = send(kwg_mine.at[1 - ylo], kwy, ypartner)
    ig_sum_b.inner()
    ig_sum_a.second()
    qwg_a_step(4)
    ig_sum_b.second()
    kwg_sent.wait_recv()
    kwy[...] = kwy[...] + kwg_mine[ylo]
    stored.append(place(kwy, kwg_out))
    ig_sum_a.total()
    fin[0] = ig[0, x, y].astype(BF16)
    cols = pl.ds(0, 512)
    mine, other = [
        fin.at[0, :, pl.ds(pl.multiple_of(lo * 512, 512), 512)] for lo in (zlo, 1 - zlo)
    ]
    stored.append(place(mine, ig_out.at[zlo, :, cols]))
    last.append(send(other, ig_out.at[zlo, :, cols], zpartner))
    ig_sum_b.total()
    fin[1] = ig[1, x, y].astype(BF16)
    cols = pl.ds(512, 512)
    mine, other = [
        fin.at[1, :, pl.ds(pl.multiple_of(lo * 512, 512), 512)] for lo in (zlo, 1 - zlo)
    ]
    stored.append(place(mine, ig_out.at[zlo, :, cols]))
    last.append(send(other, ig_out.at[zlo, :, cols], zpartner))
    stored.append(place(qwg_a_total(), qwg_out.at[pl.ds(0, 512)]))
    stored.append(place(qwg_b_total(), qwg_out.at[pl.ds(512, 512)]))
    arrive(last)
    for copy in stored:
        copy.wait()
    for copy in sent:
        copy.wait_send()


def finish(*refs):
    for source, target in zip(refs[:5], refs[5:]):
        target[...] = source[...]


def shards(layer_input, attn_out, out_grad, q_grad, k_grad, q_weight, k_weight, o_weight):
    shapes = (
        ((2, 64, 1024), BF16), ((4, 4, 2, 64, 128), BF16), ((1024, 128), F32),
        ((128, 128), F32), ((128, 1024), F32),
    )
    vmem = pltpu.VMEM
    def reduction():
        return (
            vmem((2, 2, 2, 32, 1024), F32), vmem((2, 2, 4, 32, 1024), F32),
            vmem((2, 2, 16, 1024), F32), vmem((2, 2, 32, 1024), F32),
        )

    scratch = [
        vmem((4, 4, 64, 2048), BF16),
        vmem((4, 128, 2048), BF16),
        vmem((2, 4, 4, 64, 1024), BF16),
        vmem((4, 4, 64, 768), BF16),
        vmem((4, 4, 64, 512), BF16),
        vmem((2, 1024, 768), BF16),
        vmem((2, 2, 4, 128, 128), BF16),
        vmem((4, 2, 4, 64, 128), BF16),
        vmem((2, 4, 4, 64, 1024), F32),
        vmem((2, 4, 2, 128, 512), F32),
        tuple(reduction() for _ in range(2)),
        vmem((2, 2, 1, 128, 512), F32),
        vmem((2, 2, 1, 2, 128, 512), F32),
        vmem((2, 128, 512), F32),
        vmem((2, 4, 1024, 128), F32),
        vmem((2, 2, 4, 128, 128), F32),
        vmem((2, 1, 512, 128), F32),
        vmem((2, 2, 3, 512, 128), F32),
        vmem((1, 2, 128, 128), F32),
        vmem((2, 3, 2, 128, 128), F32),
        vmem((128, 128), F32),
        vmem((4, 4, 64, 512), F32),
        vmem((2, 4, 64, 512), F32),
        vmem((2, 4, 64, 512), BF16),
        vmem((2, 64, 1024), BF16),
        pltpu.SemaphoreType.DMA((COPIES,)),
        pltpu.SemaphoreType.DMA((COPIES,)),
        pltpu.SemaphoreType.DMA((24,)),
    ]
    ig, ag, qwg, kwg, owg = pl.pallas_call(
        kernel,
        out_shape=[jax.ShapeDtypeStruct(*shape) for shape in shapes],
        in_specs=[pl.BlockSpec(memory_space=pl.ANY)] * 8,
        out_specs=[pl.BlockSpec(memory_space=pl.ANY)] * 5,
        scratch_shapes=scratch,
        compiler_params=pltpu.CompilerParams(
            collective_id=0, has_side_effects=True, vmem_limit_bytes=63 * 2**20
        ),
        cost_estimate=pl.CostEstimate(flops=14 * 10**9, bytes_accessed=5 * 10**6, transcendentals=0),
    )(
        layer_input.reshape(2, 64, 1024),
        attn_out.reshape(4, 4, 2, 64, 128),
        out_grad.reshape(2, 64, 1024),
        q_grad.reshape(4, 8, 64, 128),
        k_grad.reshape(4, 8, 64, 128),
        q_weight,
        k_weight[0],
        o_weight,
    )
    parts = (ig.reshape(128, 1024), ag.reshape(2048, 128), qwg, kwg, owg)
    ig, ag, qwg, kwg, owg = pl.pallas_call(
        finish,
        out_shape=[jax.ShapeDtypeStruct(part.shape, part.dtype) for part in parts],
        in_specs=[pl.BlockSpec(memory_space=pltpu.VMEM)] * 5,
        out_specs=[pl.BlockSpec(memory_space=pltpu.VMEM)] * 5,
    )(*parts)
    return ig, ag, qwg, kwg[None], owg


def solution(mesh):
    return jax.shard_map(
        shards,
        mesh=mesh,
        in_specs=(
            P("seq", ("row", "col")),
            P(("row", "col"), "seq"),
            P("seq", ("row", "col")),
            P(("row", "col"), "seq"),
            P(("row", "col"), "seq"),
            P(("row", "col"), "seq"),
            P("seq", ("row", "col"), None),
            P("seq", ("row", "col")),
        ),
        out_specs=(
            P("seq", ("row", "col")),
            P(("row", "col"), "seq"),
            P(("row", "col"), "seq"),
            P("seq", ("row", "col"), None),
            P("seq", ("row", "col")),
        ),
        check_vma=False,
    )
```

```python
import jax
import jax.numpy as jnp
from jax import lax
from jax.experimental import pallas as pl
from jax.experimental.pallas import tpu as pltpu
from jax.sharding import PartitionSpec as P

MESH = pl.DeviceIdType.MESH
COPIES = 176
F32 = jnp.float32
BF16 = jnp.bfloat16


def rem(value, size):
    return lax.rem(value + size, size)


def at128(index):
    return pl.ds(pl.multiple_of(index * 128, 128), 128)


def at1024(index):
    return pl.ds(pl.multiple_of(index * 1024, 1024), 1024)


def kernel(
    li, ao, og, q, k, qw, kw, ow,
    ig_out, ag_out, qwg_out, kwg_out, owg_out,
    lit, owt, ogt, qkt, aot, w3, km, kbuf,
    ig, owg, ig_got, ow_far, ow_full, owy,
    qwg, kwg, qw_far, qw_full, kw_far, kw_full, kwy,
    ag, agr, agb, fin,
    ssem, rsem, lsem,
):
    seq = lax.axis_index("seq")
    x, y, zh = lax.div(seq, 16), lax.rem(lax.div(seq, 4), 4), lax.rem(seq, 4)
    zlo, col = lax.axis_index("row"), lax.axis_index("col")
    z = zh * 2 + zlo
    yhi, ylo = lax.div(y, 2), lax.rem(y, 2)
    quarter = zlo * 2 + col

    def device(dx, dy, dz):
        zz = rem(z + dz, 8)
        return (
            rem(x + dx, 4) * 16 + rem(y + dy, 4) * 4 + lax.div(zz, 2), lax.rem(zz, 2), col
        )

    zs = [device(0, 0, d) for d in range(1, 8)]
    sibling = (seq, zlo, 1 - col)
    zpartner = device(0, 0, 1 - 2 * zlo)
    ypartner = device(0, 1 - 2 * ylo, 0)
    x_ring = (4, x, device(-1, 0, 0), device(1, 0, 0))
    y_ring = (4, y, device(0, -1, 0), device(0, 1, 0))
    z_ring = (8, z, device(0, 0, -1), device(0, 0, 1))
    odd = zlo == 1
    across = device(0, 0, 2 * zlo - 1)

    zh_ring = (4, zh, device(0, 0, -2), device(0, 0, 2))

    places = [
        (rem(y + d, 4), lo, device(0, d, dz)) for d in range(4)
        for lo, dz in ((zlo, 0), (1 - zlo, 1 - 2 * zlo))
    ]

    barrier = pltpu.get_barrier_semaphore()
    peers = list(x_ring[2:]) + [place[2] for place in places[1:]] + zs + [sibling]
    for peer in peers:
        pl.semaphore_signal(barrier, inc=1, device_id=peer, device_id_type=MESH)
    pl.semaphore_wait(barrier, len(peers))

    sent, local, last, stored = [], [], [], []

    def send(src, dst, to):
        n = len(sent)
        copy = pltpu.make_async_remote_copy(
            src_ref=src, dst_ref=dst, send_sem=ssem.at[n], recv_sem=rsem.at[n],
            device_id=to, device_id_type=MESH,
        )
        copy.start()
        sent.append(copy)
        return copy

    def place(src, dst):
        copy = pltpu.make_async_copy(src, dst, lsem.at[len(local)])
        copy.start()
        local.append(copy)
        return copy

    def arrive(copies):
        for copy in copies:
            copy.wait_recv()

    def add(dst, *parts):
        if len(dst.shape) == 3:
            def row(i, _):
                total = dst[i]
                for part in parts:
                    total = total + part[i]
                dst[i] = total
                return 0
            lax.fori_loop(0, dst.shape[0], row, 0)
        else:
            total = dst[...]
            for part in parts:
                total = total + part[...]
            dst[...] = total

    def ring_gather(ring, piece):
        n, me, left, right = ring
        own = piece(me, None)
        steps = [[send(own, own, left), send(own, own, right)]]

        def step(s):
            half = s == n // 2
            if half and n == 8:
                arrive(steps[-1])
                far = piece(lax.select(odd, rem(me - 3, n), rem(me + 3, n)), None)
                steps.append([send(far, far, across)])
                return
            a = piece(rem(me + s - 1, n), 0 if half else None)
            b = piece(rem(me - s + 1, n), 1 if half else None)
            steps[-1][0].wait_recv()
            first = send(a, a, left)
            steps[-1][1].wait_recv()
            steps.append([first, send(b, b, right)])

        return step, lambda: arrive(steps[-1])

    def ring_reduce(ring, piece, far, full):
        n, me, left, right = ring
        size = far(0).shape[0]
        halves = [pl.ds(0, size), pl.ds(size, size)]
        last = n // 2
        opposite = piece(rem(me + last, n))
        if n == 8:
            steps = [[send(opposite, far(0), across)]]
        else:
            steps = [[
                send(opposite.at[halves[0]], far(0), left),
                send(opposite.at[halves[1]], far(1), right),
            ]]

        def step(s):
            steps[-1][0].wait_recv()
            a, b = piece(rem(me - (last + 1 - s), n)), piece(rem(me + (last + 1 - s), n))
            if s == 2 and n == 8:
                add(piece(lax.select(odd, rem(me - 3, n), rem(me + 3, n))), far(0))
            elif s == 2:
                add(a.at[halves[0]], far(0))
            else:
                add(a, full(0, s - 3))
            first = send(a, full(0, s - 2), left)
            if s == 2 and n == 4:
                steps[-1][1].wait_recv()
                add(b.at[halves[1]], far(1))
            elif s > 2:
                steps[-1][1].wait_recv()
                add(b, full(1, s - 3))
            steps.append([first, send(b, full(1, s - 2), right)])

        def total():
            arrive(steps[-1])
            add(piece(me), full(0, last - 2), full(1, last - 2))
            return piece(me)

        return step, total

    def part_of(size, half):
        return pl.ds(0, size) if half is None else pl.ds(half * (size // 2), size // 2)

    def rows_of(start, half):
        return pl.ds(start, 32) if half is None else pl.ds(start + half * 16, 16)

    class Gather:
        def __init__(self, tile):
            self.tile = tile
            self.a = ring_gather(x_ring, lambda i, h: tile.at[i, y, rows_of(0, h)])
            self.b = ring_gather(y_ring, lambda j, h: tile.at[x, j, rows_of(32, h)])

        def inner(self):
            self.a[0](2)
            self.b[0](2)

        def outer(self):
            tile = self.tile
            self.a[1]()
            self.a = ring_gather(y_ring, lambda j, h: tile.at[part_of(4, h), j, pl.ds(0, 32)])
            self.b[1]()
            self.b = ring_gather(x_ring, lambda i, h: tile.at[i, part_of(4, h), pl.ds(32, 32)])

        def done(self):
            self.a[1]()
            self.b[1]()

    class Reduce:
        def __init__(self, tile, got):
            self.tile, self.got = tile, got
            far, full = got[0], got[1]
            self.a = ring_reduce(
                y_ring, lambda j: tile.at[:, j, pl.ds(0, 32)],
                lambda d: far.at[0, d], lambda d, s: full.at[0, d],
            )
            self.b = ring_reduce(
                x_ring, lambda i: tile.at[i, :, pl.ds(32, 32)],
                lambda d: far.at[1, d], lambda d, s: full.at[1, d],
            )

        def second(self):
            self.a[0](2)
            self.b[0](2)

        def inner(self):
            tile = self.tile
            far, full = self.got[2], self.got[3]
            self.a[1]()
            self.a = ring_reduce(
                x_ring, lambda i: tile.at[i, y, pl.ds(0, 32)],
                lambda d: far.at[0, d], lambda d, s: full.at[0, d],
            )
            self.b[1]()
            self.b = ring_reduce(
                y_ring, lambda j: tile.at[x, j, pl.ds(32, 32)],
                lambda d: far.at[1, d], lambda d, s: full.at[1, d],
            )

        def total(self):
            self.a[1]()
            self.b[1]()

    def spread(src, slot):
        copies = [
            send(src.at[:, rem(z + d, 8)], slot, zs[d - 1]) for d in range(1, 8)
        ]
        return place(src.at[:, z], slot), copies

    def half_of(lo):
        return pl.ds(pl.multiple_of(lo * 512, 512), 512)

    def qw_slot(c):
        def slot(zz, half):
            rows = pl.ds(c * 512, 512) if half is None else pl.ds(c * 512 + half * 256, 256)
            return w3.at[lax.rem(zz, 2), rows, at128(lax.div(zz, 2))]
        return slot

    def km_slot(zz, half):
        return km.at[lax.rem(zz, 2), part_of(2, half), lax.div(zz, 2)]

    li_slot = lit.at[x, y, :, at1024(zlo)]
    li_own = place(li.at[zlo], li_slot)
    li_sent = send(li.at[1 - zlo], li_slot, zpartner)
    og_a_slot = ogt.at[0, x, zh, :, half_of(zlo)]
    og_a_own = place(og.at[zlo, :, pl.ds(0, 512)], og_a_slot)
    og_a_sent = send(og.at[1 - zlo, :, pl.ds(0, 512)], og_a_slot, zpartner)
    qw_b_own = place(qw.at[pl.ds(512, 512)], qw_slot(1)(z, None))
    km_own = place(kw, km.at[zlo, ylo, zh])
    km_sent = send(kw, km.at[zlo, ylo, zh], ypartner)
    km_own.wait()
    km_sent.wait_recv()
    km_step, km_done = ring_gather(z_ring, km_slot)
    og_b_slot = ogt.at[1, x, zh, :, half_of(zlo)]
    og_b_own = place(og.at[zlo, :, pl.ds(512, 512)], og_b_slot)
    og_b_sent = send(og.at[1 - zlo, :, pl.ds(512, 512)], og_b_slot, zpartner)
    li_own.wait()
    li_sent.wait_recv()
    li_all = Gather(lit)
    qw_a_own = place(qw.at[pl.ds(0, 512)], qw_slot(0)(z, None))
    og_a_own.wait()
    og_a_sent.wait_recv()
    og_a_step, og_a_done = ring_gather(
        zh_ring, lambda i, h: ogt.at[0, x, i, part_of(64, h)]
    )
    li_all.inner()
    ao_slot = aot.at[quarter, :, :, at128(y)]
    ao_own = place(ao.at[y, :, zlo], ao_slot)
    ao_copies = [send(ao.at[j, :, lo], ao_slot, to) for j, lo, to in places[1:]]
    li_all.outer()
    og_a_step(2)
    ow_slot = owt.at[y, :, at1024(zlo)]
    ow_own = place(ow, ow_slot)
    ow_sent = send(ow, ow_slot, zpartner)
    og_a_done()
    og_a_step, og_a_done = ring_gather(x_ring, lambda i, h: ogt.at[0, i, part_of(4, h)])
    og_b_own.wait()
    og_b_sent.wait_recv()
    og_b_step, og_b_done = ring_gather(
        zh_ring, lambda i, h: ogt.at[1, x, i, part_of(64, h)]
    )
    qw_a_own.wait()
    qw_a_step, qw_a_done = ring_gather(z_ring, qw_slot(0))
    ow_own.wait()
    ow_sent.wait_recv()
    ow_step, ow_done = ring_gather(y_ring, lambda j, h: owt.at[j, part_of(128, h)])
    og_b_step(2)
    km_step(2)
    q_own, q_copies = spread(q, qkt.at[quarter, :, :, at128(zh)])
    ao_own.wait()
    arrive(ao_copies)
    ao_shared = [send(v, v, sibling) for v in [aot.at[lo * 2 + col] for lo in range(2)]]
    og_a_step(2)
    ow_step(2)
    og_b_done()
    og_b_step, og_b_done = ring_gather(x_ring, lambda i, h: ogt.at[1, i, part_of(4, h)])
    qw_b_own.wait()
    qw_b_step, qw_b_done = ring_gather(z_ring, qw_slot(1))
    og_a_done()
    arrive(ao_shared)
    for lo in range(2):
        for i in range(1):
            part = lax.dot_general(
                aot[...].reshape(1024, 512),
                ogt[0, :, :, :, pl.ds(lo * 512 + i * 512, 512)].reshape(1024, 512),
                (((0,), (0,)), ((), ())), preferred_element_type=F32,
            )
            owg[0, :, lo, :, pl.ds(i * 512, 512)] = part.reshape(4, 128, 512)
    owg_a_step, owg_a_total = ring_reduce(
        y_ring, lambda j: owg.at[0, j], lambda d: ow_far.at[0, d],
        lambda d, s: ow_full.at[0, d, s],
    )
    qw_a_step(2)
    km_step(3)
    k_own, k_copies = spread(k, kbuf.at[zh, zlo])
    qw_b_step(2)
    owg_a_step(2)
    og_b_step(2)
    og_b_done()
    for lo in range(2):
        for i in range(1):
            part = lax.dot_general(
                aot[...].reshape(1024, 512),
                ogt[1, :, :, :, pl.ds(lo * 512 + i * 512, 512)].reshape(1024, 512),
                (((0,), (0,)), ((), ())), preferred_element_type=F32,
            )
            owg[1, :, lo, :, pl.ds(i * 512, 512)] = part.reshape(4, 128, 512)
    owg_b_step, owg_b_total = ring_reduce(
        y_ring, lambda j: owg.at[1, j], lambda d: ow_far.at[1, d],
        lambda d, s: ow_full.at[1, d, s],
    )
    ow_done()

    def block(i, _):
        total = jnp.zeros((256, 512), F32)
        for c in range(2):
            for lo in range(2):
                total = total + lax.dot_general(
                    ogt[c, i, :, :, pl.ds(lo * 512, 512)].reshape(256, 512),
                    owt[:, :, pl.ds(lo * 1024 + c * 512, 512)].reshape(512, 512),
                    (((1,), (1,)), ((), ())), preferred_element_type=F32,
                )
        ag[i] = total.reshape(4, 64, 512)
        return 0

    lax.fori_loop(0, 4, block, 0)
    ag_sent = [send(ag.at[lo * 2 + 1 - col], agr.at[lo], sibling) for lo in range(2)]
    li_all.inner()
    qw_a_step(3)
    qw_b_step(3)
    k_own.wait()
    arrive(k_copies)
    for lo in range(2):
        total = kbuf[0, lo].astype(F32)
        for h in range(1, 4):
            total = total + kbuf[h, lo].astype(F32)
        high = total.astype(BF16)
        qkt[lo * 2 + col, :, :, pl.ds(512, 128)] = high
        qkt[lo * 2 + col, :, :, pl.ds(640, 128)] = (total - high.astype(F32)).astype(BF16)
    q_own.wait()
    arrive(q_copies)
    q_shared = [send(v, v, sibling) for v in [qkt.at[lo * 2 + col] for lo in range(2)]]
    owg_b_step(2)
    owg_a_mine = owg_a_total()
    owg_a_sent = send(owg_a_mine.at[1 - zlo], owy.at[0], zpartner)
    km_step(4)
    qw_a_step(4)
    qw_b_step(4)
    li_all.done()
    arrive(q_shared)

    for lo in range(2):
        def block(i, _, lo=lo):
            cols = pl.ds(pl.multiple_of(lo * 1024 + i * 256, 256), 256)
            rows = pl.ds(pl.multiple_of(i * 256, 256), 256)
            part = lax.dot_general(
                lit[:, :, :, cols].reshape(1024, 256), qkt[...].reshape(1024, 768),
                (((0,), (0,)), ((), ())), preferred_element_type=F32,
            )
            for h in range(4):
                qwg[lo, h, rows, :] = part[:, h * 128 : h * 128 + 128]
            sums = part[:, 512:640] + part[:, 640:768]
            kwg[lo, lax.div(i, 2), pl.ds(lax.rem(i, 2) * 2, 2)] = sums.reshape(2, 128, 128)
            return 0
        lax.fori_loop(0, 4, block, 0)
    qwg_a_step, qwg_a_total = ring_reduce(
        z_ring,
        lambda zz: qwg.at[lax.rem(zz, 2), lax.div(zz, 2), pl.ds(0, 512)],
        lambda d: qw_far.at[0, d], lambda d, s: qw_full.at[0, d, s],
    )
    qwg_b_step, qwg_b_total = ring_reduce(
        z_ring,
        lambda zz: qwg.at[lax.rem(zz, 2), lax.div(zz, 2), pl.ds(512, 512)],
        lambda d: qw_far.at[1, d], lambda d, s: qw_full.at[1, d, s],
    )
    kwg_step, kwg_total = ring_reduce(
        z_ring, lambda zz: kwg.at[lax.rem(zz, 2), :, lax.div(zz, 2)],
        lambda d: kw_far.at[d], lambda d, s: kw_full.at[d, s],
    )

    arrive(ag_sent)
    for lo in range(2):
        agb[lo] = (ag[lo * 2 + col] + agr[lo]).astype(BF16)
    ag_slot = ag_out.at[y, :, zlo]
    stored.append(place(agb.at[zlo, :, :, at128(y)], ag_slot))
    last += [send(agb.at[lo, :, :, at128(j)], ag_slot, to) for j, lo, to in places[1:]]
    qw_a_done()
    km_done()
    for lo in range(2):
        keys = km[lo].reshape(1024, 128)
        w3[lo, :, pl.ds(512, 128)] = keys
        w3[lo, :, pl.ds(640, 128)] = keys
    for lo in range(2):
        def block(i, _, lo=lo):
            rows = pl.ds(pl.multiple_of(0 + i * 256, 256), 256)
            part = lax.dot_general(
                qkt[...].reshape(1024, 768), w3[lo, rows, :],
                (((1,), (1,)), ((), ())), preferred_element_type=F32,
            )
            cols = pl.ds(pl.multiple_of(lo * 512 + i * 256, 256), 256)
            ig[0, :, :, :, cols] = part.reshape(4, 4, 64, 256)
            return 0
        lax.fori_loop(0, 2, block, 0)
    ig_sum_a = Reduce(ig.at[0], ig_got[0])
    owg_b_mine = owg_b_total()
    owg_b_sent = send(owg_b_mine.at[1 - zlo], owy.at[1], zpartner)
    qw_b_done()
    for lo in range(2):
        def block(i, _, lo=lo):
            rows = pl.ds(pl.multiple_of(512 + i * 256, 256), 256)
            part = lax.dot_general(
                qkt[...].reshape(1024, 768), w3[lo, rows, :],
                (((1,), (1,)), ((), ())), preferred_element_type=F32,
            )
            cols = pl.ds(pl.multiple_of(lo * 512 + i * 256, 256), 256)
            ig[1, :, :, :, cols] = part.reshape(4, 4, 64, 256)
            return 0
        lax.fori_loop(0, 2, block, 0)
    ig_sum_b = Reduce(ig.at[1], ig_got[1])
    qwg_b_step(2)
    kwg_step(2)
    owg_b_sent.wait_recv()
    add(owg_b_mine.at[zlo], owy.at[1])
    stored.append(place(owg_b_mine.at[zlo], owg_out.at[:, pl.ds(512, 512)]))
    ig_sum_a.second()
    qwg_a_step(2)
    kwg_step(3)
    ig_sum_b.second()
    qwg_b_step(3)
    kwg_step(4)
    qwg_a_step(3)
    qwg_b_step(4)
    ig_sum_a.inner()
    owg_a_sent.wait_recv()
    add(owg_a_mine.at[zlo], owy.at[0])
    stored.append(place(owg_a_mine.at[zlo], owg_out.at[:, pl.ds(0, 512)]))
    kwg_mine = kwg_total()
    kwg_sent = send(kwg_mine.at[1 - ylo], kwy, ypartner)
    ig_sum_b.inner()
    ig_sum_a.second()
    qwg_a_step(4)
    ig_sum_b.second()
    kwg_sent.wait_recv()
    kwy[...] = kwy[...] + kwg_mine[ylo]
    stored.append(place(kwy, kwg_out))
    ig_sum_a.total()
    fin[0] = ig[0, x, y].astype(BF16)
    cols = pl.ds(0, 512)
    mine, other = [
        fin.at[0, :, pl.ds(pl.multiple_of(lo * 512, 512), 512)] for lo in (zlo, 1 - zlo)
    ]
    stored.append(place(mine, ig_out.at[zlo, :, cols]))
    last.append(send(other, ig_out.at[zlo, :, cols], zpartner))
    ig_sum_b.total()
    fin[1] = ig[1, x, y].astype(BF16)
    cols = pl.ds(512, 512)
    mine, other = [
        fin.at[1, :, pl.ds(pl.multiple_of(lo * 512, 512), 512)] for lo in (zlo, 1 - zlo)
    ]
    stored.append(place(mine, ig_out.at[zlo, :, cols]))
    last.append(send(other, ig_out.at[zlo, :, cols], zpartner))
    stored.append(place(qwg_a_total(), qwg_out.at[pl.ds(0, 512)]))
    stored.append(place(qwg_b_total(), qwg_out.at[pl.ds(512, 512)]))
    arrive(last)
    for copy in stored:
        copy.wait()
    for copy in sent:
        copy.wait_send()


def finish(*refs):
    for source, target in zip(refs[:5], refs[5:]):
        target[...] = source[...]


def shards(layer_input, attn_out, out_grad, q_grad, k_grad, q_weight, k_weight, o_weight):
    shapes = (
        ((2, 64, 1024), BF16), ((4, 4, 2, 64, 128), BF16), ((1024, 128), F32),
        ((128, 128), F32), ((128, 1024), F32),
    )
    vmem = pltpu.VMEM
    def reduction():
        return (
            vmem((2, 2, 2, 32, 1024), F32), vmem((2, 2, 4, 32, 1024), F32),
            vmem((2, 2, 16, 1024), F32), vmem((2, 2, 32, 1024), F32),
        )

    scratch = [
        vmem((4, 4, 64, 2048), BF16),
        vmem((4, 128, 2048), BF16),
        vmem((2, 4, 4, 64, 1024), BF16),
        vmem((4, 4, 64, 768), BF16),
        vmem((4, 4, 64, 512), BF16),
        vmem((2, 1024, 768), BF16),
        vmem((2, 2, 4, 128, 128), BF16),
        vmem((4, 2, 4, 64, 128), BF16),
        vmem((2, 4, 4, 64, 1024), F32),
        vmem((2, 4, 2, 128, 512), F32),
        tuple(reduction() for _ in range(2)),
        vmem((2, 2, 1, 128, 512), F32),
        vmem((2, 2, 1, 2, 128, 512), F32),
        vmem((2, 128, 512), F32),
        vmem((2, 4, 1024, 128), F32),
        vmem((2, 2, 4, 128, 128), F32),
        vmem((2, 1, 512, 128), F32),
        vmem((2, 2, 3, 512, 128), F32),
        vmem((1, 2, 128, 128), F32),
        vmem((2, 3, 2, 128, 128), F32),
        vmem((128, 128), F32),
        vmem((4, 4, 64, 512), F32),
        vmem((2, 4, 64, 512), F32),
        vmem((2, 4, 64, 512), BF16),
        vmem((2, 64, 1024), BF16),
        pltpu.SemaphoreType.DMA((COPIES,)),
        pltpu.SemaphoreType.DMA((COPIES,)),
        pltpu.SemaphoreType.DMA((24,)),
    ]
    ig, ag, qwg, kwg, owg = pl.pallas_call(
        kernel,
        out_shape=[jax.ShapeDtypeStruct(*shape) for shape in shapes],
        in_specs=[pl.BlockSpec(memory_space=pl.ANY)] * 8,
        out_specs=[pl.BlockSpec(memory_space=pl.ANY)] * 5,
        scratch_shapes=scratch,
        compiler_params=pltpu.CompilerParams(
            collective_id=0, has_side_effects=True, vmem_limit_bytes=63 * 2**20
        ),
        cost_estimate=pl.CostEstimate(flops=14 * 10**9, bytes_accessed=5 * 10**6, transcendentals=0),
    )(
        layer_input.reshape(2, 64, 1024),
        attn_out.reshape(4, 4, 2, 64, 128),
        out_grad.reshape(2, 64, 1024),
        q_grad.reshape(4, 8, 64, 128),
        k_grad.reshape(4, 8, 64, 128),
        q_weight,
        k_weight[0],
        o_weight,
    )
    parts = (ig.reshape(128, 1024), ag.reshape(2048, 128), qwg, kwg, owg)
    ig, ag, qwg, kwg, owg = pl.pallas_call(
        finish,
        out_shape=[jax.ShapeDtypeStruct(part.shape, part.dtype) for part in parts],
        in_specs=[pl.BlockSpec(memory_space=pltpu.VMEM)] * 5,
        out_specs=[pl.BlockSpec(memory_space=pltpu.VMEM)] * 5,
    )(*parts)
    return ig, ag, qwg, kwg[None], owg


def solution(mesh):
    return jax.shard_map(
        shards,
        mesh=mesh,
        in_specs=(
            P("seq", ("row", "col")),
            P(("row", "col"), "seq"),
            P("seq", ("row", "col")),
            P(("row", "col"), "seq"),
            P(("row", "col"), "seq"),
            P(("row", "col"), "seq"),
            P("seq", ("row", "col"), None),
            P("seq", ("row", "col")),
        ),
        out_specs=(
            P("seq", ("row", "col")),
            P(("row", "col"), "seq"),
            P(("row", "col"), "seq"),
            P("seq", ("row", "col"), None),
            P("seq", ("row", "col")),
        ),
        check_vma=False,
    )
```

```python
import jax
import jax.numpy as jnp
from jax import lax
from jax.experimental import pallas as pl
from jax.experimental.pallas import tpu as pltpu
from jax.sharding import PartitionSpec as P

MESH = pl.DeviceIdType.MESH
COPIES = 176
F32 = jnp.float32
BF16 = jnp.bfloat16


def rem(value, size):
    return lax.rem(value + size, size)


def at128(index):
    return pl.ds(pl.multiple_of(index * 128, 128), 128)


def at1024(index):
    return pl.ds(pl.multiple_of(index * 1024, 1024), 1024)


def kernel(
    li, ao, og, q, k, qw, kw, ow,
    ig_out, ag_out, qwg_out, kwg_out, owg_out,
    lit, owt, ogt, qkt, aot, w3, km, kbuf,
    ig, owg, ig_got, ow_far, ow_full, owy,
    qwg, kwg, qw_far, qw_full, kw_far, kw_full, kwy,
    ag, agr, agb, fin,
    ssem, rsem, lsem,
):
    seq = lax.axis_index("seq")
    x, y, zh = lax.div(seq, 16), lax.rem(lax.div(seq, 4), 4), lax.rem(seq, 4)
    zlo, col = lax.axis_index("row"), lax.axis_index("col")
    z = zh * 2 + zlo
    yhi, ylo = lax.div(y, 2), lax.rem(y, 2)
    quarter = zlo * 2 + col

    def device(dx, dy, dz):
        zz = rem(z + dz, 8)
        return (
            rem(x + dx, 4) * 16 + rem(y + dy, 4) * 4 + lax.div(zz, 2), lax.rem(zz, 2), col
        )

    zs = [device(0, 0, d) for d in range(1, 8)]
    sibling = (seq, zlo, 1 - col)
    zpartner = device(0, 0, 1 - 2 * zlo)
    ypartner = device(0, 1 - 2 * ylo, 0)
    x_ring = (4, x, device(-1, 0, 0), device(1, 0, 0))
    y_ring = (4, y, device(0, -1, 0), device(0, 1, 0))
    z_ring = (8, z, device(0, 0, -1), device(0, 0, 1))
    odd = zlo == 1
    across = device(0, 0, 2 * zlo - 1)

    zh_ring = (4, zh, device(0, 0, -2), device(0, 0, 2))

    places = [
        (rem(y + d, 4), lo, device(0, d, dz)) for d in range(4)
        for lo, dz in ((zlo, 0), (1 - zlo, 1 - 2 * zlo))
    ]

    barrier = pltpu.get_barrier_semaphore()
    peers = list(x_ring[2:]) + [place[2] for place in places[1:]] + zs + [sibling]
    for peer in peers:
        pl.semaphore_signal(barrier, inc=1, device_id=peer, device_id_type=MESH)
    pl.semaphore_wait(barrier, len(peers))

    sent, local, last, stored = [], [], [], []

    def send(src, dst, to):
        n = len(sent)
        copy = pltpu.make_async_remote_copy(
            src_ref=src, dst_ref=dst, send_sem=ssem.at[n], recv_sem=rsem.at[n],
            device_id=to, device_id_type=MESH,
        )
        copy.start()
        sent.append(copy)
        return copy

    def place(src, dst):
        copy = pltpu.make_async_copy(src, dst, lsem.at[len(local)])
        copy.start()
        local.append(copy)
        return copy

    def arrive(copies):
        for copy in copies:
            copy.wait_recv()

    def add(dst, *parts):
        if len(dst.shape) == 3:
            def row(i, _):
                total = dst[i]
                for part in parts:
                    total = total + part[i]
                dst[i] = total
                return 0
            lax.fori_loop(0, dst.shape[0], row, 0)
        else:
            total = dst[...]
            for part in parts:
                total = total + part[...]
            dst[...] = total

    def ring_gather(ring, piece):
        n, me, left, right = ring
        own = piece(me, None)
        steps = [[send(own, own, left), send(own, own, right)]]

        def step(s):
            arrive(steps[-1])
            half = s == n // 2
            if half and n == 8:
                far = piece(lax.select(odd, rem(me - 3, n), rem(me + 3, n)), None)
                steps.append([send(far, far, across)])
                return
            a = piece(rem(me + s - 1, n), 0 if half else None)
            b = piece(rem(me - s + 1, n), 1 if half else None)
            steps.append([send(a, a, left), send(b, b, right)])

        return step, lambda: arrive(steps[-1])

    def ring_reduce(ring, piece, far, full):
        n, me, left, right = ring
        size = far(0).shape[0]
        halves = [pl.ds(0, size), pl.ds(size, size)]
        last = n // 2
        opposite = piece(rem(me + last, n))
        if n == 8:
            steps = [[send(opposite, far(0), across)]]
        else:
            steps = [[
                send(opposite.at[halves[0]], far(0), left),
                send(opposite.at[halves[1]], far(1), right),
            ]]

        def step(s):
            arrive(steps[-1])
            a, b = piece(rem(me - (last + 1 - s), n)), piece(rem(me + (last + 1 - s), n))
            if s == 2 and n == 8:
                add(piece(lax.select(odd, rem(me - 3, n), rem(me + 3, n))), far(0))
            elif s == 2:
                add(a.at[halves[0]], far(0))
                add(b.at[halves[1]], far(1))
            else:
                add(a, full(0, s - 3))
                add(b, full(1, s - 3))
            steps.append([send(a, full(0, s - 2), left), send(b, full(1, s - 2), right)])

        def total():
            arrive(steps[-1])
            add(piece(me), full(0, last - 2), full(1, last - 2))
            return piece(me)

        return step, total

    def part_of(size, half):
        return pl.ds(0, size) if half is None else pl.ds(half * (size // 2), size // 2)

    def rows_of(start, half):
        return pl.ds(start, 32) if half is None else pl.ds(start + half * 16, 16)

    class Gather:
        def __init__(self, tile):
            self.tile = tile
            self.a = ring_gather(x_ring, lambda i, h: tile.at[i, y, rows_of(0, h)])
            self.b = ring_gather(y_ring, lambda j, h: tile.at[x, j, rows_of(32, h)])

        def inner(self):
            self.a[0](2)
            self.b[0](2)

        def outer(self):
            tile = self.tile
            self.a[1]()
            self.a = ring_gather(y_ring, lambda j, h: tile.at[part_of(4, h), j, pl.ds(0, 32)])
            self.b[1]()
            self.b = ring_gather(x_ring, lambda i, h: tile.at[i, part_of(4, h), pl.ds(32, 32)])

        def done(self):
            self.a[1]()
            self.b[1]()

    class Reduce:
        def __init__(self, tile, got):
            self.tile, self.got = tile, got
            far, full = got[0], got[1]
            self.a = ring_reduce(
                y_ring, lambda j: tile.at[:, j, pl.ds(0, 32)],
                lambda d: far.at[0, d], lambda d, s: full.at[0, d],
            )
            self.b = ring_reduce(
                x_ring, lambda i: tile.at[i, :, pl.ds(32, 32)],
                lambda d: far.at[1, d], lambda d, s: full.at[1, d],
            )

        def second(self):
            self.a[0](2)
            self.b[0](2)

        def inner(self):
            tile = self.tile
            far, full = self.got[2], self.got[3]
            self.a[1]()
            self.a = ring_reduce(
                x_ring, lambda i: tile.at[i, y, pl.ds(0, 32)],
                lambda d: far.at[0, d], lambda d, s: full.at[0, d],
            )
            self.b[1]()
            self.b = ring_reduce(
                y_ring, lambda j: tile.at[x, j, pl.ds(32, 32)],
                lambda d: far.at[1, d], lambda d, s: full.at[1, d],
            )

        def total(self):
            self.a[1]()
            self.b[1]()

    def spread(src, slot):
        copies = [
            send(src.at[:, rem(z + d, 8)], slot, zs[d - 1]) for d in range(1, 8)
        ]
        return place(src.at[:, z], slot), copies

    def half_of(lo):
        return pl.ds(pl.multiple_of(lo * 512, 512), 512)

    def qw_slot(c):
        def slot(zz, half):
            rows = pl.ds(c * 512, 512) if half is None else pl.ds(c * 512 + half * 256, 256)
            return w3.at[lax.rem(zz, 2), rows, at128(lax.div(zz, 2))]
        return slot

    def km_slot(zz, half):
        return km.at[lax.rem(zz, 2), part_of(2, half), lax.div(zz, 2)]

    li_slot = lit.at[x, y, :, at1024(zlo)]
    li_own = place(li.at[zlo], li_slot)
    li_sent = send(li.at[1 - zlo], li_slot, zpartner)
    og_a_slot = ogt.at[0, x, zh, :, half_of(zlo)]
    og_a_own = place(og.at[zlo, :, pl.ds(0, 512)], og_a_slot)
    og_a_sent = send(og.at[1 - zlo, :, pl.ds(0, 512)], og_a_slot, zpartner)
    qw_b_own = place(qw.at[pl.ds(512, 512)], qw_slot(1)(z, None))
    km_own = place(kw, km.at[zlo, ylo, zh])
    km_sent = send(kw, km.at[zlo, ylo, zh], ypartner)
    km_own.wait()
    km_sent.wait_recv()
    km_step, km_done = ring_gather(z_ring, km_slot)
    og_b_slot = ogt.at[1, x, zh, :, half_of(zlo)]
    og_b_own = place(og.at[zlo, :, pl.ds(512, 512)], og_b_slot)
    og_b_sent = send(og.at[1 - zlo, :, pl.ds(512, 512)], og_b_slot, zpartner)
    li_own.wait()
    li_sent.wait_recv()
    li_all = Gather(lit)
    qw_a_own = place(qw.at[pl.ds(0, 512)], qw_slot(0)(z, None))
    og_a_own.wait()
    og_a_sent.wait_recv()
    og_a_step, og_a_done = ring_gather(
        zh_ring, lambda i, h: ogt.at[0, x, i, part_of(64, h)]
    )
    li_all.inner()
    ao_slot = aot.at[quarter, :, :, at128(y)]
    ao_own = place(ao.at[y, :, zlo], ao_slot)
    ao_copies = [send(ao.at[j, :, lo], ao_slot, to) for j, lo, to in places[1:]]
    li_all.outer()
    og_a_step(2)
    ow_slot = owt.at[y, :, at1024(zlo)]
    ow_own = place(ow, ow_slot)
    ow_sent = send(ow, ow_slot, zpartner)
    og_a_done()
    og_a_step, og_a_done = ring_gather(x_ring, lambda i, h: ogt.at[0, i, part_of(4, h)])
    og_b_own.wait()
    og_b_sent.wait_recv()
    og_b_step, og_b_done = ring_gather(
        zh_ring, lambda i, h: ogt.at[1, x, i, part_of(64, h)]
    )
    qw_a_own.wait()
    qw_a_step, qw_a_done = ring_gather(z_ring, qw_slot(0))
    ow_own.wait()
    ow_sent.wait_recv()
    ow_step, ow_done = ring_gather(y_ring, lambda j, h: owt.at[j, part_of(128, h)])
    og_b_step(2)
    km_step(2)
    q_own, q_copies = spread(q, qkt.at[quarter, :, :, at128(zh)])
    ao_own.wait()
    arrive(ao_copies)
    ao_shared = [send(v, v, sibling) for v in [aot.at[lo * 2 + col] for lo in range(2)]]
    og_a_step(2)
    ow_step(2)
    og_b_done()
    og_b_step, og_b_done = ring_gather(x_ring, lambda i, h: ogt.at[1, i, part_of(4, h)])
    qw_b_own.wait()
    qw_b_step, qw_b_done = ring_gather(z_ring, qw_slot(1))
    og_a_done()
    arrive(ao_shared)
    for lo in range(2):
        for i in range(1):
            part = lax.dot_general(
                aot[...].reshape(1024, 512),
                ogt[0, :, :, :, pl.ds(lo * 512 + i * 512, 512)].reshape(1024, 512),
                (((0,), (0,)), ((), ())), preferred_element_type=F32,
            )
            owg[0, :, lo, :, pl.ds(i * 512, 512)] = part.reshape(4, 128, 512)
    owg_a_step, owg_a_total = ring_reduce(
        y_ring, lambda j: owg.at[0, j], lambda d: ow_far.at[0, d],
        lambda d, s: ow_full.at[0, d, s],
    )
    qw_a_step(2)
    km_step(3)
    k_own, k_copies = spread(k, kbuf.at[zh, zlo])
    qw_b_step(2)
    owg_a_step(2)
    og_b_step(2)
    og_b_done()
    for lo in range(2):
        for i in range(1):
            part = lax.dot_general(
                aot[...].reshape(1024, 512),
                ogt[1, :, :, :, pl.ds(lo * 512 + i * 512, 512)].reshape(1024, 512),
                (((0,), (0,)), ((), ())), preferred_element_type=F32,
            )
            owg[1, :, lo, :, pl.ds(i * 512, 512)] = part.reshape(4, 128, 512)
    owg_b_step, owg_b_total = ring_reduce(
        y_ring, lambda j: owg.at[1, j], lambda d: ow_far.at[1, d],
        lambda d, s: ow_full.at[1, d, s],
    )
    ow_done()

    def block(i, _):
        total = jnp.zeros((256, 512), F32)
        for c in range(2):
            for lo in range(2):
                total = total + lax.dot_general(
                    ogt[c, i, :, :, pl.ds(lo * 512, 512)].reshape(256, 512),
                    owt[:, :, pl.ds(lo * 1024 + c * 512, 512)].reshape(512, 512),
                    (((1,), (1,)), ((), ())), preferred_element_type=F32,
                )
        ag[i] = total.reshape(4, 64, 512)
        return 0

    lax.fori_loop(0, 4, block, 0)
    ag_sent = [send(ag.at[lo * 2 + 1 - col], agr.at[lo], sibling) for lo in range(2)]
    li_all.inner()
    qw_a_step(3)
    qw_b_step(3)
    k_own.wait()
    arrive(k_copies)
    for lo in range(2):
        total = kbuf[0, lo].astype(F32)
        for h in range(1, 4):
            total = total + kbuf[h, lo].astype(F32)
        high = total.astype(BF16)
        qkt[lo * 2 + col, :, :, pl.ds(512, 128)] = high
        qkt[lo * 2 + col, :, :, pl.ds(640, 128)] = (total - high.astype(F32)).astype(BF16)
    q_own.wait()
    arrive(q_copies)
    q_shared = [send(v, v, sibling) for v in [qkt.at[lo * 2 + col] for lo in range(2)]]
    owg_b_step(2)
    owg_a_mine = owg_a_total()
    owg_a_sent = send(owg_a_mine.at[1 - zlo], owy.at[0], zpartner)
    km_step(4)
    qw_a_step(4)
    qw_b_step(4)
    li_all.done()
    arrive(q_shared)

    for lo in range(2):
        def block(i, _, lo=lo):
            cols = pl.ds(pl.multiple_of(lo * 1024 + i * 256, 256), 256)
            rows = pl.ds(pl.multiple_of(i * 256, 256), 256)
            part = lax.dot_general(
                lit[:, :, :, cols].reshape(1024, 256), qkt[...].reshape(1024, 768),
                (((0,), (0,)), ((), ())), preferred_element_type=F32,
            )
            for h in range(4):
                qwg[lo, h, rows, :] = part[:, h * 128 : h * 128 + 128]
            sums = part[:, 512:640] + part[:, 640:768]
            kwg[lo, lax.div(i, 2), pl.ds(lax.rem(i, 2) * 2, 2)] = sums.reshape(2, 128, 128)
            return 0
        lax.fori_loop(0, 4, block, 0)
    qwg_a_step, qwg_a_total = ring_reduce(
        z_ring,
        lambda zz: qwg.at[lax.rem(zz, 2), lax.div(zz, 2), pl.ds(0, 512)],
        lambda d: qw_far.at[0, d], lambda d, s: qw_full.at[0, d, s],
    )
    qwg_b_step, qwg_b_total = ring_reduce(
        z_ring,
        lambda zz: qwg.at[lax.rem(zz, 2), lax.div(zz, 2), pl.ds(512, 512)],
        lambda d: qw_far.at[1, d], lambda d, s: qw_full.at[1, d, s],
    )
    kwg_step, kwg_total = ring_reduce(
        z_ring, lambda zz: kwg.at[lax.rem(zz, 2), :, lax.div(zz, 2)],
        lambda d: kw_far.at[d], lambda d, s: kw_full.at[d, s],
    )

    arrive(ag_sent)
    for lo in range(2):
        agb[lo] = (ag[lo * 2 + col] + agr[lo]).astype(BF16)
    ag_slot = ag_out.at[y, :, zlo]
    stored.append(place(agb.at[zlo, :, :, at128(y)], ag_slot))
    last += [send(agb.at[lo, :, :, at128(j)], ag_slot, to) for j, lo, to in places[1:]]
    qw_a_done()
    km_done()
    for lo in range(2):
        keys = km[lo].reshape(1024, 128)
        w3[lo, :, pl.ds(512, 128)] = keys
        w3[lo, :, pl.ds(640, 128)] = keys
    for lo in range(2):
        def block(i, _, lo=lo):
            rows = pl.ds(pl.multiple_of(0 + i * 256, 256), 256)
            part = lax.dot_general(
                qkt[...].reshape(1024, 768), w3[lo, rows, :],
                (((1,), (1,)), ((), ())), preferred_element_type=F32,
            )
            cols = pl.ds(pl.multiple_of(lo * 512 + i * 256, 256), 256)
            ig[0, :, :, :, cols] = part.reshape(4, 4, 64, 256)
            return 0
        lax.fori_loop(0, 2, block, 0)
    ig_sum_a = Reduce(ig.at[0], ig_got[0])
    owg_b_mine = owg_b_total()
    owg_b_sent = send(owg_b_mine.at[1 - zlo], owy.at[1], zpartner)
    qw_b_done()
    for lo in range(2):
        def block(i, _, lo=lo):
            rows = pl.ds(pl.multiple_of(512 + i * 256, 256), 256)
            part = lax.dot_general(
                qkt[...].reshape(1024, 768), w3[lo, rows, :],
                (((1,), (1,)), ((), ())), preferred_element_type=F32,
            )
            cols = pl.ds(pl.multiple_of(lo * 512 + i * 256, 256), 256)
            ig[1, :, :, :, cols] = part.reshape(4, 4, 64, 256)
            return 0
        lax.fori_loop(0, 2, block, 0)
    ig_sum_b = Reduce(ig.at[1], ig_got[1])
    qwg_b_step(2)
    kwg_step(2)
    owg_b_sent.wait_recv()
    add(owg_b_mine.at[zlo], owy.at[1])
    stored.append(place(owg_b_mine.at[zlo], owg_out.at[:, pl.ds(512, 512)]))
    ig_sum_a.second()
    qwg_a_step(2)
    kwg_step(3)
    ig_sum_b.second()
    qwg_b_step(3)
    kwg_step(4)
    qwg_a_step(3)
    qwg_b_step(4)
    ig_sum_a.inner()
    owg_a_sent.wait_recv()
    add(owg_a_mine.at[zlo], owy.at[0])
    stored.append(place(owg_a_mine.at[zlo], owg_out.at[:, pl.ds(0, 512)]))
    kwg_mine = kwg_total()
    kwg_sent = send(kwg_mine.at[1 - ylo], kwy, ypartner)
    ig_sum_b.inner()
    ig_sum_a.second()
    qwg_a_step(4)
    ig_sum_b.second()
    kwg_sent.wait_recv()
    kwy[...] = kwy[...] + kwg_mine[ylo]
    stored.append(place(kwy, kwg_out))
    ig_sum_a.total()
    fin[0] = ig[0, x, y].astype(BF16)
    cols = pl.ds(0, 512)
    mine, other = [
        fin.at[0, :, pl.ds(pl.multiple_of(lo * 512, 512), 512)] for lo in (zlo, 1 - zlo)
    ]
    stored.append(place(mine, ig_out.at[zlo, :, cols]))
    last.append(send(other, ig_out.at[zlo, :, cols], zpartner))
    ig_sum_b.total()
    fin[1] = ig[1, x, y].astype(BF16)
    cols = pl.ds(512, 512)
    mine, other = [
        fin.at[1, :, pl.ds(pl.multiple_of(lo * 512, 512), 512)] for lo in (zlo, 1 - zlo)
    ]
    stored.append(place(mine, ig_out.at[zlo, :, cols]))
    last.append(send(other, ig_out.at[zlo, :, cols], zpartner))
    stored.append(place(qwg_a_total(), qwg_out.at[pl.ds(0, 512)]))
    stored.append(place(qwg_b_total(), qwg_out.at[pl.ds(512, 512)]))
    arrive(last)
    for copy in stored:
        copy.wait()
    for copy in sent:
        copy.wait_send()


def finish(*refs):
    sources, targets, held, sems = refs[:5], refs[5:10], refs[10:15], refs[15]
    loads = [
        pltpu.make_async_copy(sources[n], held[n], sems.at[n]) for n in range(5)
    ]
    stores = [
        pltpu.make_async_copy(held[n], targets[n], sems.at[5 + n]) for n in range(5)
    ]
    for load in loads:
        load.start()
    for load, store in zip(loads, stores):
        load.wait()
        store.start()
    for store in stores:
        store.wait()


def shards(layer_input, attn_out, out_grad, q_grad, k_grad, q_weight, k_weight, o_weight):
    shapes = (
        ((2, 64, 1024), BF16), ((4, 4, 2, 64, 128), BF16), ((1024, 128), F32),
        ((128, 128), F32), ((128, 1024), F32),
    )
    vmem = pltpu.VMEM
    def reduction():
        return (
            vmem((2, 2, 2, 32, 1024), F32), vmem((2, 2, 4, 32, 1024), F32),
            vmem((2, 2, 16, 1024), F32), vmem((2, 2, 32, 1024), F32),
        )

    scratch = [
        vmem((4, 4, 64, 2048), BF16),
        vmem((4, 128, 2048), BF16),
        vmem((2, 4, 4, 64, 1024), BF16),
        vmem((4, 4, 64, 768), BF16),
        vmem((4, 4, 64, 512), BF16),
        vmem((2, 1024, 768), BF16),
        vmem((2, 2, 4, 128, 128), BF16),
        vmem((4, 2, 4, 64, 128), BF16),
        vmem((2, 4, 4, 64, 1024), F32),
        vmem((2, 4, 2, 128, 512), F32),
        tuple(reduction() for _ in range(2)),
        vmem((2, 2, 1, 128, 512), F32),
        vmem((2, 2, 1, 2, 128, 512), F32),
        vmem((2, 128, 512), F32),
        vmem((2, 4, 1024, 128), F32),
        vmem((2, 2, 4, 128, 128), F32),
        vmem((2, 1, 512, 128), F32),
        vmem((2, 2, 3, 512, 128), F32),
        vmem((1, 2, 128, 128), F32),
        vmem((2, 3, 2, 128, 128), F32),
        vmem((128, 128), F32),
        vmem((4, 4, 64, 512), F32),
        vmem((2, 4, 64, 512), F32),
        vmem((2, 4, 64, 512), BF16),
        vmem((2, 64, 1024), BF16),
        pltpu.SemaphoreType.DMA((COPIES,)),
        pltpu.SemaphoreType.DMA((COPIES,)),
        pltpu.SemaphoreType.DMA((24,)),
    ]
    ig, ag, qwg, kwg, owg = pl.pallas_call(
        kernel,
        out_shape=[jax.ShapeDtypeStruct(*shape) for shape in shapes],
        in_specs=[pl.BlockSpec(memory_space=pl.ANY)] * 8,
        out_specs=[pl.BlockSpec(memory_space=pl.ANY)] * 5,
        scratch_shapes=scratch,
        compiler_params=pltpu.CompilerParams(
            collective_id=0, has_side_effects=True, vmem_limit_bytes=63 * 2**20
        ),
        cost_estimate=pl.CostEstimate(flops=14 * 10**9, bytes_accessed=5 * 10**6, transcendentals=0),
    )(
        layer_input.reshape(2, 64, 1024),
        attn_out.reshape(4, 4, 2, 64, 128),
        out_grad.reshape(2, 64, 1024),
        q_grad.reshape(4, 8, 64, 128),
        k_grad.reshape(4, 8, 64, 128),
        q_weight,
        k_weight[0],
        o_weight,
    )
    parts = (ig.reshape(128, 1024), ag.reshape(2048, 128), qwg, kwg, owg)
    ig, ag, qwg, kwg, owg = pl.pallas_call(
        finish,
        out_shape=[jax.ShapeDtypeStruct(part.shape, part.dtype) for part in parts],
        in_specs=[pl.BlockSpec(memory_space=pl.ANY)] * 5,
        out_specs=[pl.BlockSpec(memory_space=pl.ANY)] * 5,
        scratch_shapes=[pltpu.VMEM(part.shape, part.dtype) for part in parts]
        + [pltpu.SemaphoreType.DMA((10,))],
        compiler_params=pltpu.CompilerParams(vmem_limit_bytes=63 * 2**20),
    )(*parts)
    return ig, ag, qwg, kwg[None], owg


def solution(mesh):
    return jax.shard_map(
        shards,
        mesh=mesh,
        in_specs=(
            P("seq", ("row", "col")),
            P(("row", "col"), "seq"),
            P("seq", ("row", "col")),
            P(("row", "col"), "seq"),
            P(("row", "col"), "seq"),
            P(("row", "col"), "seq"),
            P("seq", ("row", "col"), None),
            P("seq", ("row", "col")),
        ),
        out_specs=(
            P("seq", ("row", "col")),
            P(("row", "col"), "seq"),
            P(("row", "col"), "seq"),
            P("seq", ("row", "col"), None),
            P("seq", ("row", "col")),
        ),
        check_vma=False,
    )
```
